32 devices in a mesh: px: 4 (over z), py: 8 (over y, x, core).
Axes of the slice: x: 2, y: 2, z: 4, core: 2. Of those that a mesh axis runs over, the one named last changes fastest.
Arguments:
- field_in: bfloat16 [32, 8, 512, 512], P(None, 'py', 'px'), may hold values from -6 to 6
- cotangent: bfloat16 [32, 8, 512, 512], P(None, 'py', 'px'), may hold values from -6 to 6
- spectrum_saved: float32 [32, 8, 32, 32, 2], P(None, None, 'px', 'py'), may hold values from -6 to 6
- weight_store: float32 [2048, 2, 32, 32], P(('px', 'py')), may hold values from -4.2 to 4.2
- block_slot: int32 [32, 32], P('py', 'px'), may hold values from 0 to 511, as said below
- kx_modes: int32 [32], replicated, may hold values from 0 to 511, as said below
- ky_modes: int32 [32], replicated, may hold values from 0 to 511, as said below
- pointwise: bfloat16 [32, 32], replicated, may hold values from -0.25 to 0.25
- bias_vector: float32 [32], replicated, may hold values from -3 to 3
Outputs:
- field_grad: float32 [32, 8, 512, 512], P(None, 'py', 'px')
- store_grad: float32 [2048, 2, 32, 32], P(('px', 'py'))
The draws below stay inside these ranges and needn't reach their ends.
Inputs may be any that keep to these rules, and one draw needn't show every extreme that they name: `kx_modes`: 32 distinct wave numbers k, each with k < 32 or k > 480. `ky_modes`: 32 distinct wave numbers k, each with k < 32 or k > 480. `block_slot`: within each px index's 8 second-dimension modes, the values over all 32 x 8 mode pairs are distinct; v // 64 is the py index of the device that stores the block and v % 64 its slot there; in each such group one py index stores 64 blocks, and the other slots hold unused blocks.
All inputs are finite; a program needn't handle non-finite values.
Results may differ from the reference program's by a relative error of at most 0.0003.
Values sent between devices are 32-bit elements; how exact they have to be, the bound alone decides.
No kernel may reach another device: no remote copies, remote signals or barrier semaphores. Data moves between devices by JAX's collectives and lax.ppermute only.
A program may use at most 128 MiB of HBM per device.

```python
import math
import jax
import jax.numpy as jnp
from jax import lax

C = 32
NX = 512
NY = 512
MX = 32
MY = 32
NZ = 8
MY_DEV = 8
CAP = 64
ROW_SLOTS = 512
STORE = 2048
N_PX = 4
N_PY = 8


def low_modes(key, count, length):
    picks = jax.random.permutation(key, 2 * count - 1).astype(jnp.int32)[:count]
    return jnp.where(picks < count, picks, length - (picks - count + 1)).astype(jnp.int32)


def draw_kx_modes(key, part):
    return low_modes(jax.random.fold_in(key, 11), MX, NX)


def draw_ky_modes(key, part):
    return low_modes(jax.random.fold_in(key, 23), MY, NY)


def draw_block_slot(key, part):
    rows_y = MY // N_PX
    count = MX * rows_y
    keys = jax.random.split(jax.random.fold_in(key, 37), N_PX)
    row_ids = jnp.arange(N_PX, dtype=jnp.int32)

    def one_row(row_key, row_id):
        key_order, key_busy = jax.random.split(row_key)
        order = jax.random.permutation(key_order, count).astype(jnp.int32)
        drawn = jax.random.randint(key_busy, (), 0, N_PY).astype(jnp.int32)
        busy = jnp.where(row_id == 0, N_PY - 1, drawn).astype(jnp.int32)
        place = jnp.arange(count, dtype=jnp.int32)
        others = place - CAP
        owner = jnp.where(place < CAP, busy, (busy + 1 + others % (N_PY - 1)) % N_PY)
        slot = jnp.where(place < CAP, place, others // (N_PY - 1))
        return jnp.zeros((count,), jnp.int32).at[order].set((owner * CAP + slot).astype(jnp.int32))
    table = jax.vmap(one_row)(keys, row_ids)
    return jnp.transpose(table.reshape(N_PX, MX, rows_y), (1, 0, 2)).reshape(MX, MY).astype(jnp.int32)


def levels(own_key, dims, shards, least, high):
    def one(axis_at, shards_of):
        draws = jax.random.uniform(jax.random.fold_in(jax.random.fold_in(own_key, 6), axis_at), (shards_of,), jnp.float32, least / len(shards), high / len(shards))
        return jnp.repeat(jnp.exp(draws), dims[axis_at] // shards_of).reshape((-1,) + (1,) * (len(dims) - axis_at - 1))

    factor_of = one(*shards[0])
    for cut in shards[1:]:
        factor_of = factor_of * one(*cut)
    return factor_of


def bell_draw(rng, shape, width, most, shards=(), held_as=jnp.bfloat16):
    values = jax.random.normal(rng, shape, jnp.float32) * width
    if len(shards) > 0:
        values = levels(rng, shape, shards, -0.22, 0.18) * values
    return jnp.clip(values, min=-most, max=most).astype(held_as)


def setup_inputs(seed: int = 0) -> dict:
    key_of = jax.random.split(jax.random.key(seed), 10)
    return {
        "field_in": bell_draw(key_of[0], (C, NZ, NX, NY), 1.0, 6.0, ((1, 8), (2, 4))),
        "cotangent": bell_draw(key_of[1], (C, NZ, NX, NY), 1.0, 6.0, ((1, 8), (2, 4))),
        "spectrum_saved": bell_draw(key_of[2], (C, NZ, MY, MX, 2), 1.0, 6.0, ((2, 4), (3, 8)), jnp.float32),
        "weight_store": bell_draw(key_of[3], (STORE, 2, C, C), 0.7, 4.2, ((0, 32),), jnp.float32),
        "block_slot": draw_block_slot(jax.random.fold_in(key_of[9], 71), 0),
        "kx_modes": draw_kx_modes(jax.random.fold_in(key_of[9], 71), 0),
        "ky_modes": draw_ky_modes(jax.random.fold_in(key_of[9], 71), 0),
        "pointwise": bell_draw(key_of[7], (C, C), (16 * C) ** -0.5, 0.25),
        "bias_vector": bell_draw(key_of[8], (C,), 0.5, 3.0, (), jnp.float32),
    }


precise = lax.Precision.HIGHEST

def gelu_slope(values):
    normal_cdf = 0.5 * (1.0 + lax.erf(values * 0.7071067811865476))
    density = jnp.exp(-0.5 * values * values) * 0.3989422804014327
    return normal_cdf + values * density

def reference(field_in, cotangent, spectrum_saved, weight_store, block_slot, kx_modes, ky_modes, pointwise, bias_vector):
    row_of = jnp.arange(MY, dtype=jnp.int32) // MY_DEV
    indices = (row_of[None, :] * ROW_SLOTS + block_slot).astype(jnp.int32)
    blocks = jnp.take(weight_store, indices.reshape(-1), axis=0).reshape(MX, MY, 2, C, C)
    block_re = blocks[:, :, 0]
    block_im = blocks[:, :, 1]
    factor = 1.0 / math.sqrt(NX * NY)
    weight_full = pointwise.astype(jnp.float32)
    rows_x = kx_modes[:, None]
    cols_y = ky_modes[None, :]

    def plane(total, depth):
        values = lax.dynamic_index_in_dim(field_in, depth, 1, False).astype(jnp.float32)
        upstream = lax.dynamic_index_in_dim(cotangent, depth, 1, False).astype(jnp.float32)
        saved = lax.dynamic_index_in_dim(spectrum_saved, depth, 1, False)
        spec_re = jnp.transpose(saved[..., 0], (0, 2, 1))
        spec_im = jnp.transpose(saved[..., 1], (0, 2, 1))
        form = 'aboc,cab->oab'
        mixed_re = jnp.einsum(form, block_re, spec_re, precision=precise) - jnp.einsum(form, block_im, spec_im, precision=precise)
        mixed_im = jnp.einsum(form, block_re, spec_im, precision=precise) + jnp.einsum(form, block_im, spec_re, precision=precise)
        base = jnp.zeros_like(values)
        full = lax.complex(base.at[:, rows_x, cols_y].set(mixed_re), base.at[:, rows_x, cols_y].set(mixed_im))
        spectral = jnp.real(jnp.fft.ifft2(full, axes=(1, 2))) * (NX * NY * factor)
        pre = jnp.einsum('oc,cxy->oxy', weight_full, values, precision=precise) + bias_vector[:, None, None] + spectral
        grad = upstream * gelu_slope(pre)
        transform = jnp.fft.fft2(grad, axes=(1, 2))[:, rows_x, cols_y] * factor
        grad_re = jnp.real(transform)
        grad_im = jnp.imag(transform)
        back_form = 'aboc,oab->cab'
        adj_re = jnp.einsum(back_form, block_re, grad_re, precision=precise) + jnp.einsum(back_form, block_im, grad_im, precision=precise)
        adj_im = jnp.einsum(back_form, block_re, grad_im, precision=precise) - jnp.einsum(back_form, block_im, grad_re, precision=precise)
        back = lax.complex(base.at[:, rows_x, cols_y].set(adj_re), base.at[:, rows_x, cols_y].set(adj_im))
        plane_grad = jnp.einsum('oc,oxy->cxy', weight_full, grad, precision=precise)
        plane_grad = plane_grad + jnp.real(jnp.fft.ifft2(back, axes=(1, 2))) * (NX * NY * factor)
        grad_form = 'oab,cab->aboc'
        step_re = jnp.einsum(grad_form, grad_re, spec_re, precision=precise) + jnp.einsum(grad_form, grad_im, spec_im, precision=precise)
        step_im = jnp.einsum(grad_form, grad_im, spec_re, precision=precise) - jnp.einsum(grad_form, grad_re, spec_im, precision=precise)
        return (total + jnp.stack([step_re, step_im], 2), plane_grad)
    start = jnp.zeros((MX, MY, 2, C, C), jnp.float32)
    total, grads = lax.scan(plane, start, jnp.arange(NZ, dtype=jnp.int32))
    field_grad = jnp.moveaxis(grads, 0, 1)
    store_grad = jnp.zeros_like(weight_store).at[indices.reshape(-1)].set(total.reshape(MX * MY, 2, C, C))
    return (field_grad, store_grad)
```

```python
import functools
import math

import jax
import jax.numpy as jnp
from jax import lax
from jax.experimental import pallas as pl
from jax.experimental.pallas import tpu as pltpu
from jax.sharding import PartitionSpec as P

precise = lax.Precision.HIGHEST


def phase_table(length, modes):
    points = lax.iota(jnp.int32, length)
    wrapped = points[:, None] * modes[None, :] % length
    angle = wrapped.astype(jnp.float32) * (2.0 * math.pi / length)
    return (jnp.cos(angle), jnp.sin(angle))


def gelu_slope(values):
    normal_cdf = 0.5 * (1.0 + lax.erf(values * 0.7071067811865476))
    density = jnp.exp(-0.5 * values * values) * 0.3989422804014327
    return normal_cdf + values * density


def channel_mix(blocks, spectrum):
    block_re = blocks[:, :, 0]
    block_im = blocks[:, :, 1]
    spec_re = spectrum[..., 0]
    spec_im = spectrum[..., 1]
    form = "baoc,czba->ozba"
    out_re = jnp.einsum(form, block_re, spec_re, precision=precise) - jnp.einsum(
        form, block_im, spec_im, precision=precise
    )
    out_im = jnp.einsum(form, block_re, spec_im, precision=precise) + jnp.einsum(
        form, block_im, spec_re, precision=precise
    )
    return jnp.stack([out_re, out_im], -1)


def channel_adjoint(blocks, spectrum):
    block_re = blocks[:, :, 0]
    block_im = blocks[:, :, 1]
    grad_re = spectrum[..., 0]
    grad_im = spectrum[..., 1]
    form = "baoc,ozba->czba"
    out_re = jnp.einsum(form, block_re, grad_re, precision=precise) + jnp.einsum(
        form, block_im, grad_im, precision=precise
    )
    out_im = jnp.einsum(form, block_re, grad_im, precision=precise) - jnp.einsum(
        form, block_im, grad_re, precision=precise
    )
    return jnp.stack([out_re, out_im], -1)


def block_gradient(spectrum_grad, spectrum):
    grad_re = spectrum_grad[..., 0]
    grad_im = spectrum_grad[..., 1]
    spec_re = spectrum[..., 0]
    spec_im = spectrum[..., 1]
    form = "ozba,czba->aboc"
    out_re = jnp.einsum(form, grad_re, spec_re, precision=precise) + jnp.einsum(
        form, grad_im, spec_im, precision=precise
    )
    out_im = jnp.einsum(form, grad_im, spec_re, precision=precise) - jnp.einsum(
        form, grad_re, spec_im, precision=precise
    )
    return jnp.stack([out_re, out_im], 2)


def invert_rows(spectrum, cos_rows, sin_rows):
    spec_re = spectrum[..., 0]
    spec_im = spectrum[..., 1]
    form = "czma,xa->czmx"
    back_re = jnp.einsum(form, spec_re, cos_rows, precision=precise) - jnp.einsum(
        form, spec_im, sin_rows, precision=precise
    )
    back_im = jnp.einsum(form, spec_re, sin_rows, precision=precise) + jnp.einsum(
        form, spec_im, cos_rows, precision=precise
    )
    joined = jnp.stack([back_re, back_im], 3)
    return joined.reshape(joined.shape[0], joined.shape[1], 2 * joined.shape[2], joined.shape[4])


def on_device(
    field_in,
    cotangent,
    spectrum_saved,
    weight_store,
    block_slot,
    kx_modes,
    ky_modes,
    pointwise,
    bias_vector,
):
    channels, planes, rows_x, width_y = field_in.shape
    full_x = rows_x * lax.axis_size("px")
    modes_y = ky_modes.shape[0]
    local_y = modes_y // lax.axis_size("px")
    capacity = weight_store.shape[0]
    factor = 1.0 / math.sqrt(full_x * width_y)
    cos_y, sin_y = phase_table(width_y, ky_modes)
    table_y = jnp.stack([cos_y, -sin_y], 2).reshape(width_y, 2 * modes_y)
    cos_x, sin_x = phase_table(full_x, kx_modes)
    store_row, slots_row = (
        lax.all_gather(weight_store, "py", axis=0, tiled=True),
        lax.all_gather(block_slot, "py", axis=0, tiled=True),
    )
    slots_flat = slots_row.reshape(-1)

    def inverse_planes(spectrum):
        joined = invert_rows(spectrum, cos_x, sin_x)
        returned = lax.all_to_all(joined, "px", split_axis=3, concat_axis=2, tiled=True)
        return factor * jnp.einsum("czkx,yk->czxy", returned, table_y, precision=precise)

    weight_full = pointwise.astype(jnp.float32)
    local_x = block_slot.shape[0]
    indices = jnp.transpose(block_slot).reshape(-1)
    blocks = jnp.take(store_row, indices, axis=0).reshape(local_y, local_x, 2, channels, channels)
    mixed = channel_mix(blocks, spectrum_saved)

    def from_modes(spectrum):
        return lax.all_to_all(spectrum, "py", split_axis=1, concat_axis=3, tiled=True)

    spectral = inverse_planes(from_modes(mixed))
    mapped = jnp.einsum("oc,czxy->ozxy", pointwise, field_in, preferred_element_type=jnp.float32)
    grad = cotangent.astype(jnp.float32) * gelu_slope(
        mapped + bias_vector.reshape(channels, 1, 1, 1) + spectral
    )
    partial_value = jnp.einsum("czxy,yk->czkx", grad, table_y, precision=precise)
    moved = lax.all_to_all(partial_value, "px", split_axis=2, concat_axis=3, tiled=True)
    pieces = moved.reshape(channels, planes, local_y, 2, full_x)
    part_re = pieces[:, :, :, 0]
    part_im = pieces[:, :, :, 1]
    form = "czmx,xk->czmk"
    real_part = jnp.einsum(form, part_re, cos_x, precision=precise) + jnp.einsum(
        form, part_im, sin_x, precision=precise
    )
    imag_part = jnp.einsum(form, part_im, cos_x, precision=precise) - jnp.einsum(
        form, part_re, sin_x, precision=precise
    )
    spectrum_grad = lax.all_to_all(
        factor * jnp.stack([real_part, imag_part], -1),
        "py",
        split_axis=3,
        concat_axis=1,
        tiled=True,
    )
    input_spectrum = channel_adjoint(blocks, spectrum_grad)
    local_grad = block_gradient(spectrum_grad, spectrum_saved)
    field_grad = jnp.einsum("oc,ozxy->czxy", weight_full, grad, precision=precise) + inverse_planes(
        from_modes(input_spectrum)
    )
    grads_all = lax.all_gather(local_grad, "py", axis=0, tiled=True)
    grads_flat = grads_all.reshape(slots_flat.shape[0], 2 * channels * channels)
    targets = lax.axis_index("py") * capacity + lax.iota(jnp.int32, capacity)
    select = (targets[:, None] == slots_flat[None, :]).astype(jnp.float32)
    store_flat = jnp.dot(select, grads_flat, precision=precise)
    store_grad = store_flat.reshape(capacity, 2, channels, channels)
    return (field_grad, store_grad)


def split(values):
    high = values.astype(jnp.bfloat16)
    return high, (values - high.astype(jnp.float32)).astype(jnp.bfloat16)


def dot(left, right):
    return jnp.dot(left, right, preferred_element_type=jnp.float32)


def dot_rows(left, right):
    return lax.dot_general(left, right, (((1,), (1,)), ((), ())), preferred_element_type=jnp.float32)


def lanes_of(shape):
    return lax.broadcasted_iota(jnp.int32, shape, len(shape) - 1)


def rows_of(shape):
    return lax.broadcasted_iota(jnp.int32, shape, len(shape) - 2)


def whole(count):
    return [pl.BlockSpec(memory_space=pltpu.VMEM)] * count


def params():
    return pltpu.CompilerParams(vmem_limit_bytes=56 * 1024 * 1024)


TAIL = 0.28
TAIL_TERMS = (
    0.11652062560141857,
    0.0674977537901661,
    0.26890757481260397,
    -0.2369901538988787,
    0.3898718975484817,
    -0.10580770707520248,
)


def gelu_slope_tail(values):
    size = jnp.abs(values)
    inner = pl.reciprocal(1.0 + TAIL * size, approx=False)
    total = TAIL_TERMS[-1] * inner
    for term in TAIL_TERMS[-2::-1]:
        total = (total + term) * inner
    tail = jnp.exp(-0.5 * size * size) * (total - 0.3989422804014327 * size)
    return jnp.where(values < 0.0, tail, 1.0 - tail)


def tables_kernel(start_ref, ky_ref, kx_rows_ref, kx_lanes_ref, ti_ref, tf_ref, xi_ref, xf_ref, *, full_x):
    modes_y, width = ky_ref.shape[0], ti_ref.shape[1]
    modes_x, rows_x = kx_rows_ref.shape[0], xf_ref.shape[0] // 4
    factor = 1.0 / math.sqrt(full_x * width)

    def angles(modes, points, length):
        return ((modes * points) & (length - 1)).astype(jnp.float32) * (2.0 * math.pi / length)

    angle = angles(ky_ref[...], lanes_of((modes_y, width)), width)
    high, low = split(jnp.concatenate([jnp.cos(angle), -jnp.sin(angle)], 0))
    ti_ref[...] = jnp.concatenate([high, high, low, jnp.zeros_like(low)], 0)
    tf_ref[...] = jnp.concatenate([high, low], 0)
    angle = angles(kx_rows_ref[...], start_ref[0] + lanes_of((modes_x, rows_x)), full_x)
    cos, sin, zero = factor * jnp.cos(angle), factor * jnp.sin(angle), jnp.zeros_like(angle)
    rows = [[cos, sin, zero, zero], [-sin, cos, zero, zero], [zero, zero, cos, sin], [zero, zero, -sin, cos]]
    high, low = split(jnp.concatenate([jnp.concatenate(row, 1) for row in rows], 0))
    xi_ref[...] = jnp.concatenate([high, high, low], 0)
    shape = (rows_x, 4 * modes_x)
    angle = angles(kx_lanes_ref[...], start_ref[0] + rows_of(shape), full_x)
    cos, sin, zero = factor * jnp.cos(angle), factor * jnp.sin(angle), jnp.zeros_like(angle)
    lane = lanes_of(shape)
    real = (lane // modes_x) % 2 == 0
    first = lane < 2 * modes_x
    from_re, from_im = jnp.where(real, cos, -sin), jnp.where(real, sin, cos)
    rows = [
        jnp.where(first, from_re, zero),
        jnp.where(first, from_im, zero),
        jnp.where(first, zero, from_re),
        jnp.where(first, zero, from_im),
    ]
    high, low = split(jnp.concatenate(rows, 0))
    xf_ref[...] = jnp.concatenate([high, low], 1)


def make_tables(start, ky, kx, full_x, rows_x, width):
    modes_y, modes_x = ky.shape[0], kx.shape[0]
    shapes = ((4 * 2 * modes_y, width), (2 * 2 * modes_y, width), (3 * 4 * modes_x, 4 * rows_x), (4 * rows_x, 8 * modes_x))
    return pl.pallas_call(
        functools.partial(tables_kernel, full_x=full_x),
        out_shape=[jax.ShapeDtypeStruct(shape, jnp.bfloat16) for shape in shapes],
        in_specs=[pl.BlockSpec(memory_space=pltpu.SMEM)] + whole(3),
        out_specs=whole(4),
        compiler_params=params(),
        name="tables",
    )(start, ky.reshape(-1, 1), kx.reshape(-1, 1), jnp.tile(kx, 4).reshape(1, -1))


def duplicate(values):
    return jnp.concatenate([values, values], -1)


def mix_kernel(place_ref, store_ref, spec_ref, slots_ref, kept_ref, out_ref, ra_ref, rb_ref, uc_ref, ud_ref):
    planes, channels, lanes = out_ref.shape
    capacity = lanes // 2
    wide = spec_ref.shape[1]
    for part in range(channels):
        rows = pl.ds(part * channels, channels)
        ra_ref[rows] = duplicate(store_ref[0, part])
        im = duplicate(store_ref[1, part])
        rb_ref[rows] = jnp.where(lanes_of(im.shape) < capacity, -im, im)
    numbers = jnp.transpose(slots_ref[...])
    wanted = (place_ref[0] * capacity + rows_of(numbers.shape) % capacity).astype(jnp.float32)
    chosen = (numbers == wanted).astype(jnp.bfloat16)
    high, low = split(spec_ref[...])
    placed = jnp.transpose(dot(chosen, high) + dot(chosen, low))
    kept_ref[...] = placed
    parts = placed.reshape(planes, 2, channels, lanes)
    first = lanes_of((channels, lanes)) < capacity
    for plane in range(planes):
        rows = pl.ds(plane * channels, channels)
        uc_ref[rows] = jnp.where(first, parts[plane, 0], parts[plane, 1])
        ud_ref[rows] = jnp.where(first, parts[plane, 1], parts[plane, 0])

    def step(channel, sums):
        ra = ra_ref[pl.ds(channel, channels, stride=channels)]
        rb = rb_ref[pl.ds(channel, channels, stride=channels)]
        return tuple(
            total
            + ra * uc_ref[pl.ds(plane * channels + channel, 1)]
            + rb * ud_ref[pl.ds(plane * channels + channel, 1)]
            for plane, total in enumerate(sums)
        )

    zero = jnp.zeros((channels, lanes), jnp.float32)
    sums = lax.fori_loop(0, channels, step, (zero,) * planes)
    for plane in range(planes):
        out_ref[plane] = sums[plane]


def mix(place, store, spec, slots, planes):
    channels, lanes = store.shape[1], 2 * store.shape[3]
    return pl.pallas_call(
        mix_kernel,
        out_shape=[
            jax.ShapeDtypeStruct((2 * planes * channels, lanes), jnp.float32),
            jax.ShapeDtypeStruct((planes, channels, lanes), jnp.float32),
        ],
        in_specs=[pl.BlockSpec(memory_space=pltpu.SMEM)] + whole(3),
        out_specs=whole(2),
        scratch_shapes=[pltpu.VMEM((channels * channels, lanes), jnp.float32)] * 2
        + [pltpu.VMEM((planes * channels, lanes), jnp.float32)] * 2,
        compiler_params=params(),
        name="mix",
    )(place, store, spec, slots)


def swap_halves(values):
    half = values.shape[-1] // 2
    return jnp.concatenate([values[..., half:], values[..., :half]], -1)


def adjoint_kernel(store_ref, grad_ref, out_ref, ra_ref, rb_ref, gs_ref):
    planes, channels, lanes = out_ref.shape
    capacity = lanes // 2
    for part in range(channels):
        rows = pl.ds(part * channels, channels)
        ra_ref[rows] = duplicate(store_ref[0, part])
        im = duplicate(store_ref[1, part])
        rb_ref[rows] = jnp.where(lanes_of(im.shape) < capacity, im, -im)
    for plane in range(planes):
        gs_ref[plane] = swap_halves(grad_ref[plane])

    def step(channel, sums):
        rows = pl.ds(channel * channels, channels)
        ra, rb = ra_ref[rows], rb_ref[rows]
        return tuple(
            total + ra * grad_ref[plane, pl.ds(channel, 1)] + rb * gs_ref[plane, pl.ds(channel, 1)]
            for plane, total in enumerate(sums)
        )

    zero = jnp.zeros((channels, lanes), jnp.float32)
    sums = lax.fori_loop(0, channels, step, (zero,) * planes)
    for plane in range(planes):
        out_ref[plane] = sums[plane]


def adjoint(store, grad):
    planes, channels, lanes = grad.shape
    return pl.pallas_call(
        adjoint_kernel,
        out_shape=jax.ShapeDtypeStruct(grad.shape, jnp.float32),
        in_specs=whole(2),
        out_specs=whole(1)[0],
        scratch_shapes=[pltpu.VMEM((channels * channels, lanes), jnp.float32)] * 2
        + [pltpu.VMEM((planes, channels, lanes), jnp.float32)],
        compiler_params=params(),
        name="adjoint",
    )(store, grad)


def weight_grad_kernel(kept_ref, grad_ref, out_ref, gs_ref):
    planes, channels, lanes = grad_ref.shape
    capacity = lanes // 2
    for plane in range(planes):
        swapped = swap_halves(grad_ref[plane])
        gs_ref[plane] = jnp.where(lanes_of(swapped.shape) < capacity, swapped, -swapped)

    def step(channel, carry):
        total = jnp.zeros((channels, lanes), jnp.float32)
        for plane in range(planes):
            real = kept_ref[pl.ds(plane * 2 * channels, channels)]
            imag = kept_ref[pl.ds(plane * 2 * channels + channels, channels)]
            total = total + real * grad_ref[plane, pl.ds(channel, 1)] + imag * gs_ref[plane, pl.ds(channel, 1)]
        out_ref[0, channel] = total[:, :capacity]
        out_ref[1, channel] = total[:, capacity:]
        return carry

    lax.fori_loop(0, channels, step, 0)


def weight_grad(kept, grad):
    planes, channels, lanes = grad.shape
    return pl.pallas_call(
        weight_grad_kernel,
        out_shape=jax.ShapeDtypeStruct((2, channels, channels, lanes // 2), jnp.float32),
        in_specs=whole(2),
        out_specs=whole(1)[0],
        scratch_shapes=[pltpu.VMEM((planes, channels, lanes), jnp.float32)],
        compiler_params=params(),
        name="weight_grad",
    )(kept, grad)


def fill_selection(slots_ref, chosen_ref, modes_x, capacity):
    lanes = 2 * capacity
    shape = (modes_x, lanes)
    lane = lanes_of(shape)
    first = lane < capacity
    zero = jnp.zeros(shape, jnp.float32)
    for mode in range(slots_ref.shape[0] // modes_x):
        numbers = slots_ref[pl.ds(mode * modes_x, modes_x)]
        for owner in range(chosen_ref.shape[1] // lanes):
            wanted = (owner * capacity + lane % capacity).astype(jnp.float32)
            hit = jnp.where(numbers == wanted, 1.0, 0.0)
            both = jnp.concatenate([jnp.where(first, hit, zero), jnp.where(first, zero, hit)], 0)
            chosen_ref[pl.ds(mode * 2 * modes_x, 2 * modes_x), pl.ds(owner * lanes, lanes)] = both.astype(jnp.bfloat16)


def to_modes_kernel(slots_ref, in_ref, out_ref, chosen_ref, *, modes_x):
    owners, channels, lanes = in_ref.shape
    half = channels // 2
    fill_selection(slots_ref, chosen_ref, modes_x, lanes // 2)
    high, low = split(jnp.concatenate([in_ref[owner] for owner in range(owners)], 1))
    found = dot_rows(jnp.concatenate([high, low], 0), chosen_ref[...])
    found = found[:channels] + found[channels:]
    local_y = found.shape[1] // (2 * modes_x)
    for mode in range(local_y):
        piece = found[:, mode * 2 * modes_x : (mode + 1) * 2 * modes_x]
        out_ref[pl.ds(mode, half, stride=local_y)] = jnp.concatenate([piece[:half], piece[half:]], 1)


def to_modes(slots, values, modes_x):
    owners, channels, lanes = values.shape
    local_y = slots.shape[0] // modes_x
    return pl.pallas_call(
        functools.partial(to_modes_kernel, modes_x=modes_x),
        out_shape=jax.ShapeDtypeStruct((channels // 2 * local_y, 4 * modes_x), jnp.float32),
        in_specs=whole(2),
        out_specs=whole(1)[0],
        scratch_shapes=[pltpu.VMEM((2 * slots.shape[0], owners * lanes), jnp.bfloat16)],
        compiler_params=params(),
        name="to_modes",
    )(slots, values)


def to_slots_kernel(slots_ref, *refs, modes_x):
    *pieces, out_ref, chosen_ref, sum_ref = refs
    owners, channels, lanes = out_ref.shape
    half = channels // 2
    fill_selection(slots_ref, chosen_ref, modes_x, lanes // 2)
    sum_ref[...] = sum(piece[...] for piece in pieces)
    local_y = sum_ref.shape[0] // half
    columns = []
    for mode in range(local_y):
        piece = sum_ref[pl.ds(mode, half, stride=local_y)]
        columns.append(jnp.concatenate([piece[:, : 2 * modes_x], piece[:, 2 * modes_x :]], 0))
    high, low = split(jnp.concatenate(columns, 1))
    found = dot(jnp.concatenate([high, low], 0), chosen_ref[...])
    found = found[:channels] + found[channels:]
    for owner in range(owners):
        out_ref[owner] = found[:, owner * lanes : (owner + 1) * lanes]


def to_slots(slots, pieces, owners, channels, lanes, modes_x):
    return pl.pallas_call(
        functools.partial(to_slots_kernel, modes_x=modes_x),
        out_shape=jax.ShapeDtypeStruct((owners, channels, lanes), jnp.float32),
        in_specs=whole(1 + len(pieces)),
        out_specs=whole(1)[0],
        scratch_shapes=[
            pltpu.VMEM((2 * slots.shape[0], owners * lanes), jnp.bfloat16),
            pltpu.VMEM(pieces[0].shape, jnp.float32),
        ],
        compiler_params=params(),
        name="to_slots",
    )(slots, *pieces)


def spread(small, rows):
    count = small.shape[0]
    shape = (count * rows, count)
    take = (rows_of(shape) // rows == lanes_of(shape)).astype(jnp.bfloat16)
    shape = (count, count * rows)
    put = (lanes_of(shape) // rows == rows_of(shape)).astype(jnp.bfloat16)
    full = dot(dot(take, small).astype(jnp.bfloat16), put)
    shape = full.shape
    return jnp.where(rows_of(shape) % rows == lanes_of(shape) % rows, full, 0.0).astype(jnp.bfloat16)


def pointwise_kernel(weight_ref, bias_ref, in_ref, out_ref, full_ref):
    channels, rows, width = in_ref.shape

    @pl.when(pl.program_id(0) == 0)
    def _():
        full_ref[...] = spread(weight_ref[...], rows)

    out = dot(full_ref[...], in_ref[...].reshape(channels * rows, width))
    out_ref[...] = out.reshape(channels, rows, width) + bias_ref[...]


def pointwise_map(weight, bias, values, rows=16):
    channels, rows_x, width = values.shape
    block = pl.BlockSpec((channels, rows, width), lambda i: (0, i, 0))
    return pl.pallas_call(
        pointwise_kernel,
        grid=(rows_x // rows,),
        out_shape=jax.ShapeDtypeStruct(values.shape, jnp.float32),
        in_specs=whole(2) + [block],
        out_specs=block,
        scratch_shapes=[pltpu.VMEM((channels * rows, channels * rows), jnp.bfloat16)],
        compiler_params=params(),
        cost_estimate=pl.CostEstimate(flops=4 * 10**9, bytes_accessed=12 * 2**20, transcendentals=0),
        name="pointwise_map",
    )(weight, bias.reshape(-1, 1, 1), values)


def pointwise_back_kernel(weight_ref, high_ref, low_ref, out_ref, full_ref):
    channels, rows, width = high_ref.shape

    @pl.when(pl.program_id(0) == 0)
    def _():
        full_ref[...] = spread(weight_ref[...], rows)

    full = full_ref[...]
    out = dot(full, high_ref[...].reshape(channels * rows, width))
    out = out + dot(full, low_ref[...].reshape(channels * rows, width))
    out_ref[...] = out.reshape(channels, rows, width)


def pointwise_back(weight, high, low, rows=16):
    channels, rows_x, width = high.shape
    block = pl.BlockSpec((channels, rows, width), lambda i: (0, i, 0))
    return pl.pallas_call(
        pointwise_back_kernel,
        grid=(rows_x // rows,),
        out_shape=jax.ShapeDtypeStruct(high.shape, jnp.float32),
        in_specs=whole(1) + [block, block],
        out_specs=block,
        scratch_shapes=[pltpu.VMEM((channels * rows, channels * rows), jnp.bfloat16)],
        compiler_params=params(),
        cost_estimate=pl.CostEstimate(flops=8 * 10**9, bytes_accessed=16 * 2**20, transcendentals=0),
        name="pointwise_back",
    )(jnp.transpose(weight), high, low)


def invert_x(pieces, xi_ref, st_ref):
    high, low = split(jnp.concatenate([piece[...] for piece in pieces], 0))
    deep = high.shape[1]
    left = jnp.concatenate([high, low], 1)
    found = dot(left, xi_ref[pl.ds(0, 2 * deep)]) + dot(high, xi_ref[pl.ds(2 * deep, deep)])
    st_ref[...] = found.reshape(st_ref.shape)


def spectral_part(index, half, st_ref, ti_ref):
    blocks, _, local_y, wide = st_ref.shape
    rows_x = wide // 4
    here = st_ref[:, index, :, pl.ds(half * 2 * rows_x, 2 * rows_x)].reshape(blocks * local_y, 2 * rows_x)
    parts = [here[:, :rows_x], here[:, rows_x:]]
    tall = jnp.transpose(jnp.concatenate(parts + parts, 0))
    high = tall.astype(jnp.bfloat16)
    first = lanes_of(tall.shape) < tall.shape[1] // 2
    mixed = jnp.where(first, tall, tall - high.astype(jnp.float32)).astype(jnp.bfloat16)
    return dot(jnp.concatenate([mixed, high], 1), ti_ref[...])


def slope_kernel(*refs, blocks):
    pieces, (xi_ref, ti_ref, tf_ref, xf_ref, mapped_ref, cot_ref) = refs[:blocks], refs[blocks : blocks + 6]
    outs, (st_ref, yt_ref) = refs[blocks + 6 : -2], refs[-2:]
    high_ref, low_ref = outs[:2]
    step = pl.program_id(0)
    halves, _, rows_x, width = mapped_ref.shape

    @pl.when(step == 0)
    def _():
        invert_x(pieces, xi_ref, st_ref)

    deep = tf_ref.shape[0] // 2
    modes_y = deep // 2
    local_y = modes_y // blocks
    for half in range(halves):
        before = mapped_ref[half, 0] + spectral_part(step, half, st_ref, ti_ref)
        grad = cot_ref[half, 0].astype(jnp.float32) * gelu_slope_tail(before)
        high, low = split(grad)
        high_ref[half, 0] = high
        low_ref[half, 0] = low
        both = dot_rows(tf_ref[...], high)
        found = both[:deep] + both[deep:] + dot_rows(tf_ref[pl.ds(0, deep)], low)
        for block in range(blocks):
            for part in range(2):
                at = part * modes_y + block * local_y
                columns = pl.ds((2 * half + part) * rows_x, rows_x)
                yt_ref[block, step, :, columns] = found[at : at + local_y]

    @pl.when(step == pl.num_programs(0) - 1)
    def _():
        high, low = split(yt_ref[...].reshape(-1, yt_ref.shape[-1]))
        lanes = xf_ref.shape[1] // 2
        both = dot(high, xf_ref[...])
        total = both[:, :lanes] + both[:, lanes:] + dot(low, xf_ref[:, :lanes])
        rows = total.shape[0] // blocks
        for block in range(blocks):
            outs[2 + block][...] = total[block * rows : (block + 1) * rows]


def slope_step(pieces, tables, mapped, cotangent):
    ti, tf, xi, xf = tables
    blocks = len(pieces)
    channels, rows_x, width = mapped.shape
    half = channels // 2
    local_y = pieces[0].shape[0] // half
    block = pl.BlockSpec((2, 1, rows_x, width), lambda i: (0, i, 0, 0))
    shape = (2, half, rows_x, width)
    results = pl.pallas_call(
        functools.partial(slope_kernel, blocks=blocks),
        grid=(half,),
        out_shape=[jax.ShapeDtypeStruct(shape, jnp.bfloat16)] * 2
        + [jax.ShapeDtypeStruct(pieces[0].shape, jnp.float32)] * blocks,
        in_specs=whole(blocks + 4) + [block, block],
        out_specs=[block, block] + whole(blocks),
        scratch_shapes=[pltpu.VMEM((blocks, half, local_y, 4 * rows_x), jnp.float32)] * 2,
        compiler_params=params(),
        name="slope_step",
    )(*pieces, xi, ti, tf, xf, mapped.reshape(shape), cotangent.reshape(shape))
    full = (channels, rows_x, width)
    return results[0].reshape(full), results[1].reshape(full), results[2:]


def finish_kernel(*refs, blocks):
    pieces, (xi_ref, ti_ref, part_ref, out_ref, st_ref) = refs[:blocks], refs[blocks:]
    step = pl.program_id(0)

    @pl.when(step == 0)
    def _():
        invert_x(pieces, xi_ref, st_ref)

    for half in range(part_ref.shape[0]):
        out_ref[half, 0] = part_ref[half, 0] + spectral_part(step, half, st_ref, ti_ref)


def finish(pieces, tables, part):
    ti, _, xi, _ = tables
    blocks = len(pieces)
    channels, rows_x, width = part.shape
    half = channels // 2
    local_y = pieces[0].shape[0] // half
    block = pl.BlockSpec((2, 1, rows_x, width), lambda i: (0, i, 0, 0))
    shape = (2, half, rows_x, width)
    return pl.pallas_call(
        functools.partial(finish_kernel, blocks=blocks),
        grid=(half,),
        out_shape=jax.ShapeDtypeStruct(shape, jnp.float32),
        in_specs=whole(blocks + 2) + [block],
        out_specs=block,
        scratch_shapes=[pltpu.VMEM((blocks, half, local_y, 4 * rows_x), jnp.float32)],
        compiler_params=params(),
        name="finish",
    )(*pieces, xi, ti, part.reshape(shape)).reshape(part.shape)


def from_all(piece, axis, count):
    received = [piece]
    for step in range(1, count):
        received.append(lax.ppermute(piece, axis, [(i, (i + step) % count) for i in range(count)]))
    return received


def to_all(pieces, axis, count):
    received = [pieces[0]]
    for step in range(1, count):
        received.append(lax.ppermute(pieces[step], axis, [(i, (i - step) % count) for i in range(count)]))
    return received


def on_device_packed(
    field_in,
    cotangent,
    spectrum_saved,
    weight_store,
    block_slot,
    kx_modes,
    ky_modes,
    pointwise,
    bias_vector,
):
    channels, _, rows_x, width_y = field_in.shape
    count_x, count_y = lax.axis_size("px"), lax.axis_size("py")
    full_x = rows_x * count_x
    planes, local_y, local_x = spectrum_saved.shape[1:4]
    modes_x = kx_modes.shape[0]
    place_x, place_y = lax.axis_index("px"), lax.axis_index("py")
    lanes = 2 * weight_store.shape[0]
    store = jnp.transpose(weight_store, (1, 2, 3, 0))

    wide = jnp.transpose(spectrum_saved, (2, 3, 1, 4, 0)).reshape(local_y * local_x, -1)
    numbers = jnp.transpose(block_slot).reshape(-1, 1).astype(jnp.float32)
    sent = jnp.concatenate([wide, jnp.broadcast_to(numbers, (wide.shape[0], lanes))], 1)
    gathered = lax.all_gather(sent, "py", axis=0, tiled=True)
    spec = gathered[:, : wide.shape[1]]
    slots_by_place = gathered[:, wide.shape[1] :]
    slots = jnp.transpose(slots_by_place.reshape(count_y, local_y, local_x, lanes), (1, 0, 2, 3))
    slots = slots.reshape(local_y * modes_x, lanes)

    order = (place_x - lax.iota(jnp.int32, count_x)) % count_x
    ky = jnp.take(ky_modes.reshape(count_x, local_y), order, axis=0).reshape(-1)
    tables = make_tables((place_x * rows_x).reshape(1), ky, kx_modes, full_x, rows_x, width_y)
    mapped = pointwise_map(pointwise, bias_vector, field_in[:, 0])

    def swap_places(values):
        return lax.all_to_all(values, "py", split_axis=0, concat_axis=0, tiled=True)

    kept, mixed = mix(place_y.reshape(1), store, spec, slots_by_place, planes)
    modes = to_modes(slots, swap_places(mixed), modes_x)
    high, low, sums = slope_step(from_all(modes, "px", count_x), tables, mapped, cotangent[:, 0])
    back = pointwise_back(pointwise, high, low)
    spectrum_grad = swap_places(
        to_slots(slots, to_all(sums, "px", count_x), count_y, channels, lanes, modes_x)
    )
    modes = to_modes(slots, swap_places(adjoint(store, spectrum_grad)), modes_x)
    field_grad = finish(from_all(modes, "px", count_x), tables, back)
    store_grad = jnp.transpose(weight_grad(kept, spectrum_grad), (3, 0, 1, 2))
    return (field_grad[:, None], store_grad)


def packs(mesh, channels, planes, rows, width, modes, capacity):
    count_x, count_y = mesh.shape["px"], mesh.shape["py"]
    powers = all(size & (size - 1) == 0 for size in (rows, width))
    return (
        powers
        and planes == count_y
        and channels == 32
        and 4 * modes == 128
        and 2 * capacity == 128
        and rows // count_x == 128
        and width % 256 == 0
        and modes // count_x == 8
    )


def solution(mesh):
    placed = (
        P(None, "py", "px", None),
        P(None, "py", "px", None),
        P(None, None, "px", "py", None),
        P(("px", "py"), None, None, None),
        P("py", "px"),
        P(),
        P(),
        P(),
        P(),
    )

    def run(*args):
        channels, planes, rows, width = args[0].shape
        capacity = args[3].shape[0] // mesh.size
        packed = packs(mesh, channels, planes, rows, width, args[5].shape[0], capacity)
        return jax.shard_map(
            on_device_packed if packed else on_device,
            mesh=mesh,
            in_specs=placed,
            out_specs=(P(None, "py", "px", None), P(("px", "py"), None, None, None)),
            check_vma=False,
        )(*args)

    return run
```

```python
import functools
import math

import jax
import jax.numpy as jnp
from jax import lax
from jax.experimental import pallas as pl
from jax.experimental.pallas import tpu as pltpu
from jax.sharding import PartitionSpec as P

precise = lax.Precision.HIGHEST


def phase_table(length, modes):
    points = lax.iota(jnp.int32, length)
    wrapped = points[:, None] * modes[None, :] % length
    angle = wrapped.astype(jnp.float32) * (2.0 * math.pi / length)
    return (jnp.cos(angle), jnp.sin(angle))


def gelu_slope(values):
    normal_cdf = 0.5 * (1.0 + lax.erf(values * 0.7071067811865476))
    density = jnp.exp(-0.5 * values * values) * 0.3989422804014327
    return normal_cdf + values * density


def channel_mix(blocks, spectrum):
    block_re = blocks[:, :, 0]
    block_im = blocks[:, :, 1]
    spec_re = spectrum[..., 0]
    spec_im = spectrum[..., 1]
    form = "baoc,czba->ozba"
    out_re = jnp.einsum(form, block_re, spec_re, precision=precise) - jnp.einsum(
        form, block_im, spec_im, precision=precise
    )
    out_im = jnp.einsum(form, block_re, spec_im, precision=precise) + jnp.einsum(
        form, block_im, spec_re, precision=precise
    )
    return jnp.stack([out_re, out_im], -1)


def channel_adjoint(blocks, spectrum):
    block_re = blocks[:, :, 0]
    block_im = blocks[:, :, 1]
    grad_re = spectrum[..., 0]
    grad_im = spectrum[..., 1]
    form = "baoc,ozba->czba"
    out_re = jnp.einsum(form, block_re, grad_re, precision=precise) + jnp.einsum(
        form, block_im, grad_im, precision=precise
    )
    out_im = jnp.einsum(form, block_re, grad_im, precision=precise) - jnp.einsum(
        form, block_im, grad_re, precision=precise
    )
    return jnp.stack([out_re, out_im], -1)


def block_gradient(spectrum_grad, spectrum):
    grad_re = spectrum_grad[..., 0]
    grad_im = spectrum_grad[..., 1]
    spec_re = spectrum[..., 0]
    spec_im = spectrum[..., 1]
    form = "ozba,czba->aboc"
    out_re = jnp.einsum(form, grad_re, spec_re, precision=precise) + jnp.einsum(
        form, grad_im, spec_im, precision=precise
    )
    out_im = jnp.einsum(form, grad_im, spec_re, precision=precise) - jnp.einsum(
        form, grad_re, spec_im, precision=precise
    )
    return jnp.stack([out_re, out_im], 2)


def invert_rows(spectrum, cos_rows, sin_rows):
    spec_re = spectrum[..., 0]
    spec_im = spectrum[..., 1]
    form = "czma,xa->czmx"
    back_re = jnp.einsum(form, spec_re, cos_rows, precision=precise) - jnp.einsum(
        form, spec_im, sin_rows, precision=precise
    )
    back_im = jnp.einsum(form, spec_re, sin_rows, precision=precise) + jnp.einsum(
        form, spec_im, cos_rows, precision=precise
    )
    joined = jnp.stack([back_re, back_im], 3)
    return joined.reshape(joined.shape[0], joined.shape[1], 2 * joined.shape[2], joined.shape[4])


def on_device(
    field_in,
    cotangent,
    spectrum_saved,
    weight_store,
    block_slot,
    kx_modes,
    ky_modes,
    pointwise,
    bias_vector,
):
    channels, planes, rows_x, width_y = field_in.shape
    full_x = rows_x * lax.axis_size("px")
    modes_y = ky_modes.shape[0]
    local_y = modes_y // lax.axis_size("px")
    capacity = weight_store.shape[0]
    factor = 1.0 / math.sqrt(full_x * width_y)
    cos_y, sin_y = phase_table(width_y, ky_modes)
    table_y = jnp.stack([cos_y, -sin_y], 2).reshape(width_y, 2 * modes_y)
    cos_x, sin_x = phase_table(full_x, kx_modes)
    store_row, slots_row = (
        lax.all_gather(weight_store, "py", axis=0, tiled=True),
        lax.all_gather(block_slot, "py", axis=0, tiled=True),
    )
    slots_flat = slots_row.reshape(-1)

    def inverse_planes(spectrum):
        joined = invert_rows(spectrum, cos_x, sin_x)
        returned = lax.all_to_all(joined, "px", split_axis=3, concat_axis=2, tiled=True)
        return factor * jnp.einsum("czkx,yk->czxy", returned, table_y, precision=precise)

    weight_full = pointwise.astype(jnp.float32)
    local_x = block_slot.shape[0]
    indices = jnp.transpose(block_slot).reshape(-1)
    blocks = jnp.take(store_row, indices, axis=0).reshape(local_y, local_x, 2, channels, channels)
    mixed = channel_mix(blocks, spectrum_saved)

    def from_modes(spectrum):
        return lax.all_to_all(spectrum, "py", split_axis=1, concat_axis=3, tiled=True)

    spectral = inverse_planes(from_modes(mixed))
    mapped = jnp.einsum("oc,czxy->ozxy", pointwise, field_in, preferred_element_type=jnp.float32)
    grad = cotangent.astype(jnp.float32) * gelu_slope(
        mapped + bias_vector.reshape(channels, 1, 1, 1) + spectral
    )
    partial_value = jnp.einsum("czxy,yk->czkx", grad, table_y, precision=precise)
    moved = lax.all_to_all(partial_value, "px", split_axis=2, concat_axis=3, tiled=True)
    pieces = moved.reshape(channels, planes, local_y, 2, full_x)
    part_re = pieces[:, :, :, 0]
    part_im = pieces[:, :, :, 1]
    form = "czmx,xk->czmk"
    real_part = jnp.einsum(form, part_re, cos_x, precision=precise) + jnp.einsum(
        form, part_im, sin_x, precision=precise
    )
    imag_part = jnp.einsum(form, part_im, cos_x, precision=precise) - jnp.einsum(
        form, part_re, sin_x, precision=precise
    )
    spectrum_grad = lax.all_to_all(
        factor * jnp.stack([real_part, imag_part], -1),
        "py",
        split_axis=3,
        concat_axis=1,
        tiled=True,
    )
    input_spectrum = channel_adjoint(blocks, spectrum_grad)
    local_grad = block_gradient(spectrum_grad, spectrum_saved)
    field_grad = jnp.einsum("oc,ozxy->czxy", weight_full, grad, precision=precise) + inverse_planes(
        from_modes(input_spectrum)
    )
    grads_all = lax.all_gather(local_grad, "py", axis=0, tiled=True)
    grads_flat = grads_all.reshape(slots_flat.shape[0], 2 * channels * channels)
    targets = lax.axis_index("py") * capacity + lax.iota(jnp.int32, capacity)
    select = (targets[:, None] == slots_flat[None, :]).astype(jnp.float32)
    store_flat = jnp.dot(select, grads_flat, precision=precise)
    store_grad = store_flat.reshape(capacity, 2, channels, channels)
    return (field_grad, store_grad)


def split(values):
    high = values.astype(jnp.bfloat16)
    return high, (values - high.astype(jnp.float32)).astype(jnp.bfloat16)


def dot(left, right):
    return jnp.dot(left, right, preferred_element_type=jnp.float32)


def dot_rows(left, right):
    return lax.dot_general(left, right, (((1,), (1,)), ((), ())), preferred_element_type=jnp.float32)


def lanes_of(shape):
    return lax.broadcasted_iota(jnp.int32, shape, len(shape) - 1)


def rows_of(shape):
    return lax.broadcasted_iota(jnp.int32, shape, len(shape) - 2)


def whole(count):
    return [pl.BlockSpec(memory_space=pltpu.VMEM)] * count


def params(mebibytes=12):
    return pltpu.CompilerParams(vmem_limit_bytes=mebibytes * 1024 * 1024)


def takes(microseconds):
    return pl.CostEstimate(flops=int(microseconds * 10**9), bytes_accessed=2**20, transcendentals=0)


def outside(count):
    return [pl.BlockSpec(memory_space=pltpu.HBM)] * count


def scalars(count):
    return [pl.BlockSpec(memory_space=pltpu.SMEM)] * count


BEND_TERMS = (
    0.7978849414899104,
    0.03633308440863974,
    -3.2594744583983906e-05,
    -5.5306316703040985e-05,
    3.964773129084329e-06,
    -1.322662760933859e-07,
    1.7562773353616594e-09,
)
DENSITY = math.sqrt(2.0 / math.pi)


def twice_gelu_slope(scaled):
    square = scaled * scaled
    total = BEND_TERMS[-1] / DENSITY ** (2 * len(BEND_TERMS) - 1)
    for power in range(len(BEND_TERMS) - 2, -1, -1):
        total = total * square + BEND_TERMS[power] / DENSITY ** (2 * power + 1)
    bell = jnp.exp2(square * (-0.5 * math.log2(math.e) / DENSITY**2))
    return (1.0 + jnp.tanh(scaled * total)) + scaled * bell


def column_of(ref, start, count, rows):
    shape = (rows, 128)
    row = rows_of(shape) % count
    out = jnp.zeros(shape, jnp.int32)
    for i in range(count):
        out = jnp.where(row == i, ref[start(i)], out)
    return out


def prepare_kernel(
    place_ref, ky_ref, kx_ref, store_ref, ti_ref, tf_ref, xi_ref, xf_ref, packed_ref, *, full_x, count_x, count_y
):
    for channel in range(store_ref.shape[1]):
        rows = pl.ds(channel * store_ref.shape[2], store_ref.shape[2])
        packed_ref[rows] = jnp.concatenate([store_ref[0, channel], store_ref[1, channel]], 1)
    modes_y, width = ky_ref.shape[0], tf_ref.shape[1]
    modes_x, rows_x = kx_ref.shape[0], xf_ref.shape[0] // 4
    local_y = modes_y // count_x
    factor = 1.0 / math.sqrt(full_x * width)
    place = place_ref[0]
    start = place * rows_x
    local_x = modes_x // count_y

    def angles(modes, points, length):
        return ((modes * points) & (length - 1)).astype(jnp.float32) * (2.0 * math.pi / length)

    def ky_at(i):
        return (place ^ (i // local_y)) * local_y + i % local_y

    def kx_at(i):
        return (place_ref[1] ^ (i // local_x)) * local_x + i % local_x

    ky = column_of(ky_ref, ky_at, modes_y, modes_y)
    ky = jnp.concatenate([ky] * (width // 128), 1)
    angle = angles(ky, lanes_of(ky.shape), width)
    waves = jnp.concatenate([jnp.cos(angle), -jnp.sin(angle)], 0)
    high, low = split(waves)
    tf_ref[...] = jnp.concatenate([high, low], 0)
    for index, scale in enumerate((DENSITY, 1.0)):
        high, low = split(scale * waves)
        ti_ref[index] = jnp.concatenate([high, high, low, jnp.zeros_like(low)], 0)
    kx = column_of(kx_ref, kx_at, modes_x, modes_x)
    angle = angles(kx, start + lanes_of((modes_x, rows_x)), full_x)
    cos, sin, zero = factor * jnp.cos(angle), factor * jnp.sin(angle), jnp.zeros_like(angle)
    rows = [[cos, sin, zero, zero], [-sin, cos, zero, zero], [zero, zero, cos, sin], [zero, zero, -sin, cos]]
    high, low = split(jnp.concatenate([jnp.concatenate(row, 1) for row in rows], 0))
    xi_ref[...] = jnp.concatenate([high, high, low], 0)
    shape = (rows_x, 4 * modes_x)
    kx = jnp.transpose(column_of(kx_ref, kx_at, modes_x, 4 * modes_x))
    angle = angles(kx, start + rows_of(shape), full_x)
    cos, sin, zero = 0.5 * factor * jnp.cos(angle), 0.5 * factor * jnp.sin(angle), jnp.zeros_like(angle)
    lane = lanes_of(shape)
    real = (lane // modes_x) % 2 == 0
    first = lane < 2 * modes_x
    from_re, from_im = jnp.where(real, cos, -sin), jnp.where(real, sin, cos)
    rows = [
        jnp.where(first, from_re, zero),
        jnp.where(first, from_im, zero),
        jnp.where(first, zero, from_re),
        jnp.where(first, zero, from_im),
    ]
    high, low = split(jnp.concatenate(rows, 0))
    xf_ref[...] = jnp.concatenate([high, low], 1)


def prepare(place, ky, kx, store, full_x, rows_x, width, count_y):
    modes_y, modes_x = ky.shape[0], kx.shape[0]
    shapes = (
        (2, 4 * 2 * modes_y, width),
        (2 * 2 * modes_y, width),
        (3 * 4 * modes_x, 4 * rows_x),
        (4 * rows_x, 8 * modes_x),
    )
    return pl.pallas_call(
        functools.partial(prepare_kernel, full_x=full_x, count_x=full_x // rows_x, count_y=count_y),
        out_shape=[jax.ShapeDtypeStruct(shape, jnp.bfloat16) for shape in shapes]
        + [jax.ShapeDtypeStruct((store.shape[1] * store.shape[2], 2 * store.shape[3]), jnp.float32)],
        in_specs=scalars(3) + whole(1),
        out_specs=whole(5),
        compiler_params=params(),
        cost_estimate=takes(2),
        name="prepare",
    )(place, ky, kx, store)


def duplicate(values):
    return jnp.concatenate([values, values], -1)


def pack_kernel(slots_hbm, spec_hbm, out_ref, slots_ref, spec_ref, sems):
    copies = [
        pltpu.make_async_copy(slots_hbm, slots_ref, sems.at[0]),
        pltpu.make_async_copy(spec_hbm, spec_ref, sems.at[1]),
    ]
    for copy in copies:
        copy.start()
    for copy in copies:
        copy.wait()
    local_x, local_y = slots_ref.shape
    modes = local_x * local_y
    groups = spec_ref.shape[0] // modes
    columns = []
    for group in range(groups // 2):
        for part in range(2):
            columns.append(spec_ref[pl.ds(group * 2 * modes + part, modes, stride=2)])
    shape = (modes, out_ref.shape[1] - groups * spec_ref.shape[1])
    row = rows_of(shape)
    numbers = jnp.zeros(shape, jnp.int32)
    for mode in range(modes):
        numbers = jnp.where(row == mode, slots_ref[mode % local_x, mode // local_x], numbers)
    out_ref[...] = jnp.concatenate(columns + [numbers.astype(jnp.float32)], 1)


def pack(slots, spectrum, lanes):
    modes = slots.size
    width = spectrum.size // modes + lanes
    return pl.pallas_call(
        pack_kernel,
        out_shape=jax.ShapeDtypeStruct((modes, width), jnp.float32),
        in_specs=outside(2),
        out_specs=whole(1)[0],
        scratch_shapes=[
            pltpu.SMEM(slots.shape, slots.dtype),
            pltpu.VMEM(spectrum.shape, spectrum.dtype),
            pltpu.SemaphoreType.DMA((2,)),
        ],
        compiler_params=params(60),
        name="pack",
    )(slots, spectrum)


def mix_kernel(place_ref, packed_ref, *refs, count, local_x):
    pieces, (kept_ref, slots_ref, out_ref, ra_ref, rb_ref, uc_ref, ud_ref) = refs[:count], refs[count:]
    planes, channels, lanes = out_ref.shape
    capacity = lanes // 2
    wide = pieces[0].shape[1] - lanes
    local_y = pieces[0].shape[0] // local_x
    for index, piece in enumerate(pieces):
        for mode in range(local_y):
            rows = pl.ds((mode * count + index) * local_x, local_x)
            slots_ref[rows] = piece[pl.ds(mode * local_x, local_x), pl.ds(wide, lanes)]
    numbers = jnp.transpose(jnp.concatenate([piece[:, pl.ds(wide, lanes)] for piece in pieces], 0))
    wanted = (place_ref[1] * capacity + rows_of(numbers.shape) % capacity).astype(jnp.float32)
    chosen = (numbers == wanted).astype(jnp.bfloat16)
    high, low = split(jnp.concatenate([piece[:, pl.ds(0, wide)] for piece in pieces], 0))
    placed = jnp.transpose(dot(chosen, high) + dot(chosen, low))
    kept_ref[...] = placed
    parts = placed.reshape(planes, 2, channels, lanes)
    first = lanes_of((channels, lanes)) < capacity
    for plane in range(planes):
        rows = pl.ds(plane * channels, channels)
        uc_ref[rows] = jnp.where(first, parts[plane, 0], parts[plane, 1])
        ud_ref[rows] = jnp.where(first, parts[plane, 1], parts[plane, 0])
    for part in range(channels):
        rows = pl.ds(part * channels, channels)
        block = packed_ref[rows]
        swapped = swap_halves(block)
        low_half = lanes_of(block.shape) < capacity
        ra_ref[rows] = jnp.where(low_half, block, swapped)
        rb_ref[rows] = jnp.where(low_half, -swapped, block)

    def step(channel, sums):
        ra = ra_ref[pl.ds(channel, channels, stride=channels)]
        rb = rb_ref[pl.ds(channel, channels, stride=channels)]
        return tuple(
            total
            + ra * uc_ref[pl.ds(plane * channels + channel, 1)]
            + rb * ud_ref[pl.ds(plane * channels + channel, 1)]
            for plane, total in enumerate(sums)
        )

    zero = jnp.zeros((channels, lanes), jnp.float32)
    sums = lax.fori_loop(0, channels, step, (zero,) * planes)
    for plane in range(planes):
        out_ref[plane] = sums[plane]


def mix(place, packed, pieces, planes, local_x):
    channels, lanes = math.isqrt(packed.shape[0]), packed.shape[1]
    count = len(pieces)
    return pl.pallas_call(
        functools.partial(mix_kernel, count=count, local_x=local_x),
        out_shape=[
            jax.ShapeDtypeStruct((2 * planes * channels, lanes), jnp.float32),
            jax.ShapeDtypeStruct((count * pieces[0].shape[0], lanes), jnp.float32),
            jax.ShapeDtypeStruct((planes, channels, lanes), jnp.float32),
        ],
        in_specs=scalars(1) + whole(1 + count),
        out_specs=whole(3),
        scratch_shapes=[pltpu.VMEM((channels * channels, lanes), jnp.float32)] * 2
        + [pltpu.VMEM((planes * channels, lanes), jnp.float32)] * 2,
        compiler_params=params(),
        cost_estimate=takes(3),
        name="mix",
    )(place, packed, *pieces)


def swap_halves(values):
    half = values.shape[-1] // 2
    return jnp.concatenate([values[..., half:], values[..., :half]], -1)


def weight_grad_kernel(place_ref, kept_ref, *refs):
    *pairs, out_ref, gs_ref = refs
    grads = [each.at[core] for each in pairs for core in range(2)]
    channels, lanes = grads[0].shape
    capacity = lanes // 2
    starts = []
    for index, grad in enumerate(grads):
        swapped = swap_halves(grad[...])
        gs_ref[index] = jnp.where(lanes_of(swapped.shape) < capacity, swapped, -swapped)
        starts.append((place_ref[1] ^ index) * 2 * channels)

    def step(channel, carry):
        total = jnp.zeros((channels, lanes), jnp.float32)
        for index, start in enumerate(starts):
            real = kept_ref[pl.ds(start, channels)]
            imag = kept_ref[pl.ds(start + channels, channels)]
            total = total + real * grads[index][pl.ds(channel, 1)] + imag * gs_ref[index, pl.ds(channel, 1)]
        out_ref[0, channel] = total[:, :capacity]
        out_ref[1, channel] = total[:, capacity:]
        return carry

    lax.fori_loop(0, channels, step, 0, unroll=4)


def weight_grad(place, kept, pairs):
    _, channels, lanes = pairs[0].shape
    return pl.pallas_call(
        weight_grad_kernel,
        out_shape=jax.ShapeDtypeStruct((2, channels, channels, lanes // 2), jnp.float32),
        in_specs=scalars(1) + whole(1 + len(pairs)),
        out_specs=whole(1)[0],
        scratch_shapes=[pltpu.VMEM((2 * len(pairs), channels, lanes), jnp.float32)],
        compiler_params=params(),
        cost_estimate=takes(2),
        name="weight_grad",
    )(place, kept, *pairs)


def fill_selection(slots_ref, chosen_ref, modes_x, capacity, flip=0):
    lanes = 2 * capacity
    shape = (modes_x, lanes)
    lane = lanes_of(shape)
    first = lane < capacity
    zero = jnp.zeros(shape, jnp.float32)
    for mode in range(slots_ref.shape[0] // modes_x):
        numbers = slots_ref[pl.ds(mode * modes_x, modes_x)]
        for owner in range(chosen_ref.shape[1] // lanes):
            wanted = ((owner ^ flip) * capacity + lane % capacity).astype(jnp.float32)
            hit = jnp.where(numbers == wanted, 1.0, 0.0)
            both = jnp.concatenate([jnp.where(first, hit, zero), jnp.where(first, zero, hit)], 0)
            chosen_ref[pl.ds(mode * 2 * modes_x, 2 * modes_x), pl.ds(owner * lanes, lanes)] = both.astype(jnp.bfloat16)


def slots_to_modes(blocks, chosen_ref, out_ref, modes_x):
    channels = blocks[0].shape[0]
    half = channels // 2
    high, low = split(jnp.concatenate(blocks, 1))
    found = dot_rows(jnp.concatenate([high, low], 0), chosen_ref[...])
    found = found[:channels] + found[channels:]
    local_y = found.shape[1] // (2 * modes_x)
    for mode in range(local_y):
        piece = found[:, mode * 2 * modes_x : (mode + 1) * 2 * modes_x]
        out_ref[pl.ds(mode, half, stride=local_y)] = jnp.concatenate([piece[:half], piece[half:]], 1)


def to_modes_kernel(slots_ref, in_ref, out_ref, chosen_ref, *, modes_x):
    owners, _, lanes = in_ref.shape
    fill_selection(slots_ref, chosen_ref, modes_x, lanes // 2)
    slots_to_modes([in_ref[owner] for owner in range(owners)], chosen_ref, out_ref, modes_x)


def to_modes(slots, values, modes_x):
    owners, channels, lanes = values.shape
    local_y = slots.shape[0] // modes_x
    return pl.pallas_call(
        functools.partial(to_modes_kernel, modes_x=modes_x),
        out_shape=jax.ShapeDtypeStruct((channels // 2 * local_y, 4 * modes_x), jnp.float32),
        in_specs=whole(2),
        out_specs=whole(1)[0],
        scratch_shapes=[pltpu.VMEM((2 * slots.shape[0], owners * lanes), jnp.bfloat16)],
        compiler_params=params(),
        cost_estimate=takes(1),
        name="to_modes",
    )(slots, values)


def adjoint_kernel(place_ref, slots_ref, *refs, modes_x, blocks, count):
    pieces, stores, refs = refs[:blocks], refs[blocks : -5], refs[-5:]
    same_ref, other_ref, out_ref, chosen_ref, sum_ref = refs
    _, channels, lanes = same_ref.shape
    half = channels // 2
    fill_selection(slots_ref, chosen_ref, modes_x, lanes // 2, place_ref[1])
    sum_ref[...] = sum(piece[...] for piece in pieces)
    local_y = sum_ref.shape[0] // half
    columns = []
    for mode in range(local_y):
        piece = sum_ref[pl.ds(mode, half, stride=local_y)]
        columns.append(jnp.concatenate([piece[:, : 2 * modes_x], piece[:, 2 * modes_x :]], 0))
    high, low = split(jnp.concatenate(columns, 1))
    found = dot(jnp.concatenate([high, low], 0), chosen_ref[...])
    found = found[:channels] + found[channels:]
    mixed = []
    for owner in range(count):
        values = found[:, owner * lanes : (owner + 1) * lanes]
        (other_ref if owner % 2 else same_ref)[owner // 2] = values
        swapped = swap_halves(values)
        real = jnp.zeros((channels, lanes), jnp.float32)
        imag = real
        for channel in range(channels):
            store, row = stores[owner], channel
            if owner >= count - 2:
                store = stores[owner + (2 if channel >= half else 0)]
                row = channel % half
            block = store[pl.ds(row * channels, channels)]
            real = real + block * values[channel : channel + 1]
            imag = imag + block * swapped[channel : channel + 1]
        other_re, other_im = swap_halves(real), swap_halves(imag)
        first = lanes_of(real.shape) < lanes // 2
        mixed.append(jnp.where(first, real + other_re, other_im - imag))
    slots_to_modes(mixed, chosen_ref, out_ref, modes_x)


def adjoint(place, slots, pieces, stores, modes_x):
    count, blocks = len(stores) - 2, len(pieces)
    lanes = stores[0].shape[1]
    channels = 2 * pieces[0].shape[0] * modes_x // slots.shape[0]
    return pl.pallas_call(
        functools.partial(adjoint_kernel, modes_x=modes_x, blocks=blocks, count=count),
        out_shape=[jax.ShapeDtypeStruct((count // 2, channels, lanes), jnp.float32)] * 2
        + [jax.ShapeDtypeStruct(pieces[0].shape, jnp.float32)],
        in_specs=scalars(1) + whole(1 + blocks + len(stores)),
        out_specs=whole(3),
        scratch_shapes=[
            pltpu.VMEM((2 * slots.shape[0], count * lanes), jnp.bfloat16),
            pltpu.VMEM(pieces[0].shape, jnp.float32),
        ],
        compiler_params=params(),
        cost_estimate=takes(3),
        name="adjoint",
    )(place, slots, *pieces, *stores)


def pair_kernel(same_ref, other_ref, *outs):
    for index, out in enumerate(outs):
        out[0] = same_ref[index]
        out[1] = other_ref[index]


def pair(same, other):
    return pl.pallas_call(
        pair_kernel,
        out_shape=[jax.ShapeDtypeStruct((2,) + same.shape[1:], same.dtype)] * same.shape[0],
        in_specs=whole(2),
        out_specs=whole(same.shape[0]),
        compiler_params=params(),
        cost_estimate=takes(0.3),
        name="pair",
    )(same, other)


def halves_kernel(first_ref, second_ref, low_ref, high_ref):
    half = low_ref.shape[0]
    low_ref[...] = first_ref[pl.ds(0, half)]
    high_ref[...] = second_ref[pl.ds(half, half)]


def halves(first, second):
    shape = (first.shape[0] // 2, first.shape[1])
    return pl.pallas_call(
        halves_kernel,
        out_shape=[jax.ShapeDtypeStruct(shape, first.dtype)] * 2,
        in_specs=whole(2),
        out_specs=whole(2),
        compiler_params=params(),
        cost_estimate=takes(0.3),
        name="halves",
    )(first, second)


def spread(small, rows, axis):
    count = small.shape[0]
    shape = (count * rows, count)
    take = (rows_of(shape) // rows == lanes_of(shape)).astype(jnp.bfloat16)
    shape = (count, count * rows)
    put = (lanes_of(shape) // rows == rows_of(shape)).astype(jnp.bfloat16)
    picked = dot(take, small) if axis else dot_rows(take, small)
    full = dot(picked.astype(jnp.bfloat16), put)
    shape = full.shape
    return jnp.where(rows_of(shape) % rows == lanes_of(shape) % rows, full, 0.0)


def pointwise_kernel(weight_ref, bias_ref, in_ref, out_ref, full_ref, shift_ref):
    channels, rows_x, width = in_ref.shape
    rows = full_ref.shape[0] // channels
    steps = rows_x // (2 * rows)

    full_ref[...] = spread(weight_ref[...], rows, 1).astype(jnp.bfloat16)
    for channel in range(channels):
        shift_ref[channel] = jnp.full(shift_ref.shape[1:], bias_ref[channel] * DENSITY, jnp.float32)

    def step(index, carry):
        values = in_ref[:, pl.ds(index * 2 * rows, 2 * rows), :].astype(jnp.float32)
        for half in range(2):
            block = values[:, half * rows : (half + 1) * rows].reshape(channels * rows, width)
            out = dot(full_ref[...], block.astype(jnp.bfloat16)).reshape(channels, rows, width)
            at = index * 2 * rows + half * rows
            out_ref[:, pl.ds(at, rows), :] = out * DENSITY + shift_ref[...]
        return carry

    lax.fori_loop(0, steps, step, 0)


def pointwise_map(weight, bias, values, rows=8):
    channels, rows_x, width = values.shape
    return pl.pallas_call(
        pointwise_kernel,
        out_shape=jax.ShapeDtypeStruct(values.shape, jnp.float32),
        in_specs=whole(1) + scalars(1) + whole(1),
        out_specs=whole(1)[0],
        scratch_shapes=[
            pltpu.VMEM((channels * rows, channels * rows), jnp.bfloat16),
            pltpu.VMEM((channels, rows, width), jnp.float32),
        ],
        compiler_params=params(),
        cost_estimate=takes(4),
        name="pointwise_map",
    )(weight, bias, values)


def pointwise_back_kernel(weight_ref, in_ref, out_ref, full_ref):
    channels, rows_x, width = in_ref.shape
    rows = full_ref.shape[0] // channels
    full_ref[...] = (0.5 * spread(weight_ref[...], rows, 0)).astype(jnp.bfloat16)

    def step(index, carry):
        block = in_ref[:, pl.ds(index * rows, rows), :].reshape(channels * rows, width)
        high, low = split(block)
        out = dot(full_ref[...], high) + dot(full_ref[...], low)
        out_ref[:, pl.ds(index * rows, rows), :] = out.reshape(channels, rows, width)
        return carry

    lax.fori_loop(0, rows_x // rows, step, 0)


def pointwise_back(weight, values, rows=8):
    channels = values.shape[0]
    return pl.pallas_call(
        pointwise_back_kernel,
        out_shape=jax.ShapeDtypeStruct(values.shape, jnp.float32),
        in_specs=whole(2),
        out_specs=whole(1)[0],
        scratch_shapes=[pltpu.VMEM((channels * rows, channels * rows), jnp.bfloat16)],
        compiler_params=params(),
        cost_estimate=takes(4),
        name="pointwise_back",
    )(weight, values)


def invert_x(pieces, xi_ref, st_ref):
    high, low = split(jnp.concatenate([piece[...] for piece in pieces], 0))
    deep = high.shape[1]
    left = jnp.concatenate([high, low], 1)
    found = dot(left, xi_ref[pl.ds(0, 2 * deep)]) + dot(high, xi_ref[pl.ds(2 * deep, deep)])
    st_ref[...] = found.reshape(st_ref.shape)


def spectral_part(index, half, st_ref, table):
    blocks, _, local_y, wide = st_ref.shape
    rows_x = wide // 4
    here = st_ref[:, index, :, pl.ds(half * 2 * rows_x, 2 * rows_x)].reshape(blocks * local_y, 2 * rows_x)
    parts = [here[:, :rows_x], here[:, rows_x:]]
    tall = jnp.transpose(jnp.concatenate(parts + parts, 0))
    high = tall.astype(jnp.bfloat16)
    first = lanes_of(tall.shape) < tall.shape[1] // 2
    mixed = jnp.where(first, tall, tall - high.astype(jnp.float32)).astype(jnp.bfloat16)
    return dot(jnp.concatenate([mixed, high], 1), table)


def slope_kernel(*refs, blocks):
    pieces, (xi_ref, ti_ref, tf_ref, xf_ref, mapped_ref, cot_ref) = refs[:blocks], refs[blocks : blocks + 6]
    (grad_ref, *sums), (st_ref, yt_ref) = refs[blocks + 6 : -2], refs[-2:]
    channels, rows_x, _ = mapped_ref.shape
    deep = tf_ref.shape[0] // 2
    modes_y = deep // 2
    local_y = modes_y // blocks
    invert_x(pieces, xi_ref, st_ref)

    def step(index, carry):
        for half in range(2):
            channel = half * (channels // 2) + index
            before = mapped_ref[channel] + spectral_part(index, half, st_ref, ti_ref[0])
            grad = cot_ref[channel].astype(jnp.float32) * twice_gelu_slope(before)
            grad_ref[channel] = grad
            high, low = split(grad)
            both = dot_rows(tf_ref[...], high)
            found = both[:deep] + both[deep:] + dot_rows(tf_ref[pl.ds(0, deep)], low)
            for block in range(blocks):
                for part in range(2):
                    at = part * modes_y + block * local_y
                    columns = pl.ds((2 * half + part) * rows_x, rows_x)
                    yt_ref[block, index, :, columns] = found[at : at + local_y]
        return carry

    lax.fori_loop(0, channels // 2, step, 0, unroll=2)
    high, low = split(yt_ref[...].reshape(-1, yt_ref.shape[-1]))
    lanes = xf_ref.shape[1] // 2
    both = dot(high, xf_ref[...])
    total = both[:, :lanes] + both[:, lanes:] + dot(low, xf_ref[:, :lanes])
    rows = total.shape[0] // blocks
    for block in range(blocks):
        sums[block][...] = total[block * rows : (block + 1) * rows]


def slope_step(pieces, tables, mapped, cotangent):
    ti, tf, xi, xf = tables
    blocks = len(pieces)
    channels, rows_x, _ = mapped.shape
    half = channels // 2
    local_y = pieces[0].shape[0] // half
    grad, *sums = pl.pallas_call(
        functools.partial(slope_kernel, blocks=blocks),
        out_shape=[jax.ShapeDtypeStruct(mapped.shape, jnp.float32)]
        + [jax.ShapeDtypeStruct(pieces[0].shape, jnp.float32)] * blocks,
        in_specs=whole(blocks + 6),
        out_specs=whole(1 + blocks),
        scratch_shapes=[pltpu.VMEM((blocks, half, local_y, 4 * rows_x), jnp.float32)] * 2,
        compiler_params=params(),
        cost_estimate=takes(13),
        name="slope_step",
    )(*pieces, xi, ti, tf, xf, mapped, cotangent)
    return grad, sums


def finish_kernel(*refs, blocks, group):
    pieces, (xi_ref, ti_ref, part_ref, out_ref, st_ref, sum_ref, sems) = refs[:blocks], refs[blocks:]
    channels = part_ref.shape[0]
    invert_x(pieces, xi_ref, st_ref)

    def copies(index):
        for half in range(2):
            rows = pl.ds(half * (channels // 2) + index * group, group)
            yield pltpu.make_async_copy(sum_ref.at[rows], out_ref.at[rows], sems.at[half, index])

    def step(index, carry):
        for half in range(2):
            for member in range(group):
                place = index * group + member
                channel = half * (channels // 2) + place
                sum_ref[channel] = part_ref[channel] + spectral_part(place, half, st_ref, ti_ref[1])
        for copy in copies(index):
            copy.start()
        return carry

    def settle(index, carry):
        for copy in copies(index):
            copy.wait()
        return carry

    steps = channels // (2 * group)
    lax.fori_loop(0, steps, step, 0)
    lax.fori_loop(0, steps, settle, 0)


def finish(pieces, tables, part, group=2):
    ti, _, xi, _ = tables
    blocks = len(pieces)
    channels, rows_x, _ = part.shape
    half = channels // 2
    local_y = pieces[0].shape[0] // half
    return pl.pallas_call(
        functools.partial(finish_kernel, blocks=blocks, group=group),
        out_shape=jax.ShapeDtypeStruct(part.shape, jnp.float32),
        in_specs=whole(blocks + 3),
        out_specs=outside(1)[0],
        scratch_shapes=[
            pltpu.VMEM((blocks, half, local_y, 4 * rows_x), jnp.float32),
            pltpu.VMEM(part.shape, jnp.float32),
            pltpu.SemaphoreType.DMA((2, half // group)),
        ],
        compiler_params=params(20),
        cost_estimate=takes(4),
        name="finish",
    )(*pieces, xi, ti, part)


def exchange(piece, axis, count, flip):
    return lax.ppermute(piece, axis, [(i, i ^ flip) for i in range(count)])


def between_chips(piece, count):
    return [piece] + [exchange(piece, "py", count, step) for step in range(2, count, 2)]


def between_cores(pieces, count):
    other = [exchange(piece, "py", count, 1) for piece in pieces]
    return [each for pair in zip(pieces, other) for each in pair]


def from_all(piece, axis, count):
    return [piece] + [exchange(piece, axis, count, step) for step in range(1, count)]


def to_all(pieces, axis, count):
    return pieces[:1] + [exchange(pieces[step], axis, count, step) for step in range(1, count)]


def on_device_packed(
    field_in,
    cotangent,
    spectrum_saved,
    weight_store,
    block_slot,
    kx_modes,
    ky_modes,
    pointwise,
    bias_vector,
):
    channels, _, rows_x, width_y = field_in.shape
    count_x, count_y = lax.axis_size("px"), lax.axis_size("py")
    full_x = rows_x * count_x
    planes, local_y, local_x = spectrum_saved.shape[1:4]
    modes_x = kx_modes.shape[0]
    place_x, place_y = lax.axis_index("px"), lax.axis_index("py")
    lanes = 2 * weight_store.shape[0]
    store = jnp.transpose(weight_store, (1, 2, 3, 0))
    place = jnp.stack([place_x, place_y])

    barrier = lax.optimization_barrier
    slots, spectrum, place = barrier((block_slot, spectrum_saved, place))
    spectrum = jnp.transpose(spectrum, (1, 2, 3, 4, 0)).reshape(-1, channels)
    pieces = between_chips(pack(slots, spectrum, lanes), count_y)
    *tables, packed = prepare(place, ky_modes, kx_modes, store, full_x, rows_x, width_y, count_y)
    pieces, tables, packed = barrier((pieces, tables, packed))
    pieces, packed = barrier((between_cores(pieces, count_y), packed))
    kept, slots, mixed = mix(place, packed, pieces, planes, local_x)
    stores = [packed, exchange(packed, "py", count_y, 2), exchange(packed, "py", count_y, 4)]
    mixed = lax.all_to_all(mixed, "py", split_axis=0, concat_axis=0, tiled=True)
    mixed, stores = barrier((mixed, stores))
    low, high = halves(*stores[1:])
    far = [exchange(low, "py", count_y, 4), exchange(high, "py", count_y, 2)]
    received = from_all(to_modes(slots, mixed, modes_x), "px", count_x)
    mapped = pointwise_map(pointwise, bias_vector, field_in[:, 0])
    received, mapped, far = barrier((received, mapped, far))
    stores = between_cores(stores, count_y)
    far = between_cores(far, count_y)
    stores = stores + [far[0], far[1], far[2], far[3]]
    grad, sums = slope_step(received, tables, mapped, cotangent[:, 0])
    sums, grad, stores = barrier((list(sums), grad, stores))
    received = to_all(sums, "px", count_x)
    back = pointwise_back(pointwise, grad)
    received, back = barrier((received, back))
    same, other, mixed = adjoint(place, slots, received, stores, modes_x)
    received = from_all(mixed, "px", count_x)
    pairs = list(pair(same, exchange(other, "py", count_y, 1)))
    pairs = pairs[:1] + [exchange(pairs[i], "py", count_y, 2 * i) for i in range(1, len(pairs))]
    field_grad = finish(received, tables, back)
    blocks = weight_grad(place, kept, pairs)
    return (field_grad[:, None], jnp.transpose(blocks, (3, 0, 1, 2)))


def packs(mesh, channels, planes, rows, width, modes, capacity):
    count_x, count_y = mesh.shape["px"], mesh.shape["py"]
    powers = all(size & (size - 1) == 0 for size in (rows, width))
    return (
        powers
        and (count_x, count_y, planes) == (4, 8, 8)
        and channels == 32
        and 4 * modes == 128
        and 2 * capacity == 128
        and rows // count_x == 128
        and width % 256 == 0
        and modes // count_x == 8
    )


def solution(mesh):
    placed = (
        P(None, "py", "px", None),
        P(None, "py", "px", None),
        P(None, None, "px", "py", None),
        P(("px", "py"), None, None, None),
        P("py", "px"),
        P(),
        P(),
        P(),
        P(),
    )

    def run(*args):
        channels, planes, rows, width = args[0].shape
        capacity = args[3].shape[0] // mesh.size
        packed = packs(mesh, channels, planes, rows, width, args[5].shape[0], capacity)
        return jax.shard_map(
            on_device_packed if packed else on_device,
            mesh=mesh,
            in_specs=placed,
            out_specs=(P(None, "py", "px", None), P(("px", "py"), None, None, None)),
            check_vma=False,
        )(*args)

    return run
```

```python
import functools
import math

import jax
import jax.numpy as jnp
from jax import lax
from jax.experimental import pallas as pl
from jax.experimental.pallas import tpu as pltpu
from jax.sharding import PartitionSpec as P

precise = lax.Precision.HIGHEST


def phase_table(length, modes):
    points = lax.iota(jnp.int32, length)
    wrapped = points[:, None] * modes[None, :] % length
    angle = wrapped.astype(jnp.float32) * (2.0 * math.pi / length)
    return (jnp.cos(angle), jnp.sin(angle))


def gelu_slope(values):
    normal_cdf = 0.5 * (1.0 + lax.erf(values * 0.7071067811865476))
    density = jnp.exp(-0.5 * values * values) * 0.3989422804014327
    return normal_cdf + values * density


def channel_mix(blocks, spectrum):
    block_re = blocks[:, :, 0]
    block_im = blocks[:, :, 1]
    spec_re = spectrum[..., 0]
    spec_im = spectrum[..., 1]
    form = "baoc,czba->ozba"
    out_re = jnp.einsum(form, block_re, spec_re, precision=precise) - jnp.einsum(
        form, block_im, spec_im, precision=precise
    )
    out_im = jnp.einsum(form, block_re, spec_im, precision=precise) + jnp.einsum(
        form, block_im, spec_re, precision=precise
    )
    return jnp.stack([out_re, out_im], -1)


def channel_adjoint(blocks, spectrum):
    block_re = blocks[:, :, 0]
    block_im = blocks[:, :, 1]
    grad_re = spectrum[..., 0]
    grad_im = spectrum[..., 1]
    form = "baoc,ozba->czba"
    out_re = jnp.einsum(form, block_re, grad_re, precision=precise) + jnp.einsum(
        form, block_im, grad_im, precision=precise
    )
    out_im = jnp.einsum(form, block_re, grad_im, precision=precise) - jnp.einsum(
        form, block_im, grad_re, precision=precise
    )
    return jnp.stack([out_re, out_im], -1)


def block_gradient(spectrum_grad, spectrum):
    grad_re = spectrum_grad[..., 0]
    grad_im = spectrum_grad[..., 1]
    spec_re = spectrum[..., 0]
    spec_im = spectrum[..., 1]
    form = "ozba,czba->aboc"
    out_re = jnp.einsum(form, grad_re, spec_re, precision=precise) + jnp.einsum(
        form, grad_im, spec_im, precision=precise
    )
    out_im = jnp.einsum(form, grad_im, spec_re, precision=precise) - jnp.einsum(
        form, grad_re, spec_im, precision=precise
    )
    return jnp.stack([out_re, out_im], 2)


def invert_rows(spectrum, cos_rows, sin_rows):
    spec_re = spectrum[..., 0]
    spec_im = spectrum[..., 1]
    form = "czma,xa->czmx"
    back_re = jnp.einsum(form, spec_re, cos_rows, precision=precise) - jnp.einsum(
        form, spec_im, sin_rows, precision=precise
    )
    back_im = jnp.einsum(form, spec_re, sin_rows, precision=precise) + jnp.einsum(
        form, spec_im, cos_rows, precision=precise
    )
    joined = jnp.stack([back_re, back_im], 3)
    return joined.reshape(joined.shape[0], joined.shape[1], 2 * joined.shape[2], joined.shape[4])


def on_device(
    field_in,
    cotangent,
    spectrum_saved,
    weight_store,
    block_slot,
    kx_modes,
    ky_modes,
    pointwise,
    bias_vector,
):
    channels, planes, rows_x, width_y = field_in.shape
    full_x = rows_x * lax.axis_size("px")
    modes_y = ky_modes.shape[0]
    local_y = modes_y // lax.axis_size("px")
    capacity = weight_store.shape[0]
    factor = 1.0 / math.sqrt(full_x * width_y)
    cos_y, sin_y = phase_table(width_y, ky_modes)
    table_y = jnp.stack([cos_y, -sin_y], 2).reshape(width_y, 2 * modes_y)
    cos_x, sin_x = phase_table(full_x, kx_modes)
    store_row, slots_row = (
        lax.all_gather(weight_store, "py", axis=0, tiled=True),
        lax.all_gather(block_slot, "py", axis=0, tiled=True),
    )
    slots_flat = slots_row.reshape(-1)

    def inverse_planes(spectrum):
        joined = invert_rows(spectrum, cos_x, sin_x)
        returned = lax.all_to_all(joined, "px", split_axis=3, concat_axis=2, tiled=True)
        return factor * jnp.einsum("czkx,yk->czxy", returned, table_y, precision=precise)

    weight_full = pointwise.astype(jnp.float32)
    local_x = block_slot.shape[0]
    indices = jnp.transpose(block_slot).reshape(-1)
    blocks = jnp.take(store_row, indices, axis=0).reshape(local_y, local_x, 2, channels, channels)
    mixed = channel_mix(blocks, spectrum_saved)

    def from_modes(spectrum):
        return lax.all_to_all(spectrum, "py", split_axis=1, concat_axis=3, tiled=True)

    spectral = inverse_planes(from_modes(mixed))
    mapped = jnp.einsum("oc,czxy->ozxy", pointwise, field_in, preferred_element_type=jnp.float32)
    grad = cotangent.astype(jnp.float32) * gelu_slope(
        mapped + bias_vector.reshape(channels, 1, 1, 1) + spectral
    )
    partial_value = jnp.einsum("czxy,yk->czkx", grad, table_y, precision=precise)
    moved = lax.all_to_all(partial_value, "px", split_axis=2, concat_axis=3, tiled=True)
    pieces = moved.reshape(channels, planes, local_y, 2, full_x)
    part_re = pieces[:, :, :, 0]
    part_im = pieces[:, :, :, 1]
    form = "czmx,xk->czmk"
    real_part = jnp.einsum(form, part_re, cos_x, precision=precise) + jnp.einsum(
        form, part_im, sin_x, precision=precise
    )
    imag_part = jnp.einsum(form, part_im, cos_x, precision=precise) - jnp.einsum(
        form, part_re, sin_x, precision=precise
    )
    spectrum_grad = lax.all_to_all(
        factor * jnp.stack([real_part, imag_part], -1),
        "py",
        split_axis=3,
        concat_axis=1,
        tiled=True,
    )
    input_spectrum = channel_adjoint(blocks, spectrum_grad)
    local_grad = block_gradient(spectrum_grad, spectrum_saved)
    field_grad = jnp.einsum("oc,ozxy->czxy", weight_full, grad, precision=precise) + inverse_planes(
        from_modes(input_spectrum)
    )
    grads_all = lax.all_gather(local_grad, "py", axis=0, tiled=True)
    grads_flat = grads_all.reshape(slots_flat.shape[0], 2 * channels * channels)
    targets = lax.axis_index("py") * capacity + lax.iota(jnp.int32, capacity)
    select = (targets[:, None] == slots_flat[None, :]).astype(jnp.float32)
    store_flat = jnp.dot(select, grads_flat, precision=precise)
    store_grad = store_flat.reshape(capacity, 2, channels, channels)
    return (field_grad, store_grad)


def place_of():
    return lax.axis_index("px"), lax.axis_index("py")


def split(values):
    high = values.astype(jnp.bfloat16)
    return high, (values - high.astype(jnp.float32)).astype(jnp.bfloat16)


def dot(left, right):
    return jnp.dot(left, right, preferred_element_type=jnp.float32)


def dot_rows(left, right):
    return lax.dot_general(left, right, (((1,), (1,)), ((), ())), preferred_element_type=jnp.float32)


def lanes_of(shape):
    return lax.broadcasted_iota(jnp.int32, shape, len(shape) - 1)


def rows_of(shape):
    return lax.broadcasted_iota(jnp.int32, shape, len(shape) - 2)


def whole(count):
    return [pl.BlockSpec(memory_space=pltpu.VMEM)] * count


def params(mebibytes=12):
    return pltpu.CompilerParams(vmem_limit_bytes=mebibytes * 1024 * 1024)


def takes(microseconds):
    return pl.CostEstimate(flops=int(microseconds * 10**9), bytes_accessed=2**20, transcendentals=0)


def outside(count):
    return [pl.BlockSpec(memory_space=pltpu.HBM)] * count


def scalars(count):
    return [pl.BlockSpec(memory_space=pltpu.SMEM)] * count


DENSITY = math.sqrt(2.0 / math.pi)


def twice_gelu_slope(scaled):
    normal = 1.0 + lax.erf(scaled * (math.sqrt(0.5) / DENSITY))
    return normal + scaled * jnp.exp2(scaled * scaled * (-0.5 * math.log2(math.e) / DENSITY**2))


def column_of(ref, start, count):
    shape = (count, 128)
    row = rows_of(shape)
    out = jnp.zeros(shape, ref.dtype)
    for i in range(count):
        out = jnp.where(row == i, ref[start(i)], out)
    return out


def prepare_kernel(
    small_ref,
    store_ref,
    piece_ref,
    ti_ref,
    tf_ref,
    xi_ref,
    xf_ref,
    packed_ref,
    map_ref,
    back_ref,
    shift_ref,
    kept_ref,
    *,
    full_x,
    modes_y,
    modes_x,
):
    kept_ref[...] = piece_ref[...]
    channels, width = store_ref.shape[1], tf_ref.shape[1]
    rows = map_ref.shape[0] // channels
    ky = small_ref[pl.ds(0, modes_y)].astype(jnp.int32)
    kx = small_ref[pl.ds(modes_y, modes_x)].astype(jnp.int32)
    bias = small_ref[pl.ds(modes_y + modes_x, channels)] * DENSITY
    weight = small_ref[pl.ds(modes_y + modes_x + channels, channels), :][:, :channels].astype(jnp.bfloat16)
    map_ref[...] = spread(weight, rows, 1, lambda i: i).astype(jnp.bfloat16)
    pairs = channels // 4
    back = spread(weight, rows, 0, lambda i: i % 2 * 2 * pairs + i // 2 % pairs * 2 + i // (2 * pairs))
    back_ref[...] = (0.5 * back).astype(jnp.bfloat16)
    for channel in range(channels):
        shift_ref[pl.ds(channel * rows, rows)] = jnp.broadcast_to(bias[channel : channel + 1], (rows, bias.shape[1]))
        packed = jnp.concatenate([store_ref[0, channel], store_ref[1, channel]], 1)
        packed_ref[pl.ds(channel * store_ref.shape[2], store_ref.shape[2])] = packed
    rows_x = xf_ref.shape[0] // 4
    factor = 1.0 / math.sqrt(full_x * width)
    start = place_of()[0] * rows_x

    def angles(modes, points, length):
        return ((modes * points) & (length - 1)).astype(jnp.float32) * (2.0 * math.pi / length)

    ky = jnp.concatenate([ky] * (width // ky.shape[1]), 1)
    angle = angles(ky, lanes_of(ky.shape), width)
    waves = jnp.concatenate([jnp.cos(angle), -jnp.sin(angle)], 0)
    high, low = split(waves)
    tf_ref[...] = jnp.concatenate([high, low], 0)
    for index, scale in enumerate((DENSITY, 1.0)):
        high, low = split(scale * waves)
        ti_ref[index] = jnp.concatenate([high, high, low, jnp.zeros_like(low)], 0)
    angle = angles(kx, start + lanes_of((modes_x, rows_x)), full_x)
    cos, sin, zero = factor * jnp.cos(angle), factor * jnp.sin(angle), jnp.zeros_like(angle)
    parts = [[cos, sin, zero, zero], [-sin, cos, zero, zero], [zero, zero, cos, sin], [zero, zero, -sin, cos]]
    high, low = split(jnp.concatenate([jnp.concatenate(part, 1) for part in parts], 0))
    xi_ref[...] = jnp.concatenate([high, high, low], 0)
    cos = 0.5 * jnp.transpose(jnp.concatenate([cos] * 4, 0))
    sin = 0.5 * jnp.transpose(jnp.concatenate([sin] * 4, 0))
    zero = jnp.zeros_like(cos)
    lane = lanes_of(cos.shape)
    real = (lane // modes_x) % 2 == 0
    first = lane < 2 * modes_x
    from_re, from_im = jnp.where(real, cos, -sin), jnp.where(real, sin, cos)
    parts = [
        jnp.where(first, from_re, zero),
        jnp.where(first, from_im, zero),
        jnp.where(first, zero, from_re),
        jnp.where(first, zero, from_im),
    ]
    high, low = split(jnp.concatenate(parts, 0))
    xf_ref[...] = jnp.concatenate([high, low], 1)


def prepare(small, store, piece, full_x, rows_x, width, modes_y, modes_x, rows=8):
    channels, capacity = store.shape[2:]
    shapes = (
        (2, 4 * 2 * modes_y, width),
        (2 * 2 * modes_y, width),
        (3 * 4 * modes_x, 4 * rows_x),
        (4 * rows_x, 8 * modes_x),
        (channels * channels, 2 * capacity),
        (channels * rows, channels * rows),
        (channels * rows, channels * rows),
        (channels * rows, small.shape[1]),
        piece.shape,
    )
    types = [jnp.float32 if i in (4, 7, 8) else jnp.bfloat16 for i in range(len(shapes))]
    *tables, packed, full_map, full_back, shift, piece = pl.pallas_call(
        functools.partial(prepare_kernel, full_x=full_x, modes_y=modes_y, modes_x=modes_x),
        out_shape=[jax.ShapeDtypeStruct(*each) for each in zip(shapes, types)],
        in_specs=whole(3),
        out_specs=whole(len(shapes)),
        compiler_params=params(),
        cost_estimate=takes(2),
        name="prepare",
    )(small, store, piece)
    return tables, packed, full_map, full_back, shift, piece


def duplicate(values):
    return jnp.concatenate([values, values], -1)


def pack_kernel(*refs):
    sources, (out_ref, small_ref), (*targets, sems) = refs[:6], refs[6:8], refs[8:]
    copies = [pltpu.make_async_copy(*pair, sems.at[i]) for i, pair in enumerate(zip(sources, targets))]
    for copy in copies:
        copy.start()
    for copy in copies:
        copy.wait()
    slots_ref, spec_ref, ky_ref, kx_ref, bias_ref, weight_ref = targets
    place_x, place_y = place_of()
    local_x, local_y = slots_ref.shape
    modes = local_x * local_y
    groups = spec_ref.shape[0] // modes
    columns = []
    for group in range(groups // 2):
        for part in range(2):
            columns.append(spec_ref[pl.ds(group * 2 * modes + part, modes, stride=2)])
    lanes = out_ref.shape[1] - groups * spec_ref.shape[1]
    numbers = column_of(slots_ref, lambda i: (i % local_x, i // local_x), modes)
    out_ref[...] = jnp.concatenate(columns + [numbers.astype(jnp.float32)], 1)
    modes_y, modes_x, channels = ky_ref.shape[0], kx_ref.shape[0], bias_ref.shape[0]
    ky = column_of(ky_ref, lambda i: (place_x ^ (i // local_y)) * local_y + i % local_y, modes_y)
    kx = column_of(kx_ref, lambda i: (place_y ^ (i // local_x)) * local_x + i % local_x, modes_x)
    bias = column_of(bias_ref, lambda i: i, channels)
    weight = weight_ref[...].astype(jnp.float32)
    weight = jnp.concatenate([weight, jnp.zeros((channels, lanes - channels), jnp.float32)], 1)
    small_ref[...] = jnp.concatenate([ky.astype(jnp.float32), kx.astype(jnp.float32), bias, weight], 0)


def pack(slots, spectrum, ky, kx, bias, weight, lanes):
    modes = slots.size
    width = spectrum.size // modes + lanes
    sources = (slots, spectrum, ky, kx, bias, weight)
    held = (pltpu.SMEM, pltpu.VMEM, pltpu.SMEM, pltpu.SMEM, pltpu.SMEM, pltpu.VMEM)
    rows = ky.shape[0] + kx.shape[0] + bias.shape[0] + weight.shape[0]
    return pl.pallas_call(
        pack_kernel,
        out_shape=[
            jax.ShapeDtypeStruct((modes, width), jnp.float32),
            jax.ShapeDtypeStruct((rows, lanes), jnp.float32),
        ],
        in_specs=outside(6),
        out_specs=whole(2),
        scratch_shapes=[space(each.shape, each.dtype) for space, each in zip(held, sources)]
        + [pltpu.SemaphoreType.DMA((6,))],
        compiler_params=params(60),
        name="pack",
    )(*sources)


def mix_kernel(packed_ref, *refs, count, local_x):
    pieces, refs = refs[:count], refs[count:]
    kept_ref, slots_ref, same_ref, other_ref, out_ref, ra_ref, rb_ref, uc_ref, ud_ref = refs
    planes, channels, lanes = out_ref.shape
    place = place_of()[1]
    capacity = lanes // 2
    wide = pieces[0].shape[1] - lanes
    local_y = pieces[0].shape[0] // local_x
    for index, piece in enumerate(pieces):
        for mode in range(local_y):
            rows = pl.ds((mode * count + index) * local_x, local_x)
            slots_ref[rows] = piece[pl.ds(mode * local_x, local_x), pl.ds(wide, lanes)]
    numbers = jnp.transpose(jnp.concatenate([piece[:, pl.ds(wide, lanes)] for piece in pieces], 0))
    wanted = (place * capacity + rows_of(numbers.shape) % capacity).astype(jnp.float32)
    chosen = (numbers == wanted).astype(jnp.bfloat16)
    high, low = split(jnp.concatenate([piece[:, pl.ds(0, wide)] for piece in pieces], 0))
    placed = jnp.transpose(dot(chosen, high) + dot(chosen, low))
    kept_ref[...] = placed
    parts = placed.reshape(planes, 2, channels, lanes)
    first = lanes_of((channels, lanes)) < capacity
    for plane in range(planes):
        rows = pl.ds(plane * channels, channels)
        uc_ref[rows] = jnp.where(first, parts[plane, 0], parts[plane, 1])
        ud_ref[rows] = jnp.where(first, parts[plane, 1], parts[plane, 0])
    for part in range(channels):
        rows = pl.ds(part * channels, channels)
        block = packed_ref[rows]
        swapped = swap_halves(block)
        low_half = lanes_of(block.shape) < capacity
        ra_ref[rows] = jnp.where(low_half, block, swapped)
        rb_ref[rows] = jnp.where(low_half, -swapped, block)

    def step(channel, sums):
        ra = ra_ref[pl.ds(channel, channels, stride=channels)]
        rb = rb_ref[pl.ds(channel, channels, stride=channels)]
        return tuple(
            total
            + ra * uc_ref[pl.ds(plane * channels + channel, 1)]
            + rb * ud_ref[pl.ds(plane * channels + channel, 1)]
            for plane, total in enumerate(sums)
        )

    zero = jnp.zeros((channels, lanes), jnp.float32)
    sums = lax.fori_loop(0, channels, step, (zero,) * planes, unroll=4)
    for plane in range(planes):
        out_ref[plane] = sums[plane]
    for step in range(planes):
        (other_ref if step % 2 else same_ref)[step // 2] = out_ref[place ^ step]


def mix(packed, pieces, planes, local_x):
    channels, lanes = math.isqrt(packed.shape[0]), packed.shape[1]
    count = len(pieces)
    return pl.pallas_call(
        functools.partial(mix_kernel, count=count, local_x=local_x),
        out_shape=[
            jax.ShapeDtypeStruct((2 * planes * channels, lanes), jnp.float32),
            jax.ShapeDtypeStruct((count * pieces[0].shape[0], lanes), jnp.float32),
            jax.ShapeDtypeStruct((planes // 2, channels, lanes), jnp.float32),
            jax.ShapeDtypeStruct((planes // 2, channels, lanes), jnp.float32),
        ],
        in_specs=whole(1 + count),
        out_specs=whole(4),
        scratch_shapes=[pltpu.VMEM((planes, channels, lanes), jnp.float32)]
        + [pltpu.VMEM((channels * channels, lanes), jnp.float32)] * 2
        + [pltpu.VMEM((planes * channels, lanes), jnp.float32)] * 2,
        compiler_params=params(),
        cost_estimate=takes(3),
        name="mix",
    )(packed, *pieces)


def swap_halves(values):
    half = values.shape[-1] // 2
    return jnp.concatenate([values[..., half:], values[..., :half]], -1)


def weight_grad_kernel(kept_ref, *refs):
    *pairs, out_ref, gs_ref, sum_ref, sems = refs
    grads = [each.at[core] for each in pairs for core in range(2)]
    channels, lanes = grads[0].shape
    capacity = lanes // 2
    starts = []
    for index, grad in enumerate(grads):
        swapped = swap_halves(grad[...])
        gs_ref[index] = jnp.where(lanes_of(swapped.shape) < capacity, swapped, -swapped)
        starts.append((place_of()[1] ^ index) * 2 * channels)
    chunks = sems.shape[0]
    size = channels // chunks

    def send(chunk):
        rows = pl.ds(chunk * size, size)
        return pltpu.make_async_copy(sum_ref.at[:, rows], out_ref.at[:, rows], sems.at[chunk])

    def step(pair, carry):
        totals = [jnp.zeros((channels, lanes), jnp.float32)] * 2
        for index, start in enumerate(starts):
            real = kept_ref[pl.ds(start, channels)]
            imag = kept_ref[pl.ds(start + channels, channels)]
            for each in range(2):
                row = pl.ds(2 * pair + each, 1)
                totals[each] = totals[each] + real * grads[index][row] + imag * gs_ref[index, row]
        for each, total in enumerate(totals):
            sum_ref[0, 2 * pair + each] = total[:, :capacity]
            sum_ref[1, 2 * pair + each] = total[:, capacity:]
        return carry

    for chunk in range(chunks):
        lax.fori_loop(chunk * size // 2, (chunk + 1) * size // 2, step, 0, unroll=2)
        send(chunk).start()
    for chunk in range(chunks):
        send(chunk).wait()


def weight_grad(kept, pairs, chunks=4):
    _, channels, lanes = pairs[0].shape
    shape = (2, channels, channels, lanes // 2)
    return pl.pallas_call(
        weight_grad_kernel,
        out_shape=jax.ShapeDtypeStruct(shape, jnp.float32),
        in_specs=whole(1 + len(pairs)),
        out_specs=outside(1)[0],
        scratch_shapes=[
            pltpu.VMEM((2 * len(pairs), channels, lanes), jnp.float32),
            pltpu.VMEM(shape, jnp.float32),
            pltpu.SemaphoreType.DMA((chunks,)),
        ],
        compiler_params=params(),
        cost_estimate=takes(2),
        name="weight_grad",
    )(kept, *pairs)


def fill_selection(slots_ref, chosen_ref, modes_x, capacity, flip=0):
    lanes = 2 * capacity
    shape = (modes_x, lanes)
    lane = lanes_of(shape)
    first = lane < capacity
    zero = jnp.zeros(shape, jnp.float32)
    for mode in range(slots_ref.shape[0] // modes_x):
        numbers = slots_ref[pl.ds(mode * modes_x, modes_x)]
        for owner in range(chosen_ref.shape[1] // lanes):
            wanted = ((owner ^ flip) * capacity + lane % capacity).astype(jnp.float32)
            hit = jnp.where(numbers == wanted, 1.0, 0.0)
            both = jnp.concatenate([jnp.where(first, hit, zero), jnp.where(first, zero, hit)], 0)
            chosen_ref[pl.ds(mode * 2 * modes_x, 2 * modes_x), pl.ds(owner * lanes, lanes)] = both.astype(jnp.bfloat16)


def slots_to_modes(blocks, chosen_ref, out_ref, modes_x):
    channels = blocks[0].shape[0]
    half = channels // 2
    high, low = split(jnp.concatenate(blocks, 1))
    found = dot_rows(jnp.concatenate([high, low], 0), chosen_ref[...])
    found = found[:channels] + found[channels:]
    local_y = found.shape[1] // (2 * modes_x)
    for mode in range(local_y):
        piece = found[:, mode * 2 * modes_x : (mode + 1) * 2 * modes_x]
        out_ref[pl.ds(mode, half, stride=local_y)] = jnp.concatenate([piece[:half], piece[half:]], 1)


def to_modes_kernel(slots_ref, *refs, modes_x):
    *pairs, out_ref, chosen_ref = refs
    lanes = pairs[0].shape[2]
    fill_selection(slots_ref, chosen_ref, modes_x, lanes // 2, place_of()[1])
    slots_to_modes([pair[core] for pair in pairs for core in range(2)], chosen_ref, out_ref, modes_x)


def to_modes(slots, pairs, modes_x):
    _, channels, lanes = pairs[0].shape
    local_y = slots.shape[0] // modes_x
    return pl.pallas_call(
        functools.partial(to_modes_kernel, modes_x=modes_x),
        out_shape=jax.ShapeDtypeStruct((channels // 2 * local_y, 4 * modes_x), jnp.float32),
        in_specs=whole(1 + len(pairs)),
        out_specs=whole(1)[0],
        scratch_shapes=[pltpu.VMEM((2 * slots.shape[0], 2 * len(pairs) * lanes), jnp.bfloat16)],
        compiler_params=params(),
        cost_estimate=takes(1),
        name="to_modes",
    )(slots, *pairs)


def adjoint_kernel(slots_ref, *refs, modes_x, blocks, count):
    pieces, stores, refs = refs[:blocks], refs[blocks:-5], refs[-5:]
    place = place_of()[1]
    same_ref, other_ref, out_ref, chosen_ref, sum_ref = refs
    _, channels, lanes = same_ref.shape
    half = channels // 2
    fill_selection(slots_ref, chosen_ref, modes_x, lanes // 2, place)
    sum_ref[...] = sum(piece[...] for piece in pieces)
    local_y = sum_ref.shape[0] // half
    columns = []
    for mode in range(local_y):
        piece = sum_ref[pl.ds(mode, half, stride=local_y)]
        columns.append(jnp.concatenate([piece[:, : 2 * modes_x], piece[:, 2 * modes_x :]], 0))
    high, low = split(jnp.concatenate(columns, 1))
    found = dot(jnp.concatenate([high, low], 0), chosen_ref[...])
    found = found[:channels] + found[channels:]
    mixed = []
    for owner in range(count):
        values = found[:, owner * lanes : (owner + 1) * lanes]
        (other_ref if owner % 2 else same_ref)[owner // 2] = values
        swapped = swap_halves(values)
        real = jnp.zeros((channels, lanes), jnp.float32)
        imag = real
        for channel in range(channels):
            store, row = stores[owner], channel
            if owner >= count - 2:
                store, row = stores[owner + channel // half * 2], channel % half
            block = store[pl.ds(row * channels, channels)]
            real = real + block * values[channel : channel + 1]
            imag = imag + block * swapped[channel : channel + 1]
        other_re, other_im = swap_halves(real), swap_halves(imag)
        first = lanes_of(real.shape) < lanes // 2
        mixed.append(jnp.where(first, real + other_re, other_im - imag))
    slots_to_modes(mixed, chosen_ref, out_ref, modes_x)


def adjoint(slots, pieces, stores, modes_x):
    count, blocks = len(stores) - 2, len(pieces)
    lanes = stores[0].shape[1]
    channels = 2 * pieces[0].shape[0] * modes_x // slots.shape[0]
    return pl.pallas_call(
        functools.partial(adjoint_kernel, modes_x=modes_x, blocks=blocks, count=count),
        out_shape=[jax.ShapeDtypeStruct((count // 2, channels, lanes), jnp.float32)] * 2
        + [jax.ShapeDtypeStruct(pieces[0].shape, jnp.float32)],
        in_specs=whole(1 + blocks + len(stores)),
        out_specs=whole(3),
        scratch_shapes=[
            pltpu.VMEM((2 * slots.shape[0], count * lanes), jnp.bfloat16),
            pltpu.VMEM(pieces[0].shape, jnp.float32),
        ],
        compiler_params=params(),
        cost_estimate=takes(3),
        name="adjoint",
    )(slots, *pieces, *stores)


def pair_kernel(same_ref, other_ref, *outs):
    for index, out in enumerate(outs):
        out[0] = same_ref[index]
        out[1] = other_ref[index]


def pair(same, other):
    return pl.pallas_call(
        pair_kernel,
        out_shape=[jax.ShapeDtypeStruct((2,) + same.shape[1:], same.dtype)] * same.shape[0],
        in_specs=whole(2),
        out_specs=whole(same.shape[0]),
        compiler_params=params(),
        cost_estimate=takes(0.3),
        name="pair",
    )(same, other)


def halves_kernel(first_ref, second_ref, low_ref, high_ref):
    half = low_ref.shape[0]
    low_ref[...] = first_ref[pl.ds(0, half)]
    high_ref[...] = second_ref[pl.ds(half, half)]


def halves(first, second):
    shape = (first.shape[0] // 2, first.shape[1])
    return pl.pallas_call(
        halves_kernel,
        out_shape=[jax.ShapeDtypeStruct(shape, first.dtype)] * 2,
        in_specs=whole(2),
        out_specs=whole(2),
        compiler_params=params(),
        cost_estimate=takes(0.3),
        name="halves",
    )(first, second)


def spread(small, rows, axis, channel_of):
    count = small.shape[0]
    shape = (count * rows, count)
    take = (rows_of(shape) // rows == lanes_of(shape)).astype(jnp.bfloat16)
    shape = (count, count * rows)
    put = (channel_of(lanes_of(shape) // rows) == rows_of(shape)).astype(jnp.bfloat16)
    picked = dot(take, small) if axis else dot_rows(take, small)
    full = dot(picked.astype(jnp.bfloat16), put)
    shape = full.shape
    return jnp.where(rows_of(shape) % rows == lanes_of(shape) % rows, full, 0.0)


def pointwise_kernel(full_ref, shift_ref, in_ref, out_ref):
    channels, rows_x, width = in_ref.shape
    rows = full_ref.shape[0] // channels
    shift = jnp.concatenate([shift_ref[...]] * (width // shift_ref.shape[1]), 1)

    def step(index, carry):
        values = in_ref[:, pl.ds(index * 2 * rows, 2 * rows), :].astype(jnp.float32)
        for half in range(2):
            block = values[:, half * rows : (half + 1) * rows].reshape(channels * rows, width)
            out = dot(full_ref[...], block.astype(jnp.bfloat16)) * DENSITY + shift
            out_ref[:, pl.ds(index * 2 * rows + half * rows, rows), :] = out.reshape(channels, rows, width)
        return carry

    lax.fori_loop(0, rows_x // (2 * rows), step, 0)


def pointwise_map(full, shift, values):
    return pl.pallas_call(
        pointwise_kernel,
        out_shape=jax.ShapeDtypeStruct(values.shape, jnp.float32),
        in_specs=whole(3),
        out_specs=whole(1)[0],
        compiler_params=params(),
        cost_estimate=takes(3),
        name="pointwise_map",
    )(full, shift, values)


def pointwise_back_kernel(full_ref, *refs):
    *terms, out_ref = refs
    channels, rows_x, width = out_ref.shape
    rows = full_ref.shape[0] // channels

    def step(index, carry):
        at = pl.ds(pl.multiple_of(index * 2 * rows, 2 * rows), 2 * rows)
        total = [0.0, 0.0]
        for term in range(2):
            values = [each[:, :, at, :].reshape(channels // 2, 2 * rows, width) for each in terms[term::2]]
            values = jnp.concatenate(values, 0).astype(jnp.float32)
            for half in range(2):
                block = values[:, half * rows : (half + 1) * rows].reshape(channels * rows, width)
                total[half] = total[half] + dot(full_ref[...], block.astype(jnp.bfloat16))
        for half in range(2):
            rows_at = pl.ds(index * 2 * rows + half * rows, rows)
            out_ref[:, rows_at, :] = total[half].reshape(channels, rows, width)
        return carry

    lax.fori_loop(0, rows_x // (2 * rows), step, 0)


def pointwise_back(full, terms):
    pairs, halves, rows_x, width = terms[0].shape
    return pl.pallas_call(
        pointwise_back_kernel,
        out_shape=jax.ShapeDtypeStruct((2 * pairs * halves, rows_x, width), jnp.float32),
        in_specs=whole(1 + len(terms)),
        out_specs=whole(1)[0],
        compiler_params=params(),
        cost_estimate=takes(4),
        name="pointwise_back",
    )(full, *terms)


def invert_x(pieces, xi_ref, st_ref):
    high, low = split(jnp.concatenate([piece[...] for piece in pieces], 0))
    deep = high.shape[1]
    left = jnp.concatenate([high, low], 1)
    found = dot(left, xi_ref[pl.ds(0, 2 * deep)]) + dot(high, xi_ref[pl.ds(2 * deep, deep)])
    st_ref[...] = found.reshape(st_ref.shape)


def spectral_part(index, half, st_ref, table):
    blocks, _, local_y, wide = st_ref.shape
    rows_x = wide // 4
    here = st_ref[:, index, :, pl.ds(half * 2 * rows_x, 2 * rows_x)].reshape(blocks * local_y, 2 * rows_x)
    parts = [here[:, :rows_x], here[:, rows_x:]]
    tall = jnp.transpose(jnp.concatenate(parts + parts, 0))
    high = tall.astype(jnp.bfloat16)
    first = lanes_of(tall.shape) < tall.shape[1] // 2
    mixed = jnp.where(first, tall, tall - high.astype(jnp.float32)).astype(jnp.bfloat16)
    return dot(jnp.concatenate([mixed, high], 1), table)


def slope_kernel(*refs, blocks):
    pieces, (xi_ref, ti_ref, tf_ref, xf_ref, mapped_ref, cot_ref) = refs[:blocks], refs[blocks : blocks + 6]
    terms, sums = refs[blocks + 6 : blocks + 10], refs[blocks + 10 : 2 * blocks + 10]
    st_ref, yt_ref, *before = refs[2 * blocks + 10 :]
    channels, rows_x, _ = mapped_ref.shape
    half_channels = channels // 2
    deep = tf_ref.shape[0] // 2
    modes_y = deep // 2
    local_y = modes_y // blocks
    invert_x(pieces, xi_ref, st_ref)

    def invert(index, parity):
        for half in range(2):
            channel = half * half_channels + index
            before[parity][half] = mapped_ref[channel] + spectral_part(index, half, st_ref, ti_ref[0])

    def slope(index, parity):
        for half in range(2):
            channel = half * half_channels + index
            grad = cot_ref[channel].astype(jnp.float32) * twice_gelu_slope(before[parity][half])
            high, low = split(grad)
            terms[2 * parity][index // 2, half] = high
            terms[2 * parity + 1][index // 2, half] = low

    def forward(index, parity):
        for half in range(2):
            high, low = terms[2 * parity][index // 2, half], terms[2 * parity + 1][index // 2, half]
            both = dot_rows(tf_ref[...], high)
            found = both[:deep] + both[deep:] + dot_rows(tf_ref[pl.ds(0, deep)], low)
            for block in range(blocks):
                for part in range(2):
                    at = part * modes_y + block * local_y
                    columns = pl.ds((2 * half + part) * rows_x, rows_x)
                    yt_ref[block, index, :, columns] = found[at : at + local_y]

    def step(pair, carry):
        index = 2 * pair
        forward(jnp.maximum(index - 1, 1), 1)
        invert(index + 1, 1)
        slope(index, 0)
        forward(index, 0)
        invert(jnp.minimum(index + 2, half_channels - 2), 0)
        slope(index + 1, 1)
        return carry

    invert(0, 0)
    lax.fori_loop(0, half_channels // 2, step, 0, unroll=2)
    forward(half_channels - 1, 1)
    high, low = split(yt_ref[...].reshape(-1, yt_ref.shape[-1]))
    lanes = xf_ref.shape[1] // 2
    both = dot(high, xf_ref[...])
    total = both[:, :lanes] + both[:, lanes:] + dot(low, xf_ref[:, :lanes])
    rows = total.shape[0] // blocks
    for block in range(blocks):
        sums[block][...] = total[block * rows : (block + 1) * rows]


def slope_step(pieces, tables, mapped, cotangent):
    ti, tf, xi, xf = tables
    blocks = len(pieces)
    channels, rows_x, width = mapped.shape
    half = channels // 2
    local_y = pieces[0].shape[0] // half
    results = pl.pallas_call(
        functools.partial(slope_kernel, blocks=blocks),
        out_shape=[jax.ShapeDtypeStruct((half // 2, 2, rows_x, width), jnp.bfloat16)] * 4
        + [jax.ShapeDtypeStruct(pieces[0].shape, jnp.float32)] * blocks,
        in_specs=whole(blocks + 6),
        out_specs=whole(4 + blocks),
        scratch_shapes=[pltpu.VMEM((blocks, half, local_y, 4 * rows_x), jnp.float32)] * 2
        + [pltpu.VMEM((2, rows_x, width), jnp.float32)] * 2,
        compiler_params=params(),
        cost_estimate=takes(13),
        name="slope_step",
    )(*pieces, xi, ti, tf, xf, mapped, cotangent)
    return results[:4], results[4:]


def finish_kernel(*refs, blocks, group):
    pieces, (xi_ref, ti_ref, part_ref, out_ref, st_ref, sum_ref, sems) = refs[:blocks], refs[blocks:]
    channels = part_ref.shape[0]
    invert_x(pieces, xi_ref, st_ref)

    def copies(index):
        for half in range(2):
            rows = pl.ds(half * (channels // 2) + index * group, group)
            yield pltpu.make_async_copy(sum_ref.at[rows], out_ref.at[rows], sems.at[half, index])

    def step(index, carry):
        for half in range(2):
            for member in range(group):
                place = index * group + member
                channel = half * (channels // 2) + place
                sum_ref[channel] = part_ref[channel] + spectral_part(place, half, st_ref, ti_ref[1])
        for copy in copies(index):
            copy.start()
        return carry

    def settle(index, carry):
        for copy in copies(index):
            copy.wait()
        return carry

    steps = channels // (2 * group)
    lax.fori_loop(0, steps, step, 0)
    lax.fori_loop(0, steps, settle, 0)


def finish(pieces, tables, part, group=2):
    ti, _, xi, _ = tables
    blocks = len(pieces)
    channels, rows_x, _ = part.shape
    half = channels // 2
    local_y = pieces[0].shape[0] // half
    return pl.pallas_call(
        functools.partial(finish_kernel, blocks=blocks, group=group),
        out_shape=jax.ShapeDtypeStruct(part.shape, jnp.float32),
        in_specs=whole(blocks + 3),
        out_specs=outside(1)[0],
        scratch_shapes=[
            pltpu.VMEM((blocks, half, local_y, 4 * rows_x), jnp.float32),
            pltpu.VMEM(part.shape, jnp.float32),
            pltpu.SemaphoreType.DMA((2, half // group)),
        ],
        compiler_params=params(20),
        cost_estimate=takes(4),
        name="finish",
    )(*pieces, xi, ti, part)


def exchange(piece, axis, count, flip):
    return lax.ppermute(piece, axis, [(i, i ^ flip) for i in range(count)])


def to_owners(same, other, count):
    pairs = list(pair(same, exchange(other, "py", count, 1)))
    return pairs[:1] + [exchange(pairs[i], "py", count, 2 * i) for i in range(1, len(pairs))]


def between_chips(piece, count):
    return [piece] + [exchange(piece, "py", count, step) for step in range(2, count, 2)]


def between_cores(pieces, count, beside):
    other = [beside] + [exchange(piece, "py", count, 1) for piece in pieces[1:]]
    return [each for pair in zip(pieces, other) for each in pair]


def from_all(piece, axis, count):
    return [piece] + [exchange(piece, axis, count, step) for step in range(count - 1, 0, -1)][::-1]


def to_all(pieces, axis, count):
    return pieces[:1] + [exchange(pieces[step], axis, count, step) for step in range(count - 1, 0, -1)][::-1]


def on_device_packed(
    field_in,
    cotangent,
    spectrum_saved,
    weight_store,
    block_slot,
    kx_modes,
    ky_modes,
    pointwise,
    bias_vector,
):
    channels, _, rows_x, width_y = field_in.shape
    count_x, count_y = lax.axis_size("px"), lax.axis_size("py")
    full_x = rows_x * count_x
    planes, local_y, local_x = spectrum_saved.shape[1:4]
    modes_x = kx_modes.shape[0]
    lanes = 2 * weight_store.shape[0]
    store = jnp.transpose(weight_store, (1, 2, 3, 0))
    barrier = lax.optimization_barrier
    spectrum = jnp.transpose(spectrum_saved, (1, 2, 3, 4, 0)).reshape(-1, channels)
    piece, small = pack(block_slot, spectrum, ky_modes, kx_modes, bias_vector, pointwise, lanes)
    pieces = between_chips(piece, count_y)
    beside = exchange(piece, "py", count_y, 1)
    tables, packed, full_map, full_back, shift, piece = prepare(
        small, store, piece, full_x, rows_x, width_y, ky_modes.shape[0], modes_x
    )
    pieces, beside, tables, full_map, piece = barrier((pieces, beside, tables, full_map, piece))
    pieces = between_cores([piece] + pieces[1:], count_y, beside)
    kept, slots, *mixed = mix(packed, pieces, planes, local_x)
    pairs = to_owners(*mixed, count_y)
    pairs, packed, beside = barrier((pairs, packed, exchange(packed, "py", count_y, 1)))
    across = [exchange(packed, "py", count_y, step) for step in (2, 4)]
    received = from_all(to_modes(slots, pairs, modes_x), "px", count_x)
    mapped = pointwise_map(full_map, shift, field_in[:, 0])
    received, mapped, across = barrier((received, mapped, across))
    low, high = halves(*across)
    far = [exchange(low, "py", count_y, 4), exchange(high, "py", count_y, 2)]
    other = [exchange(each, "py", count_y, 1) for each in across]
    terms, sums = slope_step(received, tables, mapped, cotangent[:, 0])
    sums, terms, far, other = barrier((list(sums), list(terms), far, other))
    received = to_all(sums, "px", count_x)
    back = pointwise_back(full_back, terms)
    stores = [packed, beside, across[0], other[0], across[1], other[1]]
    low, high = far
    stores += [low, exchange(low, "py", count_y, 1), high, exchange(high, "py", count_y, 1)]
    received, back, stores = barrier((received, back, stores))
    same, other, mixed = adjoint(slots, received, stores, modes_x)
    received = from_all(mixed, "px", count_x)
    pairs = to_owners(same, other, count_y)
    field_grad = finish(received, tables, back)
    blocks = weight_grad(kept, pairs)
    return (field_grad[:, None], jnp.transpose(blocks, (3, 0, 1, 2)))


def packs(mesh, channels, planes, rows, width, modes, capacity):
    count_x, count_y = mesh.shape["px"], mesh.shape["py"]
    powers = all(size & (size - 1) == 0 for size in (rows, width))
    return (
        powers
        and (count_x, count_y, planes) == (4, 8, 8)
        and channels == 32
        and 4 * modes == 128
        and 2 * capacity == 128
        and rows // count_x == 128
        and width % 256 == 0
        and modes // count_x == 8
    )


def solution(mesh):
    placed = (
        P(None, "py", "px", None),
        P(None, "py", "px", None),
        P(None, None, "px", "py", None),
        P(("px", "py"), None, None, None),
        P("py", "px"),
        P(),
        P(),
        P(),
        P(),
    )

    def run(*args):
        channels, planes, rows, width = args[0].shape
        capacity = args[3].shape[0] // mesh.size
        packed = packs(mesh, channels, planes, rows, width, args[5].shape[0], capacity)
        return jax.shard_map(
            on_device_packed if packed else on_device,
            mesh=mesh,
            in_specs=placed,
            out_specs=(P(None, "py", "px", None), P(("px", "py"), None, None, None)),
            check_vma=False,
        )(*args)

    return run
```

```python
import functools
import math

import jax
import jax.numpy as jnp
from jax import lax
from jax.experimental import pallas as pl
from jax.experimental.pallas import tpu as pltpu
from jax.sharding import PartitionSpec as P

precise = lax.Precision.HIGHEST


def phase_table(length, modes):
    points = lax.iota(jnp.int32, length)
    wrapped = points[:, None] * modes[None, :] % length
    angle = wrapped.astype(jnp.float32) * (2.0 * math.pi / length)
    return (jnp.cos(angle), jnp.sin(angle))


def gelu_slope(values):
    normal_cdf = 0.5 * (1.0 + lax.erf(values * 0.7071067811865476))
    density = jnp.exp(-0.5 * values * values) * 0.3989422804014327
    return normal_cdf + values * density


def channel_mix(blocks, spectrum):
    block_re = blocks[:, :, 0]
    block_im = blocks[:, :, 1]
    spec_re = spectrum[..., 0]
    spec_im = spectrum[..., 1]
    form = "baoc,czba->ozba"
    out_re = jnp.einsum(form, block_re, spec_re, precision=precise) - jnp.einsum(
        form, block_im, spec_im, precision=precise
    )
    out_im = jnp.einsum(form, block_re, spec_im, precision=precise) + jnp.einsum(
        form, block_im, spec_re, precision=precise
    )
    return jnp.stack([out_re, out_im], -1)


def channel_adjoint(blocks, spectrum):
    block_re = blocks[:, :, 0]
    block_im = blocks[:, :, 1]
    grad_re = spectrum[..., 0]
    grad_im = spectrum[..., 1]
    form = "baoc,ozba->czba"
    out_re = jnp.einsum(form, block_re, grad_re, precision=precise) + jnp.einsum(
        form, block_im, grad_im, precision=precise
    )
    out_im = jnp.einsum(form, block_re, grad_im, precision=precise) - jnp.einsum(
        form, block_im, grad_re, precision=precise
    )
    return jnp.stack([out_re, out_im], -1)


def block_gradient(spectrum_grad, spectrum):
    grad_re = spectrum_grad[..., 0]
    grad_im = spectrum_grad[..., 1]
    spec_re = spectrum[..., 0]
    spec_im = spectrum[..., 1]
    form = "ozba,czba->aboc"
    out_re = jnp.einsum(form, grad_re, spec_re, precision=precise) + jnp.einsum(
        form, grad_im, spec_im, precision=precise
    )
    out_im = jnp.einsum(form, grad_im, spec_re, precision=precise) - jnp.einsum(
        form, grad_re, spec_im, precision=precise
    )
    return jnp.stack([out_re, out_im], 2)


def invert_rows(spectrum, cos_rows, sin_rows):
    spec_re = spectrum[..., 0]
    spec_im = spectrum[..., 1]
    form = "czma,xa->czmx"
    back_re = jnp.einsum(form, spec_re, cos_rows, precision=precise) - jnp.einsum(
        form, spec_im, sin_rows, precision=precise
    )
    back_im = jnp.einsum(form, spec_re, sin_rows, precision=precise) + jnp.einsum(
        form, spec_im, cos_rows, precision=precise
    )
    joined = jnp.stack([back_re, back_im], 3)
    return joined.reshape(joined.shape[0], joined.shape[1], 2 * joined.shape[2], joined.shape[4])


def on_device(
    field_in,
    cotangent,
    spectrum_saved,
    weight_store,
    block_slot,
    kx_modes,
    ky_modes,
    pointwise,
    bias_vector,
):
    channels, planes, rows_x, width_y = field_in.shape
    full_x = rows_x * lax.axis_size("px")
    modes_y = ky_modes.shape[0]
    local_y = modes_y // lax.axis_size("px")
    capacity = weight_store.shape[0]
    factor = 1.0 / math.sqrt(full_x * width_y)
    cos_y, sin_y = phase_table(width_y, ky_modes)
    table_y = jnp.stack([cos_y, -sin_y], 2).reshape(width_y, 2 * modes_y)
    cos_x, sin_x = phase_table(full_x, kx_modes)
    store_row, slots_row = (
        lax.all_gather(weight_store, "py", axis=0, tiled=True),
        lax.all_gather(block_slot, "py", axis=0, tiled=True),
    )
    slots_flat = slots_row.reshape(-1)

    def inverse_planes(spectrum):
        joined = invert_rows(spectrum, cos_x, sin_x)
        returned = lax.all_to_all(joined, "px", split_axis=3, concat_axis=2, tiled=True)
        return factor * jnp.einsum("czkx,yk->czxy", returned, table_y, precision=precise)

    weight_full = pointwise.astype(jnp.float32)
    local_x = block_slot.shape[0]
    indices = jnp.transpose(block_slot).reshape(-1)
    blocks = jnp.take(store_row, indices, axis=0).reshape(local_y, local_x, 2, channels, channels)
    mixed = channel_mix(blocks, spectrum_saved)

    def from_modes(spectrum):
        return lax.all_to_all(spectrum, "py", split_axis=1, concat_axis=3, tiled=True)

    spectral = inverse_planes(from_modes(mixed))
    mapped = jnp.einsum("oc,czxy->ozxy", pointwise, field_in, preferred_element_type=jnp.float32)
    grad = cotangent.astype(jnp.float32) * gelu_slope(
        mapped + bias_vector.reshape(channels, 1, 1, 1) + spectral
    )
    partial_value = jnp.einsum("czxy,yk->czkx", grad, table_y, precision=precise)
    moved = lax.all_to_all(partial_value, "px", split_axis=2, concat_axis=3, tiled=True)
    pieces = moved.reshape(channels, planes, local_y, 2, full_x)
    part_re = pieces[:, :, :, 0]
    part_im = pieces[:, :, :, 1]
    form = "czmx,xk->czmk"
    real_part = jnp.einsum(form, part_re, cos_x, precision=precise) + jnp.einsum(
        form, part_im, sin_x, precision=precise
    )
    imag_part = jnp.einsum(form, part_im, cos_x, precision=precise) - jnp.einsum(
        form, part_re, sin_x, precision=precise
    )
    spectrum_grad = lax.all_to_all(
        factor * jnp.stack([real_part, imag_part], -1),
        "py",
        split_axis=3,
        concat_axis=1,
        tiled=True,
    )
    input_spectrum = channel_adjoint(blocks, spectrum_grad)
    local_grad = block_gradient(spectrum_grad, spectrum_saved)
    field_grad = jnp.einsum("oc,ozxy->czxy", weight_full, grad, precision=precise) + inverse_planes(
        from_modes(input_spectrum)
    )
    grads_all = lax.all_gather(local_grad, "py", axis=0, tiled=True)
    grads_flat = grads_all.reshape(slots_flat.shape[0], 2 * channels * channels)
    targets = lax.axis_index("py") * capacity + lax.iota(jnp.int32, capacity)
    select = (targets[:, None] == slots_flat[None, :]).astype(jnp.float32)
    store_flat = jnp.dot(select, grads_flat, precision=precise)
    store_grad = store_flat.reshape(capacity, 2, channels, channels)
    return (field_grad, store_grad)


def place_of():
    return lax.axis_index("px"), lax.axis_index("py")


def split(values):
    high = values.astype(jnp.bfloat16)
    return high, (values - high.astype(jnp.float32)).astype(jnp.bfloat16)


def dot(left, right):
    return jnp.dot(left, right, preferred_element_type=jnp.float32)


def dot_rows(left, right):
    return lax.dot_general(left, right, (((1,), (1,)), ((), ())), preferred_element_type=jnp.float32)


def lanes_of(shape):
    return lax.broadcasted_iota(jnp.int32, shape, len(shape) - 1)


def rows_of(shape):
    return lax.broadcasted_iota(jnp.int32, shape, len(shape) - 2)


def whole(count):
    return [pl.BlockSpec(memory_space=pltpu.VMEM)] * count


def params(mebibytes=12):
    return pltpu.CompilerParams(vmem_limit_bytes=mebibytes * 1024 * 1024)


def takes(microseconds):
    return pl.CostEstimate(flops=int(microseconds * 10**9), bytes_accessed=2**20, transcendentals=0)


def outside(count):
    return [pl.BlockSpec(memory_space=pltpu.HBM)] * count


def scalars(count):
    return [pl.BlockSpec(memory_space=pltpu.SMEM)] * count


DENSITY = math.sqrt(2.0 / math.pi)


def twice_gelu_slope(scaled):
    normal = 1.0 + lax.erf(scaled * (math.sqrt(0.5) / DENSITY))
    return normal + scaled * jnp.exp2(scaled * scaled * (-0.5 * math.log2(math.e) / DENSITY**2))


def column_of(ref, start, count):
    shape = (count, 128)
    row = rows_of(shape)
    out = jnp.zeros(shape, ref.dtype)
    for i in range(count):
        out = jnp.where(row == i, ref[start(i)], out)
    return out


def unpack_kernel(all_ref, store_ref, kept_ref, small_ref, packed_ref):
    wide, channels = kept_ref.shape[1], store_ref.shape[1]
    kept_ref[...] = all_ref[:, :wide]
    small_ref[...] = all_ref[:, wide:]
    for channel in range(channels):
        packed = jnp.concatenate([store_ref[0, channel], store_ref[1, channel]], 1)
        packed_ref[pl.ds(channel * channels, channels)] = packed


def unpack(everything, store, wide):
    rows, full = everything.shape
    channels, capacity = store.shape[2:]
    shapes = (rows, wide), (rows, full - wide), (channels * channels, 2 * capacity)
    return pl.pallas_call(
        unpack_kernel,
        out_shape=[jax.ShapeDtypeStruct(shape, jnp.float32) for shape in shapes],
        in_specs=whole(2),
        out_specs=whole(3),
        compiler_params=params(),
        cost_estimate=takes(0.5),
        name="unpack",
    )(everything, store)


def tables_kernel(small_ref, ti_ref, tf_ref, xi_ref, xf_ref, map_ref, back_ref, shift_ref, *, full_x):
    lanes, width = shift_ref.shape[1], tf_ref.shape[1]
    channels = small_ref.shape[0]
    rows = map_ref.shape[0] // channels
    ky, kx, bias, weight = (small_ref[:, pl.ds(i * lanes, lanes)] for i in range(4))
    ky, kx, bias = ky.astype(jnp.int32), kx.astype(jnp.int32), bias * DENSITY
    weight = weight[:, :channels].astype(jnp.bfloat16)
    map_ref[...] = spread(weight, rows, 1, lambda i: i).astype(jnp.bfloat16)
    pairs = channels // 4
    back = spread(weight, rows, 0, lambda i: i % 2 * 2 * pairs + i // 2 % pairs * 2 + i // (2 * pairs))
    back_ref[...] = (0.5 * back).astype(jnp.bfloat16)
    for channel in range(channels):
        shift_ref[pl.ds(channel * rows, rows)] = jnp.broadcast_to(bias[channel : channel + 1], (rows, bias.shape[1]))
    modes_x, rows_x = kx.shape[0], xf_ref.shape[0] // 4
    factor = 1.0 / math.sqrt(full_x * width)
    start = place_of()[0] * rows_x

    def angles(modes, points, length):
        return ((modes * points) & (length - 1)).astype(jnp.float32) * (2.0 * math.pi / length)

    ky = jnp.concatenate([ky] * (width // ky.shape[1]), 1)
    angle = angles(ky, lanes_of(ky.shape), width)
    waves = jnp.concatenate([jnp.cos(angle), -jnp.sin(angle)], 0)
    high, low = split(waves)
    tf_ref[...] = jnp.concatenate([high, low], 0)
    for index, scale in enumerate((DENSITY, 1.0)):
        high, low = split(scale * waves)
        ti_ref[index] = jnp.concatenate([high, high, low, jnp.zeros_like(low)], 0)
    angle = angles(kx, start + lanes_of((modes_x, rows_x)), full_x)
    cos, sin, zero = factor * jnp.cos(angle), factor * jnp.sin(angle), jnp.zeros_like(angle)
    parts = [[cos, sin, zero, zero], [-sin, cos, zero, zero], [zero, zero, cos, sin], [zero, zero, -sin, cos]]
    high, low = split(jnp.concatenate([jnp.concatenate(part, 1) for part in parts], 0))
    xi_ref[...] = jnp.concatenate([high, high, low], 0)
    cos = 0.5 * jnp.transpose(jnp.concatenate([cos] * 4, 0))
    sin = 0.5 * jnp.transpose(jnp.concatenate([sin] * 4, 0))
    zero = jnp.zeros_like(cos)
    lane = lanes_of(cos.shape)
    real = (lane // modes_x) % 2 == 0
    first = lane < 2 * modes_x
    from_re, from_im = jnp.where(real, cos, -sin), jnp.where(real, sin, cos)
    parts = [
        jnp.where(first, from_re, zero),
        jnp.where(first, from_im, zero),
        jnp.where(first, zero, from_re),
        jnp.where(first, zero, from_im),
    ]
    high, low = split(jnp.concatenate(parts, 0))
    xf_ref[...] = jnp.concatenate([high, low], 1)


def make_tables(small, full_x, rows_x, width, modes_y, modes_x, rows=8):
    channels, lanes = small.shape[0], small.shape[1] // 4
    shapes = (
        (2, 4 * 2 * modes_y, width),
        (2 * 2 * modes_y, width),
        (3 * 4 * modes_x, 4 * rows_x),
        (4 * rows_x, 8 * modes_x),
        (channels * rows, channels * rows),
        (channels * rows, channels * rows),
        (channels * rows, lanes),
    )
    types = [jnp.float32 if i == 6 else jnp.bfloat16 for i in range(len(shapes))]
    *tables, full_map, full_back, shift = pl.pallas_call(
        functools.partial(tables_kernel, full_x=full_x),
        out_shape=[jax.ShapeDtypeStruct(*each) for each in zip(shapes, types)],
        in_specs=whole(1),
        out_specs=whole(len(shapes)),
        compiler_params=params(),
        cost_estimate=takes(1),
        name="tables",
    )(small)
    return tables, full_map, full_back, shift


def duplicate(values):
    return jnp.concatenate([values, values], -1)


def pack_kernel(*refs):
    sources, (out_ref, all_ref), (*targets, sems) = refs[:6], refs[6:8], refs[8:]
    copies = [pltpu.make_async_copy(*pair, sems.at[i]) for i, pair in enumerate(zip(sources, targets))]
    for copy in copies:
        copy.start()
    for copy in copies:
        copy.wait()
    slots_ref, spec_ref, ky_ref, kx_ref, bias_ref, weight_ref = targets
    place_x, place_y = place_of()
    local_x, local_y = slots_ref.shape
    modes = local_x * local_y
    groups = spec_ref.shape[0] // modes
    columns = []
    for group in range(groups // 2):
        for part in range(2):
            columns.append(spec_ref[pl.ds(group * 2 * modes + part, modes, stride=2)])
    lanes = out_ref.shape[1] - groups * spec_ref.shape[1]
    numbers = column_of(slots_ref, lambda i: (i % local_x, i // local_x), modes)
    piece = jnp.concatenate(columns + [numbers.astype(jnp.float32)], 1)
    out_ref[...] = piece
    modes_y, modes_x, channels = ky_ref.shape[0], kx_ref.shape[0], bias_ref.shape[0]
    ky = column_of(ky_ref, lambda i: (place_x ^ (i // local_y)) * local_y + i % local_y, modes_y)
    kx = column_of(kx_ref, lambda i: (place_y ^ (i // local_x)) * local_x + i % local_x, modes_x)
    bias = column_of(bias_ref, lambda i: i, channels)
    weight = weight_ref[...].astype(jnp.float32)
    weight = jnp.concatenate([weight, jnp.zeros((channels, lanes - channels), jnp.float32)], 1)
    all_ref[...] = jnp.concatenate([piece, ky.astype(jnp.float32), kx.astype(jnp.float32), bias, weight], 1)


def pack(slots, spectrum, ky, kx, bias, weight, lanes):
    modes = slots.size
    width = spectrum.size // modes + lanes
    sources = (slots, spectrum, ky, kx, bias, weight)
    held = (pltpu.SMEM, pltpu.VMEM, pltpu.SMEM, pltpu.SMEM, pltpu.SMEM, pltpu.VMEM)
    return pl.pallas_call(
        pack_kernel,
        out_shape=[
            jax.ShapeDtypeStruct((modes, width), jnp.float32),
            jax.ShapeDtypeStruct((modes, width + 4 * lanes), jnp.float32),
        ],
        in_specs=outside(6),
        out_specs=whole(2),
        scratch_shapes=[space(each.shape, each.dtype) for space, each in zip(held, sources)]
        + [pltpu.SemaphoreType.DMA((6,))],
        compiler_params=params(60),
        name="pack",
    )(*sources)


def mix_kernel(packed_ref, *refs, count, local_x):
    pieces, refs = refs[:count], refs[count:]
    kept_ref, slots_ref, same_ref, other_ref, out_ref, uc_ref, ud_ref = refs
    planes, channels, lanes = out_ref.shape
    place = place_of()[1]
    capacity = lanes // 2
    wide = pieces[0].shape[1] - lanes
    local_y = pieces[0].shape[0] // local_x
    for index, piece in enumerate(pieces):
        for mode in range(local_y):
            rows = pl.ds((mode * count + index) * local_x, local_x)
            slots_ref[rows] = piece[pl.ds(mode * local_x, local_x), pl.ds(wide, lanes)]
    numbers = jnp.transpose(jnp.concatenate([piece[:, pl.ds(wide, lanes)] for piece in pieces], 0))
    wanted = (place * capacity + rows_of(numbers.shape) % capacity).astype(jnp.float32)
    chosen = (numbers == wanted).astype(jnp.bfloat16)
    high, low = split(jnp.concatenate([piece[:, pl.ds(0, wide)] for piece in pieces], 0))
    placed = jnp.transpose(dot(chosen, high) + dot(chosen, low))
    kept_ref[...] = placed
    parts = placed.reshape(planes, 2, channels, lanes)
    first = lanes_of((channels, lanes)) < capacity
    for plane in range(planes):
        rows = pl.ds(plane * channels, channels)
        uc_ref[rows] = jnp.where(first, parts[plane, 0], parts[plane, 1])
        ud_ref[rows] = jnp.where(first, parts[plane, 1], parts[plane, 0])
    def step(channel, carry):
        block = packed_ref[pl.ds(pl.multiple_of(channel * channels, channels), channels)]
        swapped = swap_halves(block)
        ra = jnp.where(first, block, swapped)
        rb = jnp.where(first, -swapped, block)
        for plane in range(planes):
            rows = pl.ds(plane * channels, channels)
            product = ra * uc_ref[rows] + rb * ud_ref[rows]
            out_ref[plane, pl.ds(channel, 1)] = jnp.sum(product, 0, keepdims=True)
        return carry

    lax.fori_loop(0, channels, step, 0, unroll=4)
    for step in range(planes):
        (other_ref if step % 2 else same_ref)[step // 2] = out_ref[place ^ step]


def mix(packed, pieces, planes, local_x):
    channels, lanes = math.isqrt(packed.shape[0]), packed.shape[1]
    count = len(pieces)
    return pl.pallas_call(
        functools.partial(mix_kernel, count=count, local_x=local_x),
        out_shape=[
            jax.ShapeDtypeStruct((2 * planes * channels, lanes), jnp.float32),
            jax.ShapeDtypeStruct((count * pieces[0].shape[0], lanes), jnp.float32),
            jax.ShapeDtypeStruct((planes // 2, channels, lanes), jnp.float32),
            jax.ShapeDtypeStruct((planes // 2, channels, lanes), jnp.float32),
        ],
        in_specs=whole(1 + count),
        out_specs=whole(4),
        scratch_shapes=[pltpu.VMEM((planes, channels, lanes), jnp.float32)]
        + [pltpu.VMEM((planes * channels, lanes), jnp.float32)] * 2,
        compiler_params=params(),
        cost_estimate=takes(3),
        name="mix",
    )(packed, *pieces)


def swap_halves(values):
    half = values.shape[-1] // 2
    return jnp.concatenate([values[..., half:], values[..., :half]], -1)


def weight_grad_kernel(kept_ref, *refs):
    *pairs, out_ref, gs_ref, sum_ref, sems = refs
    grads = [each.at[core] for each in pairs for core in range(2)]
    channels, lanes = grads[0].shape
    capacity = lanes // 2
    starts = []
    for index, grad in enumerate(grads):
        swapped = swap_halves(grad[...])
        gs_ref[index] = jnp.where(lanes_of(swapped.shape) < capacity, swapped, -swapped)
        starts.append((place_of()[1] ^ index) * 2 * channels)
    chunks = sems.shape[0]
    size = channels // chunks

    def send(chunk):
        rows = pl.ds(chunk * size, size)
        return pltpu.make_async_copy(sum_ref.at[:, rows], out_ref.at[:, rows], sems.at[chunk])

    def step(pair, carry):
        totals = [jnp.zeros((channels, lanes), jnp.float32)] * 2
        for index, start in enumerate(starts):
            real = kept_ref[pl.ds(start, channels)]
            imag = kept_ref[pl.ds(start + channels, channels)]
            for each in range(2):
                row = pl.ds(2 * pair + each, 1)
                totals[each] = totals[each] + real * grads[index][row] + imag * gs_ref[index, row]
        for each, total in enumerate(totals):
            sum_ref[0, 2 * pair + each] = total[:, :capacity]
            sum_ref[1, 2 * pair + each] = total[:, capacity:]
        return carry

    for chunk in range(chunks):
        lax.fori_loop(chunk * size // 2, (chunk + 1) * size // 2, step, 0, unroll=2)
        send(chunk).start()
    for chunk in range(chunks):
        send(chunk).wait()


def weight_grad(kept, pairs, chunks=4):
    _, channels, lanes = pairs[0].shape
    shape = (2, channels, channels, lanes // 2)
    return pl.pallas_call(
        weight_grad_kernel,
        out_shape=jax.ShapeDtypeStruct(shape, jnp.float32),
        in_specs=whole(1 + len(pairs)),
        out_specs=outside(1)[0],
        scratch_shapes=[
            pltpu.VMEM((2 * len(pairs), channels, lanes), jnp.float32),
            pltpu.VMEM(shape, jnp.float32),
            pltpu.SemaphoreType.DMA((chunks,)),
        ],
        compiler_params=params(),
        cost_estimate=takes(2),
        name="weight_grad",
    )(kept, *pairs)


def select_kernel(slots_ref, chosen_ref, *, modes_x):
    capacity = slots_ref.shape[1] // 2
    lanes = 2 * capacity
    place = place_of()[1]
    shape = (modes_x, lanes)
    lane = lanes_of(shape)
    first = lane < capacity
    zero = jnp.zeros(shape, jnp.float32)
    for mode in range(slots_ref.shape[0] // modes_x):
        numbers = slots_ref[pl.ds(mode * modes_x, modes_x)]
        for owner in range(chosen_ref.shape[1] // lanes):
            wanted = ((owner ^ place) * capacity + lane % capacity).astype(jnp.float32)
            hit = jnp.where(numbers == wanted, 1.0, 0.0)
            both = jnp.concatenate([jnp.where(first, hit, zero), jnp.where(first, zero, hit)], 0)
            chosen_ref[pl.ds(mode * 2 * modes_x, 2 * modes_x), pl.ds(owner * lanes, lanes)] = both.astype(jnp.bfloat16)


def select(slots, modes_x, count):
    return pl.pallas_call(
        functools.partial(select_kernel, modes_x=modes_x),
        out_shape=jax.ShapeDtypeStruct((2 * slots.shape[0], count * slots.shape[1]), jnp.bfloat16),
        in_specs=whole(1),
        out_specs=whole(1)[0],
        compiler_params=params(),
        cost_estimate=takes(0.5),
        name="select",
    )(slots)


def slots_to_modes(blocks, chosen_ref, out_ref, modes_x):
    channels = blocks[0].shape[0]
    half = channels // 2
    high, low = split(jnp.concatenate(blocks, 1))
    found = dot_rows(jnp.concatenate([high, low], 0), chosen_ref[...])
    found = found[:channels] + found[channels:]
    local_y = found.shape[1] // (2 * modes_x)
    for mode in range(local_y):
        piece = found[:, mode * 2 * modes_x : (mode + 1) * 2 * modes_x]
        out_ref[pl.ds(mode, half, stride=local_y)] = jnp.concatenate([piece[:half], piece[half:]], 1)


def to_modes_kernel(chosen_ref, *refs, modes_x):
    *pairs, out_ref = refs
    slots_to_modes([pair[core] for pair in pairs for core in range(2)], chosen_ref, out_ref, modes_x)


def to_modes(chosen, pairs, modes_x):
    _, channels, _ = pairs[0].shape
    local_y = chosen.shape[0] // (2 * modes_x)
    return pl.pallas_call(
        functools.partial(to_modes_kernel, modes_x=modes_x),
        out_shape=jax.ShapeDtypeStruct((channels // 2 * local_y, 4 * modes_x), jnp.float32),
        in_specs=whole(1 + len(pairs)),
        out_specs=whole(1)[0],
        compiler_params=params(),
        cost_estimate=takes(1),
        name="to_modes",
    )(chosen, *pairs)


def mix_back(store, row, values):
    channels, lanes = values.shape
    swapped = swap_halves(values)
    real = jnp.zeros((channels, lanes), jnp.float32)
    imag = real
    for channel in range(channels):
        block = store[pl.ds(row + channel * channels, channels)]
        real = real + block * values[channel : channel + 1]
        imag = imag + block * swapped[channel : channel + 1]
    other_re, other_im = swap_halves(real), swap_halves(imag)
    return jnp.where(lanes_of(real.shape) < lanes // 2, real + other_re, other_im - imag)


def adjoint_kernel(chosen_ref, *refs, modes_x, blocks):
    pieces, stores, (same_ref, other_ref, out_ref, sum_ref) = refs[:blocks], refs[blocks:-4], refs[-4:]
    steps, channels, lanes = same_ref.shape
    half = channels // 2
    sum_ref[...] = sum(piece[...] for piece in pieces)
    local_y = sum_ref.shape[0] // half
    columns = []
    for mode in range(local_y):
        piece = sum_ref[pl.ds(mode, half, stride=local_y)]
        columns.append(jnp.concatenate([piece[:, : 2 * modes_x], piece[:, 2 * modes_x :]], 0))
    high, low = split(jnp.concatenate(columns, 1))
    found = dot(jnp.concatenate([high, low], 0), chosen_ref[...])
    found = found[:channels] + found[channels:]
    mixed = []
    for owner in range(2 * steps):
        values = found[:, owner * lanes : (owner + 1) * lanes]
        (other_ref if owner % 2 else same_ref)[owner // 2] = values
        row = max(owner // 2 - 1, 0) * channels * channels
        mixed.append(mix_back(stores[owner % 2 + (2 if owner > 1 else 0)], row, values))
    slots_to_modes(mixed, chosen_ref, out_ref, modes_x)


def adjoint(chosen, pieces, stores, modes_x):
    blocks = len(pieces)
    channels, lanes = math.isqrt(stores[0].shape[0]), stores[0].shape[1]
    steps = chosen.shape[1] // (2 * lanes)
    return pl.pallas_call(
        functools.partial(adjoint_kernel, modes_x=modes_x, blocks=blocks),
        out_shape=[jax.ShapeDtypeStruct((steps, channels, lanes), jnp.float32)] * 2
        + [jax.ShapeDtypeStruct(pieces[0].shape, jnp.float32)],
        in_specs=whole(1 + blocks + len(stores)),
        out_specs=whole(3),
        scratch_shapes=[pltpu.VMEM(pieces[0].shape, jnp.float32)],
        compiler_params=params(),
        cost_estimate=takes(2),
        name="adjoint",
    )(chosen, *pieces, *stores)


def pair_kernel(same_ref, other_ref, *outs):
    for index, out in enumerate(outs):
        out[0] = same_ref[index]
        out[1] = other_ref[index]


def pair(same, other):
    return pl.pallas_call(
        pair_kernel,
        out_shape=[jax.ShapeDtypeStruct((2,) + same.shape[1:], same.dtype)] * same.shape[0],
        in_specs=whole(2),
        out_specs=whole(same.shape[0]),
        compiler_params=params(),
        cost_estimate=takes(0.3),
        name="pair",
    )(same, other)


def halves_kernel(first_ref, second_ref, low_ref, high_ref):
    half = low_ref.shape[0]
    low_ref[...] = first_ref[pl.ds(0, half)]
    high_ref[...] = second_ref[pl.ds(half, half)]


def halves(first, second):
    shape = (first.shape[0] // 2, first.shape[1])
    return pl.pallas_call(
        halves_kernel,
        out_shape=[jax.ShapeDtypeStruct(shape, first.dtype)] * 2,
        in_specs=whole(2),
        out_specs=whole(2),
        compiler_params=params(),
        cost_estimate=takes(0.1),
        name="halves",
    )(first, second)


def join_kernel(*refs):
    *parts, out_ref = refs
    start = 0
    for part in parts:
        out_ref[pl.ds(start, part.shape[0])] = part[...]
        start += part.shape[0]


def join(parts):
    rows = sum(part.shape[0] for part in parts)
    return pl.pallas_call(
        join_kernel,
        out_shape=jax.ShapeDtypeStruct((rows, parts[0].shape[1]), parts[0].dtype),
        in_specs=whole(len(parts)),
        out_specs=whole(1)[0],
        compiler_params=params(),
        cost_estimate=takes(0.1),
        name="join",
    )(*parts)


def spread(small, rows, axis, channel_of):
    count = small.shape[0]
    shape = (count * rows, count)
    take = (rows_of(shape) // rows == lanes_of(shape)).astype(jnp.bfloat16)
    shape = (count, count * rows)
    put = (channel_of(lanes_of(shape) // rows) == rows_of(shape)).astype(jnp.bfloat16)
    picked = dot(take, small) if axis else dot_rows(take, small)
    full = dot(picked.astype(jnp.bfloat16), put)
    shape = full.shape
    return jnp.where(rows_of(shape) % rows == lanes_of(shape) % rows, full, 0.0)


def pointwise_kernel(full_ref, shift_ref, in_ref, out_ref):
    channels, rows_x, width = in_ref.shape
    rows = full_ref.shape[0] // channels
    shift = jnp.concatenate([shift_ref[...]] * (width // shift_ref.shape[1]), 1)

    def step(index, carry):
        values = in_ref[:, pl.ds(index * 2 * rows, 2 * rows), :].astype(jnp.float32)
        for half in range(2):
            block = values[:, half * rows : (half + 1) * rows].reshape(channels * rows, width)
            out = dot(full_ref[...], block.astype(jnp.bfloat16)) * DENSITY + shift
            out_ref[:, pl.ds(index * 2 * rows + half * rows, rows), :] = out.reshape(channels, rows, width)
        return carry

    lax.fori_loop(0, rows_x // (2 * rows), step, 0)


def pointwise_map(full, shift, values):
    return pl.pallas_call(
        pointwise_kernel,
        out_shape=jax.ShapeDtypeStruct(values.shape, jnp.float32),
        in_specs=whole(3),
        out_specs=whole(1)[0],
        compiler_params=params(),
        cost_estimate=takes(3),
        name="pointwise_map",
    )(full, shift, values)


def pointwise_back_kernel(full_ref, *refs):
    *terms, out_ref = refs
    channels, rows_x, width = out_ref.shape
    rows = full_ref.shape[0] // channels

    def step(index, carry):
        at = pl.ds(pl.multiple_of(index * 2 * rows, 2 * rows), 2 * rows)
        total = [0.0, 0.0]
        for term in range(2):
            values = [each[:, :, at, :].reshape(channels // 2, 2 * rows, width) for each in terms[term::2]]
            values = jnp.concatenate(values, 0).astype(jnp.float32)
            for half in range(2):
                block = values[:, half * rows : (half + 1) * rows].reshape(channels * rows, width)
                total[half] = total[half] + dot(full_ref[...], block.astype(jnp.bfloat16))
        for half in range(2):
            rows_at = pl.ds(index * 2 * rows + half * rows, rows)
            out_ref[:, rows_at, :] = total[half].reshape(channels, rows, width)
        return carry

    lax.fori_loop(0, rows_x // (2 * rows), step, 0)


def pointwise_back(full, terms):
    pairs, halves, rows_x, width = terms[0].shape
    return pl.pallas_call(
        pointwise_back_kernel,
        out_shape=jax.ShapeDtypeStruct((2 * pairs * halves, rows_x, width), jnp.float32),
        in_specs=whole(1 + len(terms)),
        out_specs=whole(1)[0],
        compiler_params=params(),
        cost_estimate=takes(4),
        name="pointwise_back",
    )(full, *terms)


def invert_x(pieces, xi_ref, st_ref):
    high, low = split(jnp.concatenate([piece[...] for piece in pieces], 0))
    deep = high.shape[1]
    left = jnp.concatenate([high, low], 1)
    found = dot(left, xi_ref[pl.ds(0, 2 * deep)]) + dot(high, xi_ref[pl.ds(2 * deep, deep)])
    st_ref[...] = found.reshape(st_ref.shape)


def spectral_part(index, half, st_ref, table):
    blocks, _, local_y, wide = st_ref.shape
    rows_x = wide // 4
    here = st_ref[:, index, :, pl.ds(half * 2 * rows_x, 2 * rows_x)].reshape(blocks * local_y, 2 * rows_x)
    parts = [here[:, :rows_x], here[:, rows_x:]]
    tall = jnp.transpose(jnp.concatenate(parts + parts, 0))
    high = tall.astype(jnp.bfloat16)
    first = lanes_of(tall.shape) < tall.shape[1] // 2
    mixed = jnp.where(first, tall, tall - high.astype(jnp.float32)).astype(jnp.bfloat16)
    return dot(jnp.concatenate([mixed, high], 1), table)


def slope_kernel(*refs, blocks):
    pieces, (xi_ref, ti_ref, tf_ref, xf_ref, mapped_ref, cot_ref) = refs[:blocks], refs[blocks : blocks + 6]
    terms, sums = refs[blocks + 6 : blocks + 10], refs[blocks + 10 : 2 * blocks + 10]
    st_ref, yt_ref, *before = refs[2 * blocks + 10 :]
    channels, rows_x, _ = mapped_ref.shape
    half_channels = channels // 2
    deep = tf_ref.shape[0] // 2
    modes_y = deep // 2
    local_y = modes_y // blocks
    invert_x(pieces, xi_ref, st_ref)

    def invert(index, parity):
        for half in range(2):
            channel = half * half_channels + index
            before[parity][half] = mapped_ref[channel] + spectral_part(index, half, st_ref, ti_ref[0])

    def slope(index, parity):
        for half in range(2):
            channel = half * half_channels + index
            grad = cot_ref[channel].astype(jnp.float32) * twice_gelu_slope(before[parity][half])
            high, low = split(grad)
            terms[2 * parity][index // 2, half] = high
            terms[2 * parity + 1][index // 2, half] = low

    def forward(index, parity):
        for half in range(2):
            high, low = terms[2 * parity][index // 2, half], terms[2 * parity + 1][index // 2, half]
            both = dot_rows(tf_ref[...], high)
            found = both[:deep] + both[deep:] + dot_rows(tf_ref[pl.ds(0, deep)], low)
            for block in range(blocks):
                for part in range(2):
                    at = part * modes_y + block * local_y
                    columns = pl.ds((2 * half + part) * rows_x, rows_x)
                    yt_ref[block, index, :, columns] = found[at : at + local_y]

    def step(pair, carry):
        index = 2 * pair
        forward(jnp.maximum(index - 1, 1), 1)
        invert(index + 1, 1)
        slope(index, 0)
        forward(index, 0)
        invert(jnp.minimum(index + 2, half_channels - 2), 0)
        slope(index + 1, 1)
        return carry

    invert(0, 0)
    lax.fori_loop(0, half_channels // 2, step, 0, unroll=2)
    forward(half_channels - 1, 1)
    high, low = split(yt_ref[...].reshape(-1, yt_ref.shape[-1]))
    lanes = xf_ref.shape[1] // 2
    both = dot(high, xf_ref[...])
    total = both[:, :lanes] + both[:, lanes:] + dot(low, xf_ref[:, :lanes])
    rows = total.shape[0] // blocks
    for block in range(blocks):
        sums[block][...] = total[block * rows : (block + 1) * rows]


def slope_step(pieces, tables, mapped, cotangent):
    ti, tf, xi, xf = tables
    blocks = len(pieces)
    channels, rows_x, width = mapped.shape
    half = channels // 2
    local_y = pieces[0].shape[0] // half
    results = pl.pallas_call(
        functools.partial(slope_kernel, blocks=blocks),
        out_shape=[jax.ShapeDtypeStruct((half // 2, 2, rows_x, width), jnp.bfloat16)] * 4
        + [jax.ShapeDtypeStruct(pieces[0].shape, jnp.float32)] * blocks,
        in_specs=whole(blocks + 6),
        out_specs=whole(4 + blocks),
        scratch_shapes=[pltpu.VMEM((blocks, half, local_y, 4 * rows_x), jnp.float32)] * 2
        + [pltpu.VMEM((2, rows_x, width), jnp.float32)] * 2,
        compiler_params=params(),
        cost_estimate=takes(8),
        name="slope_step",
    )(*pieces, xi, ti, tf, xf, mapped, cotangent)
    return results[:4], results[4:]


def finish_kernel(*refs, blocks, group):
    pieces, (xi_ref, ti_ref, part_ref, out_ref, st_ref, sum_ref, sems) = refs[:blocks], refs[blocks:]
    channels = part_ref.shape[0]
    invert_x(pieces, xi_ref, st_ref)

    def copies(index):
        for half in range(2):
            rows = pl.ds(half * (channels // 2) + index * group, group)
            yield pltpu.make_async_copy(sum_ref.at[rows], out_ref.at[rows], sems.at[half, index])

    def step(index, carry):
        for half in range(2):
            for member in range(group):
                place = index * group + member
                channel = half * (channels // 2) + place
                sum_ref[channel] = part_ref[channel] + spectral_part(place, half, st_ref, ti_ref[1])
        for copy in copies(index):
            copy.start()
        return carry

    def settle(index, carry):
        for copy in copies(index):
            copy.wait()
        return carry

    steps = channels // (2 * group)
    lax.fori_loop(0, steps, step, 0)
    lax.fori_loop(0, steps, settle, 0)


def finish(pieces, tables, part, group=2):
    ti, _, xi, _ = tables
    blocks = len(pieces)
    channels, rows_x, _ = part.shape
    half = channels // 2
    local_y = pieces[0].shape[0] // half
    return pl.pallas_call(
        functools.partial(finish_kernel, blocks=blocks, group=group),
        out_shape=jax.ShapeDtypeStruct(part.shape, jnp.float32),
        in_specs=whole(blocks + 3),
        out_specs=outside(1)[0],
        scratch_shapes=[
            pltpu.VMEM((blocks, half, local_y, 4 * rows_x), jnp.float32),
            pltpu.VMEM(part.shape, jnp.float32),
            pltpu.SemaphoreType.DMA((2, half // group)),
        ],
        compiler_params=params(20),
        cost_estimate=takes(4),
        name="finish",
    )(*pieces, xi, ti, part)


def exchange(piece, axis, count, flip):
    return lax.ppermute(piece, axis, [(i, i ^ flip) for i in range(count)])


def to_owners(same, other, count):
    pairs = list(pair(same, exchange(other, "py", count, 1)))
    return pairs[:1] + [exchange(pairs[i], "py", count, 2 * i) for i in range(1, len(pairs))]


def between_chips(piece, count):
    return [piece] + [exchange(piece, "py", count, step) for step in range(2, count, 2)]


def between_cores(pieces, count, beside):
    other = [beside] + [exchange(piece, "py", count, 1) for piece in pieces[1:]]
    return [each for pair in zip(pieces, other) for each in pair]


def from_all(piece, axis, count):
    return [piece] + [exchange(piece, axis, count, step) for step in range(count - 1, 0, -1)][::-1]


def to_all(pieces, axis, count):
    return pieces[:1] + [exchange(pieces[step], axis, count, step) for step in range(count - 1, 0, -1)][::-1]


def on_device_packed(
    field_in,
    cotangent,
    spectrum_saved,
    weight_store,
    block_slot,
    kx_modes,
    ky_modes,
    pointwise,
    bias_vector,
):
    channels, _, rows_x, width_y = field_in.shape
    count_x, count_y = lax.axis_size("px"), lax.axis_size("py")
    full_x = rows_x * count_x
    planes, local_y, local_x = spectrum_saved.shape[1:4]
    modes_x = kx_modes.shape[0]
    lanes = 2 * weight_store.shape[0]
    store = jnp.transpose(weight_store, (1, 2, 3, 0))
    barrier = lax.optimization_barrier
    spectrum = jnp.transpose(spectrum_saved, (1, 2, 3, 4, 0)).reshape(-1, channels)
    piece, everything = pack(block_slot, spectrum, ky_modes, kx_modes, bias_vector, pointwise, lanes)
    pieces = between_chips(piece, count_y)
    beside = exchange(piece, "py", count_y, 1)
    piece, small, packed = unpack(everything, store, piece.shape[1])
    pieces, beside, piece = barrier((pieces, beside, piece))
    pieces = between_cores([piece] + pieces[1:], count_y, beside)
    kept, slots, *mixed = mix(packed, pieces, planes, local_x)
    chosen = select(slots, modes_x, count_y)
    pairs = to_owners(*mixed, count_y)
    beside = exchange(packed, "py", count_y, 1)
    tables, full_map, full_back, shift = make_tables(small, full_x, rows_x, width_y, ky_modes.shape[0], modes_x)
    pairs, chosen, full_map, packed, beside = barrier((pairs, chosen, full_map, packed, beside))
    near = [exchange(packed, "py", count_y, step) for step in (2, 4)]
    received = from_all(to_modes(chosen, pairs, modes_x), "px", count_x)
    mapped = pointwise_map(full_map, shift, field_in[:, 0])
    received, mapped, near = barrier((received, mapped, near))
    low, high = halves(*near)
    far = [exchange(low, "py", count_y, 4), exchange(high, "py", count_y, 2)]
    terms, sums = slope_step(received, tables, mapped, cotangent[:, 0])
    sums, terms, far = barrier((list(sums), list(terms), far))
    others = join(near + far)
    others_beside = exchange(others, "py", count_y, 1)
    received = to_all(sums, "px", count_x)
    back = pointwise_back(full_back, terms)
    received, back, others_beside = barrier((received, back, others_beside))
    same, other, mixed = adjoint(chosen, received, [packed, beside, others, others_beside], modes_x)
    received = from_all(mixed, "px", count_x)
    pairs = to_owners(same, other, count_y)
    field_grad = finish(received, tables, back)
    blocks = weight_grad(kept, pairs)
    return (field_grad[:, None], jnp.transpose(blocks, (3, 0, 1, 2)))


def packs(mesh, channels, planes, rows, width, modes, capacity):
    count_x, count_y = mesh.shape["px"], mesh.shape["py"]
    powers = all(size & (size - 1) == 0 for size in (rows, width))
    return (
        powers
        and (count_x, count_y, planes) == (4, 8, 8)
        and channels == 32
        and 4 * modes == 128
        and 2 * capacity == 128
        and rows // count_x == 128
        and width % 256 == 0
        and modes // count_x == 8
    )


def solution(mesh):
    placed = (
        P(None, "py", "px", None),
        P(None, "py", "px", None),
        P(None, None, "px", "py", None),
        P(("px", "py"), None, None, None),
        P("py", "px"),
        P(),
        P(),
        P(),
        P(),
    )

    def run(*args):
        channels, planes, rows, width = args[0].shape
        capacity = args[3].shape[0] // mesh.size
        packed = packs(mesh, channels, planes, rows, width, args[5].shape[0], capacity)
        return jax.shard_map(
            on_device_packed if packed else on_device,
            mesh=mesh,
            in_specs=placed,
            out_specs=(P(None, "py", "px", None), P(("px", "py"), None, None, None)),
            check_vma=False,
        )(*args)

    return run
```

```python
import functools
import math

import jax
import jax.numpy as jnp
from jax import lax
from jax.experimental import pallas as pl
from jax.experimental.pallas import tpu as pltpu
from jax.sharding import PartitionSpec as P

precise = lax.Precision.HIGHEST


def phase_table(length, modes):
    points = lax.iota(jnp.int32, length)
    wrapped = points[:, None] * modes[None, :] % length
    angle = wrapped.astype(jnp.float32) * (2.0 * math.pi / length)
    return (jnp.cos(angle), jnp.sin(angle))


def gelu_slope(values):
    normal_cdf = 0.5 * (1.0 + lax.erf(values * 0.7071067811865476))
    density = jnp.exp(-0.5 * values * values) * 0.3989422804014327
    return normal_cdf + values * density


def channel_mix(blocks, spectrum):
    block_re = blocks[:, :, 0]
    block_im = blocks[:, :, 1]
    spec_re = spectrum[..., 0]
    spec_im = spectrum[..., 1]
    form = "baoc,czba->ozba"
    out_re = jnp.einsum(form, block_re, spec_re, precision=precise) - jnp.einsum(
        form, block_im, spec_im, precision=precise
    )
    out_im = jnp.einsum(form, block_re, spec_im, precision=precise) + jnp.einsum(
        form, block_im, spec_re, precision=precise
    )
    return jnp.stack([out_re, out_im], -1)


def channel_adjoint(blocks, spectrum):
    block_re = blocks[:, :, 0]
    block_im = blocks[:, :, 1]
    grad_re = spectrum[..., 0]
    grad_im = spectrum[..., 1]
    form = "baoc,ozba->czba"
    out_re = jnp.einsum(form, block_re, grad_re, precision=precise) + jnp.einsum(
        form, block_im, grad_im, precision=precise
    )
    out_im = jnp.einsum(form, block_re, grad_im, precision=precise) - jnp.einsum(
        form, block_im, grad_re, precision=precise
    )
    return jnp.stack([out_re, out_im], -1)


def block_gradient(spectrum_grad, spectrum):
    grad_re = spectrum_grad[..., 0]
    grad_im = spectrum_grad[..., 1]
    spec_re = spectrum[..., 0]
    spec_im = spectrum[..., 1]
    form = "ozba,czba->aboc"
    out_re = jnp.einsum(form, grad_re, spec_re, precision=precise) + jnp.einsum(
        form, grad_im, spec_im, precision=precise
    )
    out_im = jnp.einsum(form, grad_im, spec_re, precision=precise) - jnp.einsum(
        form, grad_re, spec_im, precision=precise
    )
    return jnp.stack([out_re, out_im], 2)


def invert_rows(spectrum, cos_rows, sin_rows):
    spec_re = spectrum[..., 0]
    spec_im = spectrum[..., 1]
    form = "czma,xa->czmx"
    back_re = jnp.einsum(form, spec_re, cos_rows, precision=precise) - jnp.einsum(
        form, spec_im, sin_rows, precision=precise
    )
    back_im = jnp.einsum(form, spec_re, sin_rows, precision=precise) + jnp.einsum(
        form, spec_im, cos_rows, precision=precise
    )
    joined = jnp.stack([back_re, back_im], 3)
    return joined.reshape(joined.shape[0], joined.shape[1], 2 * joined.shape[2], joined.shape[4])


def on_device(
    field_in,
    cotangent,
    spectrum_saved,
    weight_store,
    block_slot,
    kx_modes,
    ky_modes,
    pointwise,
    bias_vector,
):
    channels, planes, rows_x, width_y = field_in.shape
    full_x = rows_x * lax.axis_size("px")
    modes_y = ky_modes.shape[0]
    local_y = modes_y // lax.axis_size("px")
    capacity = weight_store.shape[0]
    factor = 1.0 / math.sqrt(full_x * width_y)
    cos_y, sin_y = phase_table(width_y, ky_modes)
    table_y = jnp.stack([cos_y, -sin_y], 2).reshape(width_y, 2 * modes_y)
    cos_x, sin_x = phase_table(full_x, kx_modes)
    store_row, slots_row = (
        lax.all_gather(weight_store, "py", axis=0, tiled=True),
        lax.all_gather(block_slot, "py", axis=0, tiled=True),
    )
    slots_flat = slots_row.reshape(-1)

    def inverse_planes(spectrum):
        joined = invert_rows(spectrum, cos_x, sin_x)
        returned = lax.all_to_all(joined, "px", split_axis=3, concat_axis=2, tiled=True)
        return factor * jnp.einsum("czkx,yk->czxy", returned, table_y, precision=precise)

    weight_full = pointwise.astype(jnp.float32)
    local_x = block_slot.shape[0]
    indices = jnp.transpose(block_slot).reshape(-1)
    blocks = jnp.take(store_row, indices, axis=0).reshape(local_y, local_x, 2, channels, channels)
    mixed = channel_mix(blocks, spectrum_saved)

    def from_modes(spectrum):
        return lax.all_to_all(spectrum, "py", split_axis=1, concat_axis=3, tiled=True)

    spectral = inverse_planes(from_modes(mixed))
    mapped = jnp.einsum("oc,czxy->ozxy", pointwise, field_in, preferred_element_type=jnp.float32)
    grad = cotangent.astype(jnp.float32) * gelu_slope(
        mapped + bias_vector.reshape(channels, 1, 1, 1) + spectral
    )
    partial_value = jnp.einsum("czxy,yk->czkx", grad, table_y, precision=precise)
    moved = lax.all_to_all(partial_value, "px", split_axis=2, concat_axis=3, tiled=True)
    pieces = moved.reshape(channels, planes, local_y, 2, full_x)
    part_re = pieces[:, :, :, 0]
    part_im = pieces[:, :, :, 1]
    form = "czmx,xk->czmk"
    real_part = jnp.einsum(form, part_re, cos_x, precision=precise) + jnp.einsum(
        form, part_im, sin_x, precision=precise
    )
    imag_part = jnp.einsum(form, part_im, cos_x, precision=precise) - jnp.einsum(
        form, part_re, sin_x, precision=precise
    )
    spectrum_grad = lax.all_to_all(
        factor * jnp.stack([real_part, imag_part], -1),
        "py",
        split_axis=3,
        concat_axis=1,
        tiled=True,
    )
    input_spectrum = channel_adjoint(blocks, spectrum_grad)
    local_grad = block_gradient(spectrum_grad, spectrum_saved)
    field_grad = jnp.einsum("oc,ozxy->czxy", weight_full, grad, precision=precise) + inverse_planes(
        from_modes(input_spectrum)
    )
    grads_all = lax.all_gather(local_grad, "py", axis=0, tiled=True)
    grads_flat = grads_all.reshape(slots_flat.shape[0], 2 * channels * channels)
    targets = lax.axis_index("py") * capacity + lax.iota(jnp.int32, capacity)
    select = (targets[:, None] == slots_flat[None, :]).astype(jnp.float32)
    store_flat = jnp.dot(select, grads_flat, precision=precise)
    store_grad = store_flat.reshape(capacity, 2, channels, channels)
    return (field_grad, store_grad)


def place_of():
    return lax.axis_index("px"), lax.axis_index("py")


def split(values):
    high = values.astype(jnp.bfloat16)
    return high, (values - high.astype(jnp.float32)).astype(jnp.bfloat16)


def dot(left, right):
    return jnp.dot(left, right, preferred_element_type=jnp.float32)


def dot_rows(left, right):
    return lax.dot_general(left, right, (((1,), (1,)), ((), ())), preferred_element_type=jnp.float32)


def lanes_of(shape):
    return lax.broadcasted_iota(jnp.int32, shape, len(shape) - 1)


def rows_of(shape):
    return lax.broadcasted_iota(jnp.int32, shape, len(shape) - 2)


def whole(count):
    return [pl.BlockSpec(memory_space=pltpu.VMEM)] * count


def params(mebibytes=12):
    return pltpu.CompilerParams(vmem_limit_bytes=mebibytes * 1024 * 1024)


def takes(microseconds):
    return pl.CostEstimate(flops=int(microseconds * 10**9), bytes_accessed=2**20, transcendentals=0)


def outside(count):
    return [pl.BlockSpec(memory_space=pltpu.HBM)] * count


def scalars(count):
    return [pl.BlockSpec(memory_space=pltpu.SMEM)] * count


DENSITY = math.sqrt(2.0 / math.pi)


def twice_gelu_slope(scaled):
    normal = 1.0 + lax.erf(scaled * (math.sqrt(0.5) / DENSITY))
    return normal + scaled * jnp.exp2(scaled * scaled * (-0.5 * math.log2(math.e) / DENSITY**2))


def column_of(ref, start, count):
    shape = (count, 128)
    row = rows_of(shape)
    out = jnp.zeros(shape, ref.dtype)
    for i in range(count):
        out = jnp.where(row == i, ref[start(i)], out)
    return out


def unpack_kernel(all_ref, store_ref, kept_ref, small_ref, packed_ref):
    wide, channels = kept_ref.shape[1], store_ref.shape[1]
    kept_ref[...] = all_ref[:, :wide]
    small_ref[...] = all_ref[:, wide:]
    for channel in range(channels):
        packed = jnp.concatenate([store_ref[0, channel], store_ref[1, channel]], 1)
        packed_ref[pl.ds(channel * channels, channels)] = packed


def unpack(everything, store, wide):
    rows, full = everything.shape
    channels, capacity = store.shape[2:]
    shapes = (rows, wide), (rows, full - wide), (channels * channels, 2 * capacity)
    return pl.pallas_call(
        unpack_kernel,
        out_shape=[jax.ShapeDtypeStruct(shape, jnp.float32) for shape in shapes],
        in_specs=whole(2),
        out_specs=whole(3),
        compiler_params=params(),
        cost_estimate=takes(0.5),
        name="unpack",
    )(everything, store)


def tables_kernel(small_ref, ti_ref, tf_ref, xi_ref, xf_ref, map_ref, back_ref, shift_ref, *, full_x):
    lanes, width = shift_ref.shape[1], tf_ref.shape[1]
    channels = small_ref.shape[0]
    rows = map_ref.shape[0] // channels
    ky, kx, bias, weight = (small_ref[:, pl.ds(i * lanes, lanes)] for i in range(4))
    ky, kx, bias = ky.astype(jnp.int32), kx.astype(jnp.int32), bias * DENSITY
    weight = weight[:, :channels].astype(jnp.bfloat16)
    map_ref[...] = spread(weight, rows, 1, lambda i: i).astype(jnp.bfloat16)
    pairs = channels // 4
    back = spread(weight, rows, 0, lambda i: i % 2 * 2 * pairs + i // 2 % pairs * 2 + i // (2 * pairs))
    back_ref[...] = (0.5 * back).astype(jnp.bfloat16)
    for channel in range(channels):
        shift_ref[pl.ds(channel * rows, rows)] = jnp.broadcast_to(bias[channel : channel + 1], (rows, bias.shape[1]))
    modes_x, rows_x = kx.shape[0], xf_ref.shape[0] // 4
    factor = 1.0 / math.sqrt(full_x * width)
    start = place_of()[0] * rows_x

    def angles(modes, points, length):
        return ((modes * points) & (length - 1)).astype(jnp.float32) * (2.0 * math.pi / length)

    ky = jnp.concatenate([ky] * (width // ky.shape[1]), 1)
    angle = angles(ky, lanes_of(ky.shape), width)
    waves = jnp.concatenate([jnp.cos(angle), -jnp.sin(angle)], 0)
    high, low = split(waves)
    tf_ref[...] = jnp.concatenate([high, low], 0)
    for index, scale in enumerate((DENSITY, 1.0)):
        high, low = split(scale * waves)
        ti_ref[index] = jnp.concatenate([high, high, low, jnp.zeros_like(low)], 0)
    angle = angles(kx, start + lanes_of((modes_x, rows_x)), full_x)
    cos, sin, zero = factor * jnp.cos(angle), factor * jnp.sin(angle), jnp.zeros_like(angle)
    parts = [[cos, sin, zero, zero], [-sin, cos, zero, zero], [zero, zero, cos, sin], [zero, zero, -sin, cos]]
    high, low = split(jnp.concatenate([jnp.concatenate(part, 1) for part in parts], 0))
    xi_ref[...] = jnp.concatenate([high, high, low], 0)
    cos = 0.5 * jnp.transpose(jnp.concatenate([cos] * 4, 0))
    sin = 0.5 * jnp.transpose(jnp.concatenate([sin] * 4, 0))
    zero = jnp.zeros_like(cos)
    lane = lanes_of(cos.shape)
    real = (lane // modes_x) % 2 == 0
    first = lane < 2 * modes_x
    from_re, from_im = jnp.where(real, cos, -sin), jnp.where(real, sin, cos)
    parts = [
        jnp.where(first, from_re, zero),
        jnp.where(first, from_im, zero),
        jnp.where(first, zero, from_re),
        jnp.where(first, zero, from_im),
    ]
    high, low = split(jnp.concatenate(parts, 0))
    xf_ref[...] = jnp.concatenate([high, low], 1)


def make_tables(small, full_x, rows_x, width, modes_y, modes_x, rows=8):
    channels, lanes = small.shape[0], small.shape[1] // 4
    shapes = (
        (2, 4 * 2 * modes_y, width),
        (2 * 2 * modes_y, width),
        (3 * 4 * modes_x, 4 * rows_x),
        (4 * rows_x, 8 * modes_x),
        (channels * rows, channels * rows),
        (channels * rows, channels * rows),
        (channels * rows, lanes),
    )
    types = [jnp.float32 if i == 6 else jnp.bfloat16 for i in range(len(shapes))]
    *tables, full_map, full_back, shift = pl.pallas_call(
        functools.partial(tables_kernel, full_x=full_x),
        out_shape=[jax.ShapeDtypeStruct(*each) for each in zip(shapes, types)],
        in_specs=whole(1),
        out_specs=whole(len(shapes)),
        compiler_params=params(),
        cost_estimate=takes(1),
        name="tables",
    )(small)
    return tables, full_map, full_back, shift


def duplicate(values):
    return jnp.concatenate([values, values], -1)


def pack_kernel(*refs):
    sources, (out_ref, all_ref), (*targets, sems) = refs[:6], refs[6:8], refs[8:]
    copies = [pltpu.make_async_copy(*pair, sems.at[i]) for i, pair in enumerate(zip(sources, targets))]
    for copy in copies:
        copy.start()
    for copy in copies:
        copy.wait()
    slots_ref, spec_ref, ky_ref, kx_ref, bias_ref, weight_ref = targets
    place_x, place_y = place_of()
    local_x, local_y = slots_ref.shape
    modes = local_x * local_y
    groups = spec_ref.shape[0] // modes
    columns = []
    for group in range(groups // 2):
        for part in range(2):
            columns.append(spec_ref[pl.ds(group * 2 * modes + part, modes, stride=2)])
    lanes = out_ref.shape[1] - groups * spec_ref.shape[1]
    numbers = column_of(slots_ref, lambda i: (i % local_x, i // local_x), modes)
    piece = jnp.concatenate(columns + [numbers.astype(jnp.float32)], 1)
    out_ref[...] = piece
    modes_y, modes_x, channels = ky_ref.shape[0], kx_ref.shape[0], bias_ref.shape[0]
    ky = column_of(ky_ref, lambda i: (place_x ^ (i // local_y)) * local_y + i % local_y, modes_y)
    kx = column_of(kx_ref, lambda i: (place_y ^ (i // local_x)) * local_x + i % local_x, modes_x)
    bias = column_of(bias_ref, lambda i: i, channels)
    weight = weight_ref[...].astype(jnp.float32)
    weight = jnp.concatenate([weight, jnp.zeros((channels, lanes - channels), jnp.float32)], 1)
    all_ref[...] = jnp.concatenate([piece, ky.astype(jnp.float32), kx.astype(jnp.float32), bias, weight], 1)


def pack(slots, spectrum, ky, kx, bias, weight, lanes):
    modes = slots.size
    width = spectrum.size // modes + lanes
    sources = (slots, spectrum, ky, kx, bias, weight)
    held = (pltpu.SMEM, pltpu.VMEM, pltpu.SMEM, pltpu.SMEM, pltpu.SMEM, pltpu.VMEM)
    return pl.pallas_call(
        pack_kernel,
        out_shape=[
            jax.ShapeDtypeStruct((modes, width), jnp.float32),
            jax.ShapeDtypeStruct((modes, width + 4 * lanes), jnp.float32),
        ],
        in_specs=outside(6),
        out_specs=whole(2),
        scratch_shapes=[space(each.shape, each.dtype) for space, each in zip(held, sources)]
        + [pltpu.SemaphoreType.DMA((6,))],
        compiler_params=params(60),
        name="pack",
    )(*sources)


def mix_kernel(packed_ref, *refs, count, local_x):
    pieces, refs = refs[:count], refs[count:]
    kept_ref, slots_ref, same_ref, other_ref, out_ref, uc_ref, ud_ref = refs
    planes, channels, lanes = out_ref.shape
    place = place_of()[1]
    capacity = lanes // 2
    wide = pieces[0].shape[1] - lanes
    local_y = pieces[0].shape[0] // local_x
    for index, piece in enumerate(pieces):
        for mode in range(local_y):
            rows = pl.ds((mode * count + index) * local_x, local_x)
            slots_ref[rows] = piece[pl.ds(mode * local_x, local_x), pl.ds(wide, lanes)]
    numbers = jnp.transpose(jnp.concatenate([piece[:, pl.ds(wide, lanes)] for piece in pieces], 0))
    wanted = (place * capacity + rows_of(numbers.shape) % capacity).astype(jnp.float32)
    chosen = (numbers == wanted).astype(jnp.bfloat16)
    high, low = split(jnp.concatenate([piece[:, pl.ds(0, wide)] for piece in pieces], 0))
    placed = jnp.transpose(dot(chosen, high) + dot(chosen, low))
    kept_ref[...] = placed
    parts = placed.reshape(planes, 2, channels, lanes)
    first = lanes_of((channels, lanes)) < capacity
    for plane in range(planes):
        rows = pl.ds(plane * channels, channels)
        uc_ref[rows] = jnp.where(first, parts[plane, 0], parts[plane, 1])
        ud_ref[rows] = jnp.where(first, parts[plane, 1], parts[plane, 0])
    def step(channel, carry):
        block = packed_ref[pl.ds(pl.multiple_of(channel * channels, channels), channels)]
        swapped = swap_halves(block)
        ra = jnp.where(first, block, swapped)
        rb = jnp.where(first, -swapped, block)
        for plane in range(planes):
            rows = pl.ds(plane * channels, channels)
            product = ra * uc_ref[rows] + rb * ud_ref[rows]
            out_ref[plane, pl.ds(channel, 1)] = jnp.sum(product, 0, keepdims=True)
        return carry

    lax.fori_loop(0, channels, step, 0, unroll=4)
    for step in range(planes):
        (other_ref if step % 2 else same_ref)[step // 2] = out_ref[place ^ step]


def mix(packed, pieces, planes, local_x):
    channels, lanes = math.isqrt(packed.shape[0]), packed.shape[1]
    count = len(pieces)
    return pl.pallas_call(
        functools.partial(mix_kernel, count=count, local_x=local_x),
        out_shape=[
            jax.ShapeDtypeStruct((2 * planes * channels, lanes), jnp.float32),
            jax.ShapeDtypeStruct((count * pieces[0].shape[0], lanes), jnp.float32),
            jax.ShapeDtypeStruct((planes // 2, channels, lanes), jnp.float32),
            jax.ShapeDtypeStruct((planes // 2, channels, lanes), jnp.float32),
        ],
        in_specs=whole(1 + count),
        out_specs=whole(4),
        scratch_shapes=[pltpu.VMEM((planes, channels, lanes), jnp.float32)]
        + [pltpu.VMEM((planes * channels, lanes), jnp.float32)] * 2,
        compiler_params=params(),
        cost_estimate=takes(3),
        name="mix",
    )(packed, *pieces)


def swap_halves(values):
    half = values.shape[-1] // 2
    return jnp.concatenate([values[..., half:], values[..., :half]], -1)


def weight_grad_kernel(kept_ref, *refs):
    *pairs, out_ref, gs_ref, sum_ref, sems = refs
    grads = [each.at[core] for each in pairs for core in range(2)]
    channels, lanes = grads[0].shape
    capacity = lanes // 2
    starts = []
    for index, grad in enumerate(grads):
        swapped = swap_halves(grad[...])
        gs_ref[index] = jnp.where(lanes_of(swapped.shape) < capacity, swapped, -swapped)
        starts.append((place_of()[1] ^ index) * 2 * channels)
    chunks = sems.shape[0]
    size = channels // chunks

    def send(chunk):
        rows = pl.ds(chunk * size, size)
        return pltpu.make_async_copy(sum_ref.at[:, rows], out_ref.at[:, rows], sems.at[chunk])

    def step(pair, carry):
        totals = [jnp.zeros((channels, lanes), jnp.float32)] * 2
        for index, start in enumerate(starts):
            real = kept_ref[pl.ds(start, channels)]
            imag = kept_ref[pl.ds(start + channels, channels)]
            for each in range(2):
                row = pl.ds(2 * pair + each, 1)
                totals[each] = totals[each] + real * grads[index][row] + imag * gs_ref[index, row]
        for each, total in enumerate(totals):
            sum_ref[0, 2 * pair + each] = total[:, :capacity]
            sum_ref[1, 2 * pair + each] = total[:, capacity:]
        return carry

    for chunk in range(chunks):
        lax.fori_loop(chunk * size // 2, (chunk + 1) * size // 2, step, 0, unroll=2)
        send(chunk).start()
    for chunk in range(chunks):
        send(chunk).wait()


def weight_grad(kept, pairs, chunks=4):
    _, channels, lanes = pairs[0].shape
    shape = (2, channels, channels, lanes // 2)
    return pl.pallas_call(
        weight_grad_kernel,
        out_shape=jax.ShapeDtypeStruct(shape, jnp.float32),
        in_specs=whole(1 + len(pairs)),
        out_specs=outside(1)[0],
        scratch_shapes=[
            pltpu.VMEM((2 * len(pairs), channels, lanes), jnp.float32),
            pltpu.VMEM(shape, jnp.float32),
            pltpu.SemaphoreType.DMA((chunks,)),
        ],
        compiler_params=params(),
        cost_estimate=takes(2),
        name="weight_grad",
    )(kept, *pairs)


def select_kernel(slots_ref, chosen_ref, *, modes_x):
    capacity = slots_ref.shape[1] // 2
    lanes = 2 * capacity
    place = place_of()[1]
    shape = (modes_x, lanes)
    lane = lanes_of(shape)
    first = lane < capacity
    zero = jnp.zeros(shape, jnp.float32)
    for mode in range(slots_ref.shape[0] // modes_x):
        numbers = slots_ref[pl.ds(mode * modes_x, modes_x)]
        for owner in range(chosen_ref.shape[1] // lanes):
            wanted = ((owner ^ place) * capacity + lane % capacity).astype(jnp.float32)
            hit = jnp.where(numbers == wanted, 1.0, 0.0)
            both = jnp.concatenate([jnp.where(first, hit, zero), jnp.where(first, zero, hit)], 0)
            chosen_ref[pl.ds(mode * 2 * modes_x, 2 * modes_x), pl.ds(owner * lanes, lanes)] = both.astype(jnp.bfloat16)


def select(slots, modes_x, count):
    return pl.pallas_call(
        functools.partial(select_kernel, modes_x=modes_x),
        out_shape=jax.ShapeDtypeStruct((2 * slots.shape[0], count * slots.shape[1]), jnp.bfloat16),
        in_specs=whole(1),
        out_specs=whole(1)[0],
        compiler_params=params(),
        cost_estimate=takes(0.5),
        name="select",
    )(slots)


def slots_to_modes(blocks, chosen_ref, out_ref, modes_x):
    channels = blocks[0].shape[0]
    half = channels // 2
    high, low = split(jnp.concatenate(blocks, 1))
    found = dot_rows(jnp.concatenate([high, low], 0), chosen_ref[...])
    found = found[:channels] + found[channels:]
    local_y = found.shape[1] // (2 * modes_x)
    for mode in range(local_y):
        piece = found[:, mode * 2 * modes_x : (mode + 1) * 2 * modes_x]
        out_ref[pl.ds(mode, half, stride=local_y)] = jnp.concatenate([piece[:half], piece[half:]], 1)


def to_modes_kernel(chosen_ref, *refs, modes_x):
    *pairs, out_ref = refs
    slots_to_modes([pair[core] for pair in pairs for core in range(2)], chosen_ref, out_ref, modes_x)


def to_modes(chosen, pairs, modes_x):
    _, channels, _ = pairs[0].shape
    local_y = chosen.shape[0] // (2 * modes_x)
    return pl.pallas_call(
        functools.partial(to_modes_kernel, modes_x=modes_x),
        out_shape=jax.ShapeDtypeStruct((channels // 2 * local_y, 4 * modes_x), jnp.float32),
        in_specs=whole(1 + len(pairs)),
        out_specs=whole(1)[0],
        compiler_params=params(),
        cost_estimate=takes(1),
        name="to_modes",
    )(chosen, *pairs)


def mix_back(block_of, values):
    channels, lanes = values.shape
    swapped = swap_halves(values)
    real = jnp.zeros((channels, lanes), jnp.float32)
    imag = real
    for channel in range(channels):
        block = block_of(channel)
        real = real + block * values[channel : channel + 1]
        imag = imag + block * swapped[channel : channel + 1]
    other_re, other_im = swap_halves(real), swap_halves(imag)
    return jnp.where(lanes_of(real.shape) < lanes // 2, real + other_re, other_im - imag)


def adjoint_kernel(chosen_ref, *refs, modes_x, blocks):
    pieces, stores, (same_ref, other_ref, out_ref, sum_ref) = refs[:blocks], refs[blocks:-4], refs[-4:]
    steps, channels, lanes = same_ref.shape
    half = channels // 2
    sum_ref[...] = sum(piece[...] for piece in pieces)
    local_y = sum_ref.shape[0] // half
    columns = []
    for mode in range(local_y):
        piece = sum_ref[pl.ds(mode, half, stride=local_y)]
        columns.append(jnp.concatenate([piece[:, : 2 * modes_x], piece[:, 2 * modes_x :]], 0))
    high, low = split(jnp.concatenate(columns, 1))
    found = dot(jnp.concatenate([high, low], 0), chosen_ref[...])
    found = found[:channels] + found[channels:]
    core = place_of()[1] % 2
    size = channels * channels
    here, beside, others, over = stores

    def block_at(owner):
        chip, other = owner // 2, owner % 2
        if chip == 0:
            return lambda channel: (beside if other else here)[pl.ds(channel * channels, channels)]
        if chip == 3:
            return lambda channel: (over if other else others)[pl.ds(2 * size + channel * channels, channels)]

        def block(channel):
            own = others[pl.ds(other * size + channel * channels, channels)]
            came = over[pl.ds((1 - other) * size + channel * channels, channels)]
            return jnp.where(core == 2 - chip, own, came)

        return block

    mixed = []
    for owner in range(2 * steps):
        values = found[:, owner * lanes : (owner + 1) * lanes]
        (other_ref if owner % 2 else same_ref)[owner // 2] = values
        mixed.append(mix_back(block_at(owner), values))
    slots_to_modes(mixed, chosen_ref, out_ref, modes_x)


def adjoint(chosen, pieces, stores, modes_x):
    blocks = len(pieces)
    channels, lanes = math.isqrt(stores[0].shape[0]), stores[0].shape[1]
    steps = chosen.shape[1] // (2 * lanes)
    return pl.pallas_call(
        functools.partial(adjoint_kernel, modes_x=modes_x, blocks=blocks),
        out_shape=[jax.ShapeDtypeStruct((steps, channels, lanes), jnp.float32)] * 2
        + [jax.ShapeDtypeStruct(pieces[0].shape, jnp.float32)],
        in_specs=whole(1 + blocks + len(stores)),
        out_specs=whole(3),
        scratch_shapes=[pltpu.VMEM(pieces[0].shape, jnp.float32)],
        compiler_params=params(),
        cost_estimate=takes(2),
        name="adjoint",
    )(chosen, *pieces, *stores)


def pair_kernel(same_ref, other_ref, *outs):
    for index, out in enumerate(outs):
        out[0] = same_ref[index]
        out[1] = other_ref[index]


def pair(same, other):
    return pl.pallas_call(
        pair_kernel,
        out_shape=[jax.ShapeDtypeStruct((2,) + same.shape[1:], same.dtype)] * same.shape[0],
        in_specs=whole(2),
        out_specs=whole(same.shape[0]),
        compiler_params=params(),
        cost_estimate=takes(0.3),
        name="pair",
    )(same, other)


def join_kernel(*refs):
    *parts, out_ref = refs
    start = 0
    for part in parts:
        out_ref[pl.ds(start, part.shape[0])] = part[...]
        start += part.shape[0]


def join(parts):
    rows = sum(part.shape[0] for part in parts)
    return pl.pallas_call(
        join_kernel,
        out_shape=jax.ShapeDtypeStruct((rows, parts[0].shape[1]), parts[0].dtype),
        in_specs=whole(len(parts)),
        out_specs=whole(1)[0],
        compiler_params=params(),
        cost_estimate=takes(0.1),
        name="join",
    )(*parts)


def spread(small, rows, axis, channel_of):
    count = small.shape[0]
    shape = (count * rows, count)
    take = (rows_of(shape) // rows == lanes_of(shape)).astype(jnp.bfloat16)
    shape = (count, count * rows)
    put = (channel_of(lanes_of(shape) // rows) == rows_of(shape)).astype(jnp.bfloat16)
    picked = dot(take, small) if axis else dot_rows(take, small)
    full = dot(picked.astype(jnp.bfloat16), put)
    shape = full.shape
    return jnp.where(rows_of(shape) % rows == lanes_of(shape) % rows, full, 0.0)


def pointwise_kernel(full_ref, shift_ref, in_ref, out_ref):
    channels, rows_x, width = in_ref.shape
    rows = full_ref.shape[0] // channels
    shift = jnp.concatenate([shift_ref[...]] * (width // shift_ref.shape[1]), 1)

    def step(index, carry):
        values = in_ref[:, pl.ds(index * 2 * rows, 2 * rows), :].astype(jnp.float32)
        for half in range(2):
            block = values[:, half * rows : (half + 1) * rows].reshape(channels * rows, width)
            out = dot(full_ref[...], block.astype(jnp.bfloat16)) * DENSITY + shift
            out_ref[:, pl.ds(index * 2 * rows + half * rows, rows), :] = out.reshape(channels, rows, width)
        return carry

    lax.fori_loop(0, rows_x // (2 * rows), step, 0)


def pointwise_map(full, shift, values):
    return pl.pallas_call(
        pointwise_kernel,
        out_shape=jax.ShapeDtypeStruct(values.shape, jnp.float32),
        in_specs=whole(3),
        out_specs=whole(1)[0],
        compiler_params=params(),
        cost_estimate=takes(3),
        name="pointwise_map",
    )(full, shift, values)


def pointwise_back_kernel(full_ref, *refs):
    *terms, out_ref = refs
    channels, rows_x, width = out_ref.shape
    rows = full_ref.shape[0] // channels

    def step(index, carry):
        at = pl.ds(pl.multiple_of(index * 2 * rows, 2 * rows), 2 * rows)
        total = [0.0, 0.0]
        for term in range(2):
            values = [each[:, :, at, :].reshape(channels // 2, 2 * rows, width) for each in terms[term::2]]
            values = jnp.concatenate(values, 0).astype(jnp.float32)
            for half in range(2):
                block = values[:, half * rows : (half + 1) * rows].reshape(channels * rows, width)
                total[half] = total[half] + dot(full_ref[...], block.astype(jnp.bfloat16))
        for half in range(2):
            rows_at = pl.ds(index * 2 * rows + half * rows, rows)
            out_ref[:, rows_at, :] = total[half].reshape(channels, rows, width)
        return carry

    lax.fori_loop(0, rows_x // (2 * rows), step, 0)


def pointwise_back(full, terms):
    pairs, halves, rows_x, width = terms[0].shape
    return pl.pallas_call(
        pointwise_back_kernel,
        out_shape=jax.ShapeDtypeStruct((2 * pairs * halves, rows_x, width), jnp.float32),
        in_specs=whole(1 + len(terms)),
        out_specs=whole(1)[0],
        compiler_params=params(),
        cost_estimate=takes(4),
        name="pointwise_back",
    )(full, *terms)


def invert_x(pieces, xi_ref, st_ref):
    high, low = split(jnp.concatenate([piece[...] for piece in pieces], 0))
    deep = high.shape[1]
    left = jnp.concatenate([high, low], 1)
    found = dot(left, xi_ref[pl.ds(0, 2 * deep)]) + dot(high, xi_ref[pl.ds(2 * deep, deep)])
    st_ref[...] = found.reshape(st_ref.shape)


def spectral_part(index, half, st_ref, table):
    blocks, _, local_y, wide = st_ref.shape
    rows_x = wide // 4
    here = st_ref[:, index, :, pl.ds(half * 2 * rows_x, 2 * rows_x)].reshape(blocks * local_y, 2 * rows_x)
    parts = [here[:, :rows_x], here[:, rows_x:]]
    tall = jnp.transpose(jnp.concatenate(parts + parts, 0))
    high = tall.astype(jnp.bfloat16)
    first = lanes_of(tall.shape) < tall.shape[1] // 2
    mixed = jnp.where(first, tall, tall - high.astype(jnp.float32)).astype(jnp.bfloat16)
    return dot(jnp.concatenate([mixed, high], 1), table)


def slope_kernel(*refs, blocks):
    pieces, (xi_ref, ti_ref, tf_ref, xf_ref, mapped_ref, cot_ref) = refs[:blocks], refs[blocks : blocks + 6]
    terms, sums = refs[blocks + 6 : blocks + 10], refs[blocks + 10 : 2 * blocks + 10]
    st_ref, yt_ref, *before = refs[2 * blocks + 10 :]
    channels, rows_x, _ = mapped_ref.shape
    half_channels = channels // 2
    deep = tf_ref.shape[0] // 2
    modes_y = deep // 2
    local_y = modes_y // blocks
    invert_x(pieces, xi_ref, st_ref)

    def invert(index, parity):
        for half in range(2):
            channel = half * half_channels + index
            before[parity][half] = mapped_ref[channel] + spectral_part(index, half, st_ref, ti_ref[0])

    def slope(index, parity):
        for half in range(2):
            channel = half * half_channels + index
            grad = cot_ref[channel].astype(jnp.float32) * twice_gelu_slope(before[parity][half])
            high, low = split(grad)
            terms[2 * parity][index // 2, half] = high
            terms[2 * parity + 1][index // 2, half] = low

    def forward(index, parity):
        for half in range(2):
            high, low = terms[2 * parity][index // 2, half], terms[2 * parity + 1][index // 2, half]
            both = dot_rows(tf_ref[...], high)
            found = both[:deep] + both[deep:] + dot_rows(tf_ref[pl.ds(0, deep)], low)
            for block in range(blocks):
                for part in range(2):
                    at = part * modes_y + block * local_y
                    columns = pl.ds((2 * half + part) * rows_x, rows_x)
                    yt_ref[block, index, :, columns] = found[at : at + local_y]

    def step(pair, carry):
        index = 2 * pair
        forward(jnp.maximum(index - 1, 1), 1)
        invert(index + 1, 1)
        slope(index, 0)
        forward(index, 0)
        invert(jnp.minimum(index + 2, half_channels - 2), 0)
        slope(index + 1, 1)
        return carry

    invert(0, 0)
    lax.fori_loop(0, half_channels // 2, step, 0, unroll=2)
    forward(half_channels - 1, 1)
    high, low = split(yt_ref[...].reshape(-1, yt_ref.shape[-1]))
    lanes = xf_ref.shape[1] // 2
    both = dot(high, xf_ref[...])
    total = both[:, :lanes] + both[:, lanes:] + dot(low, xf_ref[:, :lanes])
    rows = total.shape[0] // blocks
    for block in range(blocks):
        sums[block][...] = total[block * rows : (block + 1) * rows]


def slope_step(pieces, tables, mapped, cotangent):
    ti, tf, xi, xf = tables
    blocks = len(pieces)
    channels, rows_x, width = mapped.shape
    half = channels // 2
    local_y = pieces[0].shape[0] // half
    results = pl.pallas_call(
        functools.partial(slope_kernel, blocks=blocks),
        out_shape=[jax.ShapeDtypeStruct((half // 2, 2, rows_x, width), jnp.bfloat16)] * 4
        + [jax.ShapeDtypeStruct(pieces[0].shape, jnp.float32)] * blocks,
        in_specs=whole(blocks + 6),
        out_specs=whole(4 + blocks),
        scratch_shapes=[pltpu.VMEM((blocks, half, local_y, 4 * rows_x), jnp.float32)] * 2
        + [pltpu.VMEM((2, rows_x, width), jnp.float32)] * 2,
        compiler_params=params(),
        cost_estimate=takes(8),
        name="slope_step",
    )(*pieces, xi, ti, tf, xf, mapped, cotangent)
    return results[:4], results[4:]


def finish_kernel(*refs, blocks, group):
    pieces, (xi_ref, ti_ref, part_ref, out_ref, st_ref, sum_ref, sems) = refs[:blocks], refs[blocks:]
    channels = part_ref.shape[0]
    invert_x(pieces, xi_ref, st_ref)

    def copies(index):
        for half in range(2):
            rows = pl.ds(half * (channels // 2) + index * group, group)
            yield pltpu.make_async_copy(sum_ref.at[rows], out_ref.at[rows], sems.at[half, index])

    def step(index, carry):
        for half in range(2):
            for member in range(group):
                place = index * group + member
                channel = half * (channels // 2) + place
                sum_ref[channel] = part_ref[channel] + spectral_part(place, half, st_ref, ti_ref[1])
        for copy in copies(index):
            copy.start()
        return carry

    def settle(index, carry):
        for copy in copies(index):
            copy.wait()
        return carry

    steps = channels // (2 * group)
    lax.fori_loop(0, steps, step, 0)
    lax.fori_loop(0, steps, settle, 0)


def finish(pieces, tables, part, group=2):
    ti, _, xi, _ = tables
    blocks = len(pieces)
    channels, rows_x, _ = part.shape
    half = channels // 2
    local_y = pieces[0].shape[0] // half
    return pl.pallas_call(
        functools.partial(finish_kernel, blocks=blocks, group=group),
        out_shape=jax.ShapeDtypeStruct(part.shape, jnp.float32),
        in_specs=whole(blocks + 3),
        out_specs=outside(1)[0],
        scratch_shapes=[
            pltpu.VMEM((blocks, half, local_y, 4 * rows_x), jnp.float32),
            pltpu.VMEM(part.shape, jnp.float32),
            pltpu.SemaphoreType.DMA((2, half // group)),
        ],
        compiler_params=params(20),
        cost_estimate=takes(4),
        name="finish",
    )(*pieces, xi, ti, part)


def exchange(piece, axis, count, flip):
    return lax.ppermute(piece, axis, [(i, i ^ flip) for i in range(count)])


def exchange_two(piece, axis, count, *flips):
    return lax.ppermute(piece, axis, [(i, i ^ flips[i % 2]) for i in range(count)])


def to_owners(same, other, count):
    pairs = list(pair(same, exchange(other, "py", count, 1)))
    return pairs[:1] + [exchange(pairs[i], "py", count, 2 * i) for i in range(1, len(pairs))]


def between_chips(piece, count):
    return [piece] + [exchange(piece, "py", count, step) for step in range(2, count, 2)]


def between_cores(pieces, count, beside):
    other = [beside] + [exchange(piece, "py", count, 1) for piece in pieces[1:]]
    return [each for pair in zip(pieces, other) for each in pair]


def from_all(piece, axis, count):
    return [piece] + [exchange(piece, axis, count, step) for step in range(count - 1, 0, -1)][::-1]


def to_all(pieces, axis, count):
    return pieces[:1] + [exchange(pieces[step], axis, count, step) for step in range(count - 1, 0, -1)][::-1]


def on_device_packed(
    field_in,
    cotangent,
    spectrum_saved,
    weight_store,
    block_slot,
    kx_modes,
    ky_modes,
    pointwise,
    bias_vector,
):
    channels, _, rows_x, width_y = field_in.shape
    count_x, count_y = lax.axis_size("px"), lax.axis_size("py")
    full_x = rows_x * count_x
    planes, local_y, local_x = spectrum_saved.shape[1:4]
    modes_x = kx_modes.shape[0]
    lanes = 2 * weight_store.shape[0]
    store = jnp.transpose(weight_store, (1, 2, 3, 0))
    barrier = lax.optimization_barrier
    spectrum = jnp.transpose(spectrum_saved, (1, 2, 3, 4, 0)).reshape(-1, channels)
    piece, everything = pack(block_slot, spectrum, ky_modes, kx_modes, bias_vector, pointwise, lanes)
    pieces = between_chips(piece, count_y)
    beside = exchange(piece, "py", count_y, 1)
    piece, small, packed = unpack(everything, store, piece.shape[1])
    pieces, beside, piece = barrier((pieces, beside, piece))
    pieces = between_cores([piece] + pieces[1:], count_y, beside)
    kept, slots, *mixed = mix(packed, pieces, planes, local_x)
    chosen = select(slots, modes_x, count_y)
    pairs = to_owners(*mixed, count_y)
    beside = exchange(packed, "py", count_y, 1)
    tables, full_map, full_back, shift = make_tables(small, full_x, rows_x, width_y, ky_modes.shape[0], modes_x)
    pairs, chosen, full_map, packed, beside = barrier((pairs, chosen, full_map, packed, beside))
    near = exchange_two(packed, "py", count_y, 4, 2)
    near_other = exchange_two(beside, "py", count_y, 4, 2)
    received = from_all(to_modes(chosen, pairs, modes_x), "px", count_x)
    mapped = pointwise_map(full_map, shift, field_in[:, 0])
    received, mapped, near = barrier((received, mapped, near))
    far = exchange_two(near, "py", count_y, 2, 4)
    terms, sums = slope_step(received, tables, mapped, cotangent[:, 0])
    sums, terms, far, near_other = barrier((list(sums), list(terms), far, near_other))
    others = join([near, near_other, far])
    others_beside = exchange(others, "py", count_y, 1)
    received = to_all(sums, "px", count_x)
    back = pointwise_back(full_back, terms)
    received, back, others_beside = barrier((received, back, others_beside))
    same, other, mixed = adjoint(chosen, received, [packed, beside, others, others_beside], modes_x)
    received = from_all(mixed, "px", count_x)
    pairs = to_owners(same, other, count_y)
    field_grad = finish(received, tables, back)
    blocks = weight_grad(kept, pairs)
    return (field_grad[:, None], jnp.transpose(blocks, (3, 0, 1, 2)))


def packs(mesh, channels, planes, rows, width, modes, capacity):
    count_x, count_y = mesh.shape["px"], mesh.shape["py"]
    powers = all(size & (size - 1) == 0 for size in (rows, width))
    return (
        powers
        and (count_x, count_y, planes) == (4, 8, 8)
        and channels == 32
        and 4 * modes == 128
        and 2 * capacity == 128
        and rows // count_x == 128
        and width % 256 == 0
        and modes // count_x == 8
    )


def solution(mesh):
    placed = (
        P(None, "py", "px", None),
        P(None, "py", "px", None),
        P(None, None, "px", "py", None),
        P(("px", "py"), None, None, None),
        P("py", "px"),
        P(),
        P(),
        P(),
        P(),
    )

    def run(*args):
        channels, planes, rows, width = args[0].shape
        capacity = args[3].shape[0] // mesh.size
        packed = packs(mesh, channels, planes, rows, width, args[5].shape[0], capacity)
        return jax.shard_map(
            on_device_packed if packed else on_device,
            mesh=mesh,
            in_specs=placed,
            out_specs=(P(None, "py", "px", None), P(("px", "py"), None, None, None)),
            check_vma=False,
        )(*args)

    return run
```

```python
import functools
import math

import jax
import jax.numpy as jnp
from jax import lax
from jax.experimental import pallas as pl
from jax.experimental.pallas import tpu as pltpu
from jax.sharding import PartitionSpec as P

precise = lax.Precision.HIGHEST


def phase_table(length, modes):
    points = lax.iota(jnp.int32, length)
    wrapped = points[:, None] * modes[None, :] % length
    angle = wrapped.astype(jnp.float32) * (2.0 * math.pi / length)
    return (jnp.cos(angle), jnp.sin(angle))


def gelu_slope(values):
    normal_cdf = 0.5 * (1.0 + lax.erf(values * 0.7071067811865476))
    density = jnp.exp(-0.5 * values * values) * 0.3989422804014327
    return normal_cdf + values * density


def channel_mix(blocks, spectrum):
    block_re = blocks[:, :, 0]
    block_im = blocks[:, :, 1]
    spec_re = spectrum[..., 0]
    spec_im = spectrum[..., 1]
    form = "baoc,czba->ozba"
    out_re = jnp.einsum(form, block_re, spec_re, precision=precise) - jnp.einsum(
        form, block_im, spec_im, precision=precise
    )
    out_im = jnp.einsum(form, block_re, spec_im, precision=precise) + jnp.einsum(
        form, block_im, spec_re, precision=precise
    )
    return jnp.stack([out_re, out_im], -1)


def channel_adjoint(blocks, spectrum):
    block_re = blocks[:, :, 0]
    block_im = blocks[:, :, 1]
    grad_re = spectrum[..., 0]
    grad_im = spectrum[..., 1]
    form = "baoc,ozba->czba"
    out_re = jnp.einsum(form, block_re, grad_re, precision=precise) + jnp.einsum(
        form, block_im, grad_im, precision=precise
    )
    out_im = jnp.einsum(form, block_re, grad_im, precision=precise) - jnp.einsum(
        form, block_im, grad_re, precision=precise
    )
    return jnp.stack([out_re, out_im], -1)


def block_gradient(spectrum_grad, spectrum):
    grad_re = spectrum_grad[..., 0]
    grad_im = spectrum_grad[..., 1]
    spec_re = spectrum[..., 0]
    spec_im = spectrum[..., 1]
    form = "ozba,czba->aboc"
    out_re = jnp.einsum(form, grad_re, spec_re, precision=precise) + jnp.einsum(
        form, grad_im, spec_im, precision=precise
    )
    out_im = jnp.einsum(form, grad_im, spec_re, precision=precise) - jnp.einsum(
        form, grad_re, spec_im, precision=precise
    )
    return jnp.stack([out_re, out_im], 2)


def invert_rows(spectrum, cos_rows, sin_rows):
    spec_re = spectrum[..., 0]
    spec_im = spectrum[..., 1]
    form = "czma,xa->czmx"
    back_re = jnp.einsum(form, spec_re, cos_rows, precision=precise) - jnp.einsum(
        form, spec_im, sin_rows, precision=precise
    )
    back_im = jnp.einsum(form, spec_re, sin_rows, precision=precise) + jnp.einsum(
        form, spec_im, cos_rows, precision=precise
    )
    joined = jnp.stack([back_re, back_im], 3)
    return joined.reshape(joined.shape[0], joined.shape[1], 2 * joined.shape[2], joined.shape[4])


def on_device(
    field_in,
    cotangent,
    spectrum_saved,
    weight_store,
    block_slot,
    kx_modes,
    ky_modes,
    pointwise,
    bias_vector,
):
    channels, planes, rows_x, width_y = field_in.shape
    full_x = rows_x * lax.axis_size("px")
    modes_y = ky_modes.shape[0]
    local_y = modes_y // lax.axis_size("px")
    capacity = weight_store.shape[0]
    factor = 1.0 / math.sqrt(full_x * width_y)
    cos_y, sin_y = phase_table(width_y, ky_modes)
    table_y = jnp.stack([cos_y, -sin_y], 2).reshape(width_y, 2 * modes_y)
    cos_x, sin_x = phase_table(full_x, kx_modes)
    store_row, slots_row = (
        lax.all_gather(weight_store, "py", axis=0, tiled=True),
        lax.all_gather(block_slot, "py", axis=0, tiled=True),
    )
    slots_flat = slots_row.reshape(-1)

    def inverse_planes(spectrum):
        joined = invert_rows(spectrum, cos_x, sin_x)
        returned = lax.all_to_all(joined, "px", split_axis=3, concat_axis=2, tiled=True)
        return factor * jnp.einsum("czkx,yk->czxy", returned, table_y, precision=precise)

    weight_full = pointwise.astype(jnp.float32)
    local_x = block_slot.shape[0]
    indices = jnp.transpose(block_slot).reshape(-1)
    blocks = jnp.take(store_row, indices, axis=0).reshape(local_y, local_x, 2, channels, channels)
    mixed = channel_mix(blocks, spectrum_saved)

    def from_modes(spectrum):
        return lax.all_to_all(spectrum, "py", split_axis=1, concat_axis=3, tiled=True)

    spectral = inverse_planes(from_modes(mixed))
    mapped = jnp.einsum("oc,czxy->ozxy", pointwise, field_in, preferred_element_type=jnp.float32)
    grad = cotangent.astype(jnp.float32) * gelu_slope(
        mapped + bias_vector.reshape(channels, 1, 1, 1) + spectral
    )
    partial_value = jnp.einsum("czxy,yk->czkx", grad, table_y, precision=precise)
    moved = lax.all_to_all(partial_value, "px", split_axis=2, concat_axis=3, tiled=True)
    pieces = moved.reshape(channels, planes, local_y, 2, full_x)
    part_re = pieces[:, :, :, 0]
    part_im = pieces[:, :, :, 1]
    form = "czmx,xk->czmk"
    real_part = jnp.einsum(form, part_re, cos_x, precision=precise) + jnp.einsum(
        form, part_im, sin_x, precision=precise
    )
    imag_part = jnp.einsum(form, part_im, cos_x, precision=precise) - jnp.einsum(
        form, part_re, sin_x, precision=precise
    )
    spectrum_grad = lax.all_to_all(
        factor * jnp.stack([real_part, imag_part], -1),
        "py",
        split_axis=3,
        concat_axis=1,
        tiled=True,
    )
    input_spectrum = channel_adjoint(blocks, spectrum_grad)
    local_grad = block_gradient(spectrum_grad, spectrum_saved)
    field_grad = jnp.einsum("oc,ozxy->czxy", weight_full, grad, precision=precise) + inverse_planes(
        from_modes(input_spectrum)
    )
    grads_all = lax.all_gather(local_grad, "py", axis=0, tiled=True)
    grads_flat = grads_all.reshape(slots_flat.shape[0], 2 * channels * channels)
    targets = lax.axis_index("py") * capacity + lax.iota(jnp.int32, capacity)
    select = (targets[:, None] == slots_flat[None, :]).astype(jnp.float32)
    store_flat = jnp.dot(select, grads_flat, precision=precise)
    store_grad = store_flat.reshape(capacity, 2, channels, channels)
    return (field_grad, store_grad)


def place_of():
    return lax.axis_index("px"), lax.axis_index("py")


TURN = (0, 2, 1, 3)


def flip_at(step):
    chip, other = step // 2, step % 2
    core = lax.axis_index("py") % 2
    return jnp.where(core == 1, 2 * chip + other, 2 * TURN[chip] + other)


def split(values):
    high = values.astype(jnp.bfloat16)
    return high, (values - high.astype(jnp.float32)).astype(jnp.bfloat16)


def dot(left, right):
    return jnp.dot(left, right, preferred_element_type=jnp.float32)


def dot_rows(left, right):
    return lax.dot_general(left, right, (((1,), (1,)), ((), ())), preferred_element_type=jnp.float32)


def lanes_of(shape):
    return lax.broadcasted_iota(jnp.int32, shape, len(shape) - 1)


def rows_of(shape):
    return lax.broadcasted_iota(jnp.int32, shape, len(shape) - 2)


def whole(count):
    return [pl.BlockSpec(memory_space=pltpu.VMEM)] * count


def params(mebibytes=12):
    return pltpu.CompilerParams(vmem_limit_bytes=mebibytes * 1024 * 1024)


def takes(microseconds):
    return pl.CostEstimate(flops=int(microseconds * 10**9), bytes_accessed=2**20, transcendentals=0)


def outside(count):
    return [pl.BlockSpec(memory_space=pltpu.HBM)] * count


def scalars(count):
    return [pl.BlockSpec(memory_space=pltpu.SMEM)] * count


DENSITY = math.sqrt(2.0 / math.pi)


def twice_gelu_slope(scaled):
    normal = 1.0 + lax.erf(scaled * (math.sqrt(0.5) / DENSITY))
    return normal + scaled * jnp.exp2(scaled * scaled * (-0.5 * math.log2(math.e) / DENSITY**2))


def column_of(ref, start, count):
    shape = (count, 128)
    row = rows_of(shape)
    out = jnp.zeros(shape, ref.dtype)
    for i in range(count):
        out = jnp.where(row == i, ref[start(i)], out)
    return out


def unpack_kernel(all_ref, store_ref, kept_ref, small_ref, packed_ref):
    wide, channels = kept_ref.shape[1], store_ref.shape[1]
    kept_ref[...] = all_ref[:, :wide]
    small_ref[...] = all_ref[:, wide:]
    for channel in range(channels):
        packed = jnp.concatenate([store_ref[0, channel], store_ref[1, channel]], 1)
        packed_ref[pl.ds(channel * channels, channels)] = packed


def unpack(everything, store, wide):
    rows, full = everything.shape
    channels, capacity = store.shape[2:]
    shapes = (rows, wide), (rows, full - wide), (channels * channels, 2 * capacity)
    return pl.pallas_call(
        unpack_kernel,
        out_shape=[jax.ShapeDtypeStruct(shape, jnp.float32) for shape in shapes],
        in_specs=whole(2),
        out_specs=whole(3),
        compiler_params=params(),
        cost_estimate=takes(0.5),
        name="unpack",
    )(everything, store)


def tables_kernel(small_ref, ti_ref, tf_ref, xi_ref, xf_ref, map_ref, back_ref, shift_ref, *, full_x):
    lanes, width = shift_ref.shape[1], tf_ref.shape[1]
    channels = small_ref.shape[0]
    rows = map_ref.shape[0] // channels
    ky, kx, bias, weight = (small_ref[:, pl.ds(i * lanes, lanes)] for i in range(4))
    ky, kx, bias = ky.astype(jnp.int32), kx.astype(jnp.int32), bias * DENSITY
    weight = weight[:, :channels].astype(jnp.bfloat16)
    map_ref[...] = spread(weight, rows, 1, lambda i: i).astype(jnp.bfloat16)
    pairs = channels // 4
    back = spread(weight, rows, 0, lambda i: i % 2 * 2 * pairs + i // 2 % pairs * 2 + i // (2 * pairs))
    back_ref[...] = (0.5 * back).astype(jnp.bfloat16)
    for channel in range(channels):
        shift_ref[pl.ds(channel * rows, rows)] = jnp.broadcast_to(bias[channel : channel + 1], (rows, bias.shape[1]))
    modes_x, rows_x = kx.shape[0], xf_ref.shape[0] // 4
    factor = 1.0 / math.sqrt(full_x * width)
    start = place_of()[0] * rows_x

    def angles(modes, points, length):
        return ((modes * points) & (length - 1)).astype(jnp.float32) * (2.0 * math.pi / length)

    ky = jnp.concatenate([ky] * (width // ky.shape[1]), 1)
    angle = angles(ky, lanes_of(ky.shape), width)
    waves = jnp.concatenate([jnp.cos(angle), -jnp.sin(angle)], 0)
    high, low = split(waves)
    tf_ref[...] = jnp.concatenate([high, low], 0)
    for index, scale in enumerate((DENSITY, 1.0)):
        high, low = split(scale * waves)
        ti_ref[index] = jnp.concatenate([high, high, low, jnp.zeros_like(low)], 0)
    angle = angles(kx, start + lanes_of((modes_x, rows_x)), full_x)
    cos, sin, zero = factor * jnp.cos(angle), factor * jnp.sin(angle), jnp.zeros_like(angle)
    parts = [[cos, sin, zero, zero], [-sin, cos, zero, zero], [zero, zero, cos, sin], [zero, zero, -sin, cos]]
    high, low = split(jnp.concatenate([jnp.concatenate(part, 1) for part in parts], 0))
    xi_ref[...] = jnp.concatenate([high, high, low], 0)
    cos = 0.5 * jnp.transpose(jnp.concatenate([cos] * 4, 0))
    sin = 0.5 * jnp.transpose(jnp.concatenate([sin] * 4, 0))
    zero = jnp.zeros_like(cos)
    lane = lanes_of(cos.shape)
    real = (lane // modes_x) % 2 == 0
    first = lane < 2 * modes_x
    from_re, from_im = jnp.where(real, cos, -sin), jnp.where(real, sin, cos)
    parts = [
        jnp.where(first, from_re, zero),
        jnp.where(first, from_im, zero),
        jnp.where(first, zero, from_re),
        jnp.where(first, zero, from_im),
    ]
    high, low = split(jnp.concatenate(parts, 0))
    xf_ref[...] = jnp.concatenate([high, low], 1)


def make_tables(small, full_x, rows_x, width, modes_y, modes_x, rows=8):
    channels, lanes = small.shape[0], small.shape[1] // 4
    shapes = (
        (2, 4 * 2 * modes_y, width),
        (2 * 2 * modes_y, width),
        (3 * 4 * modes_x, 4 * rows_x),
        (4 * rows_x, 8 * modes_x),
        (channels * rows, channels * rows),
        (channels * rows, channels * rows),
        (channels * rows, lanes),
    )
    types = [jnp.float32 if i == 6 else jnp.bfloat16 for i in range(len(shapes))]
    *tables, full_map, full_back, shift = pl.pallas_call(
        functools.partial(tables_kernel, full_x=full_x),
        out_shape=[jax.ShapeDtypeStruct(*each) for each in zip(shapes, types)],
        in_specs=whole(1),
        out_specs=whole(len(shapes)),
        compiler_params=params(),
        cost_estimate=takes(1),
        name="tables",
    )(small)
    return tables, full_map, full_back, shift


def duplicate(values):
    return jnp.concatenate([values, values], -1)


def pack_kernel(*refs):
    sources, (out_ref, all_ref), (*targets, sems) = refs[:6], refs[6:8], refs[8:]
    copies = [pltpu.make_async_copy(*pair, sems.at[i]) for i, pair in enumerate(zip(sources, targets))]
    for copy in copies:
        copy.start()
    for copy in copies:
        copy.wait()
    slots_ref, spec_ref, ky_ref, kx_ref, bias_ref, weight_ref = targets
    place_x, place_y = place_of()
    local_x, local_y = slots_ref.shape
    modes = local_x * local_y
    groups = spec_ref.shape[0] // modes
    columns = []
    for group in range(groups // 2):
        for part in range(2):
            columns.append(spec_ref[pl.ds(group * 2 * modes + part, modes, stride=2)])
    lanes = out_ref.shape[1] - groups * spec_ref.shape[1]
    numbers = column_of(slots_ref, lambda i: (i % local_x, i // local_x), modes)
    piece = jnp.concatenate(columns + [numbers.astype(jnp.float32)], 1)
    out_ref[...] = piece
    modes_y, modes_x, channels = ky_ref.shape[0], kx_ref.shape[0], bias_ref.shape[0]
    ky = column_of(ky_ref, lambda i: (place_x ^ (i // local_y)) * local_y + i % local_y, modes_y)
    kx = column_of(kx_ref, lambda i: (place_y ^ flip_at(i // local_x)) * local_x + i % local_x, modes_x)
    bias = column_of(bias_ref, lambda i: i, channels)
    weight = weight_ref[...].astype(jnp.float32)
    weight = jnp.concatenate([weight, jnp.zeros((channels, lanes - channels), jnp.float32)], 1)
    all_ref[...] = jnp.concatenate([piece, ky.astype(jnp.float32), kx.astype(jnp.float32), bias, weight], 1)


def pack(slots, spectrum, ky, kx, bias, weight, lanes):
    modes = slots.size
    width = spectrum.size // modes + lanes
    sources = (slots, spectrum, ky, kx, bias, weight)
    held = (pltpu.SMEM, pltpu.VMEM, pltpu.SMEM, pltpu.SMEM, pltpu.SMEM, pltpu.VMEM)
    return pl.pallas_call(
        pack_kernel,
        out_shape=[
            jax.ShapeDtypeStruct((modes, width), jnp.float32),
            jax.ShapeDtypeStruct((modes, width + 4 * lanes), jnp.float32),
        ],
        in_specs=outside(6),
        out_specs=whole(2),
        scratch_shapes=[space(each.shape, each.dtype) for space, each in zip(held, sources)]
        + [pltpu.SemaphoreType.DMA((6,))],
        compiler_params=params(60),
        name="pack",
    )(*sources)


def mix_kernel(packed_ref, *refs, count, local_x):
    pieces, refs = refs[:count], refs[count:]
    kept_ref, slots_ref, same_ref, other_ref, out_ref, uc_ref, ud_ref = refs
    planes, channels, lanes = out_ref.shape
    place = place_of()[1]
    capacity = lanes // 2
    wide = pieces[0].shape[1] - lanes
    local_y = pieces[0].shape[0] // local_x
    for index, piece in enumerate(pieces):
        for mode in range(local_y):
            rows = pl.ds((mode * count + index) * local_x, local_x)
            slots_ref[rows] = piece[pl.ds(mode * local_x, local_x), pl.ds(wide, lanes)]
    numbers = jnp.transpose(jnp.concatenate([piece[:, pl.ds(wide, lanes)] for piece in pieces], 0))
    wanted = (place * capacity + rows_of(numbers.shape) % capacity).astype(jnp.float32)
    chosen = (numbers == wanted).astype(jnp.bfloat16)
    high, low = split(jnp.concatenate([piece[:, pl.ds(0, wide)] for piece in pieces], 0))
    placed = jnp.transpose(dot(chosen, high) + dot(chosen, low))
    kept_ref[...] = placed
    parts = placed.reshape(planes, 2, channels, lanes)
    first = lanes_of((channels, lanes)) < capacity
    for plane in range(planes):
        rows = pl.ds(plane * channels, channels)
        uc_ref[rows] = jnp.where(first, parts[plane, 0], parts[plane, 1])
        ud_ref[rows] = jnp.where(first, parts[plane, 1], parts[plane, 0])
    def step(channel, carry):
        block = packed_ref[pl.ds(pl.multiple_of(channel * channels, channels), channels)]
        swapped = swap_halves(block)
        ra = jnp.where(first, block, swapped)
        rb = jnp.where(first, -swapped, block)
        for plane in range(planes):
            rows = pl.ds(plane * channels, channels)
            product = ra * uc_ref[rows] + rb * ud_ref[rows]
            out_ref[plane, pl.ds(channel, 1)] = jnp.sum(product, 0, keepdims=True)
        return carry

    lax.fori_loop(0, channels, step, 0, unroll=4)
    for step in range(planes):
        (other_ref if step % 2 else same_ref)[step // 2] = out_ref[place ^ flip_at(step)]


def mix(packed, pieces, planes, local_x):
    channels, lanes = math.isqrt(packed.shape[0]), packed.shape[1]
    count = len(pieces)
    return pl.pallas_call(
        functools.partial(mix_kernel, count=count, local_x=local_x),
        out_shape=[
            jax.ShapeDtypeStruct((2 * planes * channels, lanes), jnp.float32),
            jax.ShapeDtypeStruct((count * pieces[0].shape[0], lanes), jnp.float32),
            jax.ShapeDtypeStruct((planes // 2, channels, lanes), jnp.float32),
            jax.ShapeDtypeStruct((planes // 2, channels, lanes), jnp.float32),
        ],
        in_specs=whole(1 + count),
        out_specs=whole(4),
        scratch_shapes=[pltpu.VMEM((planes, channels, lanes), jnp.float32)]
        + [pltpu.VMEM((planes * channels, lanes), jnp.float32)] * 2,
        compiler_params=params(),
        cost_estimate=takes(3),
        name="mix",
    )(packed, *pieces)


def swap_halves(values):
    half = values.shape[-1] // 2
    return jnp.concatenate([values[..., half:], values[..., :half]], -1)


def weight_grad_kernel(kept_ref, *refs):
    *pairs, out_ref, gs_ref, sum_ref, sems = refs
    grads = [each.at[core] for each in pairs for core in range(2)]
    channels, lanes = grads[0].shape
    capacity = lanes // 2
    starts = []
    for index, grad in enumerate(grads):
        swapped = swap_halves(grad[...])
        gs_ref[index] = jnp.where(lanes_of(swapped.shape) < capacity, swapped, -swapped)
        starts.append((place_of()[1] ^ flip_at(index)) * 2 * channels)
    chunks = sems.shape[0]
    size = channels // chunks

    def send(chunk):
        rows = pl.ds(chunk * size, size)
        return pltpu.make_async_copy(sum_ref.at[:, rows], out_ref.at[:, rows], sems.at[chunk])

    def step(pair, carry):
        totals = [jnp.zeros((channels, lanes), jnp.float32)] * 2
        for index, start in enumerate(starts):
            real = kept_ref[pl.ds(start, channels)]
            imag = kept_ref[pl.ds(start + channels, channels)]
            for each in range(2):
                row = pl.ds(2 * pair + each, 1)
                totals[each] = totals[each] + real * grads[index][row] + imag * gs_ref[index, row]
        for each, total in enumerate(totals):
            sum_ref[0, 2 * pair + each] = total[:, :capacity]
            sum_ref[1, 2 * pair + each] = total[:, capacity:]
        return carry

    for chunk in range(chunks):
        lax.fori_loop(chunk * size // 2, (chunk + 1) * size // 2, step, 0, unroll=2)
        send(chunk).start()
    for chunk in range(chunks):
        send(chunk).wait()


def weight_grad(kept, pairs, chunks=4):
    _, channels, lanes = pairs[0].shape
    shape = (2, channels, channels, lanes // 2)
    return pl.pallas_call(
        weight_grad_kernel,
        out_shape=jax.ShapeDtypeStruct(shape, jnp.float32),
        in_specs=whole(1 + len(pairs)),
        out_specs=outside(1)[0],
        scratch_shapes=[
            pltpu.VMEM((2 * len(pairs), channels, lanes), jnp.float32),
            pltpu.VMEM(shape, jnp.float32),
            pltpu.SemaphoreType.DMA((chunks,)),
        ],
        compiler_params=params(),
        cost_estimate=takes(2),
        name="weight_grad",
    )(kept, *pairs)


def select_kernel(slots_ref, chosen_ref, *, modes_x):
    capacity = slots_ref.shape[1] // 2
    lanes = 2 * capacity
    place = place_of()[1]
    shape = (modes_x, lanes)
    lane = lanes_of(shape)
    first = lane < capacity
    zero = jnp.zeros(shape, jnp.float32)
    for mode in range(slots_ref.shape[0] // modes_x):
        numbers = slots_ref[pl.ds(mode * modes_x, modes_x)]
        for owner in range(chosen_ref.shape[1] // lanes):
            wanted = ((place ^ flip_at(owner)) * capacity + lane % capacity).astype(jnp.float32)
            hit = jnp.where(numbers == wanted, 1.0, 0.0)
            both = jnp.concatenate([jnp.where(first, hit, zero), jnp.where(first, zero, hit)], 0)
            chosen_ref[pl.ds(mode * 2 * modes_x, 2 * modes_x), pl.ds(owner * lanes, lanes)] = both.astype(jnp.bfloat16)


def select(slots, modes_x, count):
    return pl.pallas_call(
        functools.partial(select_kernel, modes_x=modes_x),
        out_shape=jax.ShapeDtypeStruct((2 * slots.shape[0], count * slots.shape[1]), jnp.bfloat16),
        in_specs=whole(1),
        out_specs=whole(1)[0],
        compiler_params=params(),
        cost_estimate=takes(0.5),
        name="select",
    )(slots)


def slots_to_modes(blocks, chosen_ref, out_ref, modes_x):
    channels = blocks[0].shape[0]
    half = channels // 2
    high, low = split(jnp.concatenate(blocks, 1))
    found = dot_rows(jnp.concatenate([high, low], 0), chosen_ref[...])
    found = found[:channels] + found[channels:]
    local_y = found.shape[1] // (2 * modes_x)
    for mode in range(local_y):
        piece = found[:, mode * 2 * modes_x : (mode + 1) * 2 * modes_x]
        out_ref[pl.ds(mode, half, stride=local_y)] = jnp.concatenate([piece[:half], piece[half:]], 1)


def to_modes_kernel(chosen_ref, *refs, modes_x):
    *pairs, out_ref = refs
    slots_to_modes([pair[core] for pair in pairs for core in range(2)], chosen_ref, out_ref, modes_x)


def to_modes(chosen, pairs, modes_x):
    _, channels, _ = pairs[0].shape
    local_y = chosen.shape[0] // (2 * modes_x)
    return pl.pallas_call(
        functools.partial(to_modes_kernel, modes_x=modes_x),
        out_shape=jax.ShapeDtypeStruct((channels // 2 * local_y, 4 * modes_x), jnp.float32),
        in_specs=whole(1 + len(pairs)),
        out_specs=whole(1)[0],
        compiler_params=params(),
        cost_estimate=takes(1),
        name="to_modes",
    )(chosen, *pairs)


def mix_back(block_of, values):
    channels, lanes = values.shape
    swapped = swap_halves(values)
    real = jnp.zeros((channels, lanes), jnp.float32)
    imag = real
    for channel in range(channels):
        block = block_of(channel)
        real = real + block * values[channel : channel + 1]
        imag = imag + block * swapped[channel : channel + 1]
    other_re, other_im = swap_halves(real), swap_halves(imag)
    return jnp.where(lanes_of(real.shape) < lanes // 2, real + other_re, other_im - imag)


def adjoint_kernel(chosen_ref, *refs, modes_x, blocks):
    pieces, stores, (same_ref, other_ref, out_ref, sum_ref) = refs[:blocks], refs[blocks:-4], refs[-4:]
    steps, channels, lanes = same_ref.shape
    half = channels // 2
    sum_ref[...] = sum(piece[...] for piece in pieces)
    local_y = sum_ref.shape[0] // half
    columns = []
    for mode in range(local_y):
        piece = sum_ref[pl.ds(mode, half, stride=local_y)]
        columns.append(jnp.concatenate([piece[:, : 2 * modes_x], piece[:, 2 * modes_x :]], 0))
    high, low = split(jnp.concatenate(columns, 1))
    found = dot(jnp.concatenate([high, low], 0), chosen_ref[...])
    found = found[:channels] + found[channels:]
    size = channels * channels
    here, beside, others, over = stores

    def block_at(owner):
        chip, other = owner // 2, owner % 2
        if chip == 0:
            return lambda channel: (beside if other else here)[pl.ds(channel * channels, channels)]
        start = (2 if chip == 3 else abs(chip - 1 - other)) * size
        source = over if chip == 2 or chip == 3 and other else others
        return lambda channel: source[pl.ds(start + channel * channels, channels)]

    mixed = []
    for owner in range(2 * steps):
        values = found[:, owner * lanes : (owner + 1) * lanes]
        (other_ref if owner % 2 else same_ref)[owner // 2] = values
        mixed.append(mix_back(block_at(owner), values))
    slots_to_modes(mixed, chosen_ref, out_ref, modes_x)


def adjoint(chosen, pieces, stores, modes_x):
    blocks = len(pieces)
    channels, lanes = math.isqrt(stores[0].shape[0]), stores[0].shape[1]
    steps = chosen.shape[1] // (2 * lanes)
    return pl.pallas_call(
        functools.partial(adjoint_kernel, modes_x=modes_x, blocks=blocks),
        out_shape=[jax.ShapeDtypeStruct((steps, channels, lanes), jnp.float32)] * 2
        + [jax.ShapeDtypeStruct(pieces[0].shape, jnp.float32)],
        in_specs=whole(1 + blocks + len(stores)),
        out_specs=whole(3),
        scratch_shapes=[pltpu.VMEM(pieces[0].shape, jnp.float32)],
        compiler_params=params(),
        cost_estimate=takes(2),
        name="adjoint",
    )(chosen, *pieces, *stores)


def pair_kernel(same_ref, other_ref, *outs):
    for index, out in enumerate(outs):
        out[0] = same_ref[index]
        out[1] = other_ref[TURN[index]]


def pair(same, other):
    return pl.pallas_call(
        pair_kernel,
        out_shape=[jax.ShapeDtypeStruct((2,) + same.shape[1:], same.dtype)] * same.shape[0],
        in_specs=whole(2),
        out_specs=whole(same.shape[0]),
        compiler_params=params(),
        cost_estimate=takes(0.3),
        name="pair",
    )(same, other)


def join_kernel(*refs):
    *parts, out_ref = refs
    start = 0
    for part in parts:
        out_ref[pl.ds(start, part.shape[0])] = part[...]
        start += part.shape[0]


def join(parts):
    rows = sum(part.shape[0] for part in parts)
    return pl.pallas_call(
        join_kernel,
        out_shape=jax.ShapeDtypeStruct((rows, parts[0].shape[1]), parts[0].dtype),
        in_specs=whole(len(parts)),
        out_specs=whole(1)[0],
        compiler_params=params(),
        cost_estimate=takes(0.1),
        name="join",
    )(*parts)


def spread(small, rows, axis, channel_of):
    count = small.shape[0]
    shape = (count * rows, count)
    take = (rows_of(shape) // rows == lanes_of(shape)).astype(jnp.bfloat16)
    shape = (count, count * rows)
    put = (channel_of(lanes_of(shape) // rows) == rows_of(shape)).astype(jnp.bfloat16)
    picked = dot(take, small) if axis else dot_rows(take, small)
    full = dot(picked.astype(jnp.bfloat16), put)
    shape = full.shape
    return jnp.where(rows_of(shape) % rows == lanes_of(shape) % rows, full, 0.0)


def pointwise_kernel(full_ref, shift_ref, in_ref, out_ref):
    channels, rows_x, width = in_ref.shape
    rows = full_ref.shape[0] // channels
    shift = jnp.concatenate([shift_ref[...]] * (width // shift_ref.shape[1]), 1)

    def step(index, carry):
        values = in_ref[:, pl.ds(index * 2 * rows, 2 * rows), :].astype(jnp.float32)
        for half in range(2):
            block = values[:, half * rows : (half + 1) * rows].reshape(channels * rows, width)
            out = dot(full_ref[...], block.astype(jnp.bfloat16)) * DENSITY + shift
            out_ref[:, pl.ds(index * 2 * rows + half * rows, rows), :] = out.reshape(channels, rows, width)
        return carry

    lax.fori_loop(0, rows_x // (2 * rows), step, 0)


def pointwise_map(full, shift, values):
    return pl.pallas_call(
        pointwise_kernel,
        out_shape=jax.ShapeDtypeStruct(values.shape, jnp.float32),
        in_specs=whole(3),
        out_specs=whole(1)[0],
        compiler_params=params(),
        cost_estimate=takes(3),
        name="pointwise_map",
    )(full, shift, values)


def pointwise_back_kernel(full_ref, *refs):
    *terms, out_ref = refs
    channels, rows_x, width = out_ref.shape
    rows = full_ref.shape[0] // channels

    def step(index, carry):
        at = pl.ds(pl.multiple_of(index * 2 * rows, 2 * rows), 2 * rows)
        total = [0.0, 0.0]
        for term in range(2):
            values = [each[:, :, at, :].reshape(channels // 2, 2 * rows, width) for each in terms[term::2]]
            values = jnp.concatenate(values, 0).astype(jnp.float32)
            for half in range(2):
                block = values[:, half * rows : (half + 1) * rows].reshape(channels * rows, width)
                total[half] = total[half] + dot(full_ref[...], block.astype(jnp.bfloat16))
        for half in range(2):
            rows_at = pl.ds(index * 2 * rows + half * rows, rows)
            out_ref[:, rows_at, :] = total[half].reshape(channels, rows, width)
        return carry

    lax.fori_loop(0, rows_x // (2 * rows), step, 0)


def pointwise_back(full, terms):
    pairs, halves, rows_x, width = terms[0].shape
    return pl.pallas_call(
        pointwise_back_kernel,
        out_shape=jax.ShapeDtypeStruct((2 * pairs * halves, rows_x, width), jnp.float32),
        in_specs=whole(1 + len(terms)),
        out_specs=whole(1)[0],
        compiler_params=params(),
        cost_estimate=takes(4),
        name="pointwise_back",
    )(full, *terms)


def invert_x(pieces, xi_ref, st_ref):
    high, low = split(jnp.concatenate([piece[...] for piece in pieces], 0))
    deep = high.shape[1]
    left = jnp.concatenate([high, low], 1)
    found = dot(left, xi_ref[pl.ds(0, 2 * deep)]) + dot(high, xi_ref[pl.ds(2 * deep, deep)])
    st_ref[...] = found.reshape(st_ref.shape)


def spectral_part(index, half, st_ref, table):
    blocks, _, local_y, wide = st_ref.shape
    rows_x = wide // 4
    here = st_ref[:, index, :, pl.ds(half * 2 * rows_x, 2 * rows_x)].reshape(blocks * local_y, 2 * rows_x)
    parts = [here[:, :rows_x], here[:, rows_x:]]
    tall = jnp.transpose(jnp.concatenate(parts + parts, 0))
    high = tall.astype(jnp.bfloat16)
    first = lanes_of(tall.shape) < tall.shape[1] // 2
    mixed = jnp.where(first, tall, tall - high.astype(jnp.float32)).astype(jnp.bfloat16)
    return dot(jnp.concatenate([mixed, high], 1), table)


def slope_kernel(*refs, blocks):
    pieces, (xi_ref, ti_ref, tf_ref, xf_ref, mapped_ref, cot_ref) = refs[:blocks], refs[blocks : blocks + 6]
    terms, sums = refs[blocks + 6 : blocks + 10], refs[blocks + 10 : 2 * blocks + 10]
    st_ref, yt_ref, *before = refs[2 * blocks + 10 :]
    channels, rows_x, _ = mapped_ref.shape
    half_channels = channels // 2
    deep = tf_ref.shape[0] // 2
    modes_y = deep // 2
    local_y = modes_y // blocks
    invert_x(pieces, xi_ref, st_ref)

    def invert(index, parity):
        for half in range(2):
            channel = half * half_channels + index
            before[parity][half] = mapped_ref[channel] + spectral_part(index, half, st_ref, ti_ref[0])

    def slope(index, parity):
        for half in range(2):
            channel = half * half_channels + index
            grad = cot_ref[channel].astype(jnp.float32) * twice_gelu_slope(before[parity][half])
            high, low = split(grad)
            terms[2 * parity][index // 2, half] = high
            terms[2 * parity + 1][index // 2, half] = low

    def forward(index, parity):
        for half in range(2):
            high, low = terms[2 * parity][index // 2, half], terms[2 * parity + 1][index // 2, half]
            both = dot_rows(tf_ref[...], high)
            found = both[:deep] + both[deep:] + dot_rows(tf_ref[pl.ds(0, deep)], low)
            for block in range(blocks):
                for part in range(2):
                    at = part * modes_y + block * local_y
                    columns = pl.ds((2 * half + part) * rows_x, rows_x)
                    yt_ref[block, index, :, columns] = found[at : at + local_y]

    def step(pair, carry):
        index = 2 * pair
        forward(jnp.maximum(index - 1, 1), 1)
        invert(index + 1, 1)
        slope(index, 0)
        forward(index, 0)
        invert(jnp.minimum(index + 2, half_channels - 2), 0)
        slope(index + 1, 1)
        return carry

    invert(0, 0)
    lax.fori_loop(0, half_channels // 2, step, 0, unroll=2)
    forward(half_channels - 1, 1)
    high, low = split(yt_ref[...].reshape(-1, yt_ref.shape[-1]))
    lanes = xf_ref.shape[1] // 2
    both = dot(high, xf_ref[...])
    total = both[:, :lanes] + both[:, lanes:] + dot(low, xf_ref[:, :lanes])
    rows = total.shape[0] // blocks
    for block in range(blocks):
        sums[block][...] = total[block * rows : (block + 1) * rows]


def slope_step(pieces, tables, mapped, cotangent):
    ti, tf, xi, xf = tables
    blocks = len(pieces)
    channels, rows_x, width = mapped.shape
    half = channels // 2
    local_y = pieces[0].shape[0] // half
    results = pl.pallas_call(
        functools.partial(slope_kernel, blocks=blocks),
        out_shape=[jax.ShapeDtypeStruct((half // 2, 2, rows_x, width), jnp.bfloat16)] * 4
        + [jax.ShapeDtypeStruct(pieces[0].shape, jnp.float32)] * blocks,
        in_specs=whole(blocks + 6),
        out_specs=whole(4 + blocks),
        scratch_shapes=[pltpu.VMEM((blocks, half, local_y, 4 * rows_x), jnp.float32)] * 2
        + [pltpu.VMEM((2, rows_x, width), jnp.float32)] * 2,
        compiler_params=params(),
        cost_estimate=takes(8),
        name="slope_step",
    )(*pieces, xi, ti, tf, xf, mapped, cotangent)
    return results[:4], results[4:]


def finish_kernel(*refs, blocks, group):
    pieces, (xi_ref, ti_ref, part_ref, out_ref, st_ref, sum_ref, sems) = refs[:blocks], refs[blocks:]
    channels = part_ref.shape[0]
    invert_x(pieces, xi_ref, st_ref)

    def copies(index):
        for half in range(2):
            rows = pl.ds(half * (channels // 2) + index * group, group)
            yield pltpu.make_async_copy(sum_ref.at[rows], out_ref.at[rows], sems.at[half, index])

    def step(index, carry):
        for half in range(2):
            for member in range(group):
                place = index * group + member
                channel = half * (channels // 2) + place
                sum_ref[channel] = part_ref[channel] + spectral_part(place, half, st_ref, ti_ref[1])
        for copy in copies(index):
            copy.start()
        return carry

    def settle(index, carry):
        for copy in copies(index):
            copy.wait()
        return carry

    steps = channels // (2 * group)
    lax.fori_loop(0, steps, step, 0)
    lax.fori_loop(0, steps, settle, 0)


def finish(pieces, tables, part, group=4):
    ti, _, xi, _ = tables
    blocks = len(pieces)
    channels, rows_x, _ = part.shape
    half = channels // 2
    local_y = pieces[0].shape[0] // half
    return pl.pallas_call(
        functools.partial(finish_kernel, blocks=blocks, group=group),
        out_shape=jax.ShapeDtypeStruct(part.shape, jnp.float32),
        in_specs=whole(blocks + 3),
        out_specs=outside(1)[0],
        scratch_shapes=[
            pltpu.VMEM((blocks, half, local_y, 4 * rows_x), jnp.float32),
            pltpu.VMEM(part.shape, jnp.float32),
            pltpu.SemaphoreType.DMA((2, half // group)),
        ],
        compiler_params=params(20),
        cost_estimate=takes(4),
        name="finish",
    )(*pieces, xi, ti, part)


def exchange(piece, axis, count, flip):
    return lax.ppermute(piece, axis, [(i, i ^ flip) for i in range(count)])


def exchange_two(piece, axis, count, *flips):
    return lax.ppermute(piece, axis, [(i, i ^ flips[i % 2]) for i in range(count)])


def around(pieces, count):
    return [
        pieces[0],
        exchange_two(pieces[1], "py", count, 4, 2),
        exchange_two(pieces[2], "py", count, 2, 4),
        exchange(pieces[3], "py", count, 6),
    ]


def to_owners(same, other, count):
    return around(pair(same, exchange(other, "py", count, 1)), count)


def between_chips(piece, count):
    return around([piece] * 4, count)


def between_cores(pieces, count, beside):
    other = [beside] + [exchange(piece, "py", count, 1) for piece in pieces[1:]]
    return [each for i, piece in enumerate(pieces) for each in (piece, other[TURN[i]])]


def from_all(piece, axis, count):
    return [piece] + [exchange(piece, axis, count, step) for step in range(count - 1, 0, -1)][::-1]


def to_all(pieces, axis, count):
    return pieces[:1] + [exchange(pieces[step], axis, count, step) for step in range(count - 1, 0, -1)][::-1]


def on_device_packed(
    field_in,
    cotangent,
    spectrum_saved,
    weight_store,
    block_slot,
    kx_modes,
    ky_modes,
    pointwise,
    bias_vector,
):
    channels, _, rows_x, width_y = field_in.shape
    count_x, count_y = lax.axis_size("px"), lax.axis_size("py")
    full_x = rows_x * count_x
    planes, local_y, local_x = spectrum_saved.shape[1:4]
    modes_x = kx_modes.shape[0]
    lanes = 2 * weight_store.shape[0]
    store = jnp.transpose(weight_store, (1, 2, 3, 0))
    barrier = lax.optimization_barrier
    spectrum = jnp.transpose(spectrum_saved, (1, 2, 3, 4, 0)).reshape(-1, channels)
    piece, everything = pack(block_slot, spectrum, ky_modes, kx_modes, bias_vector, pointwise, lanes)
    pieces = between_chips(piece, count_y)
    beside = exchange(piece, "py", count_y, 1)
    piece, small, packed = unpack(everything, store, piece.shape[1])
    pieces, beside, piece = barrier((pieces, beside, piece))
    pieces = between_cores([piece] + pieces[1:], count_y, beside)
    kept, slots, *mixed = mix(packed, pieces, planes, local_x)
    chosen = select(slots, modes_x, count_y)
    pairs = to_owners(*mixed, count_y)
    beside = exchange(packed, "py", count_y, 1)
    tables, full_map, full_back, shift = make_tables(small, full_x, rows_x, width_y, ky_modes.shape[0], modes_x)
    pairs, chosen, full_map, packed, beside = barrier((pairs, chosen, full_map, packed, beside))
    near = exchange_two(packed, "py", count_y, 4, 2)
    near_other = exchange_two(beside, "py", count_y, 4, 2)
    received = from_all(to_modes(chosen, pairs, modes_x), "px", count_x)
    mapped = pointwise_map(full_map, shift, field_in[:, 0])
    received, mapped, near = barrier((received, mapped, near))
    far = exchange_two(near, "py", count_y, 2, 4)
    terms, sums = slope_step(received, tables, mapped, cotangent[:, 0])
    sums, terms, far, near_other = barrier((list(sums), list(terms), far, near_other))
    others = join([near, near_other, far])
    others_beside = exchange(others, "py", count_y, 1)
    received = to_all(sums, "px", count_x)
    back = pointwise_back(full_back, terms)
    received, back, others_beside = barrier((received, back, others_beside))
    same, other, mixed = adjoint(chosen, received, [packed, beside, others, others_beside], modes_x)
    received = from_all(mixed, "px", count_x)
    pairs = to_owners(same, other, count_y)
    field_grad = finish(received, tables, back)
    blocks = weight_grad(kept, pairs)
    return (field_grad[:, None], jnp.transpose(blocks, (3, 0, 1, 2)))


def packs(mesh, channels, planes, rows, width, modes, capacity):
    count_x, count_y = mesh.shape["px"], mesh.shape["py"]
    powers = all(size & (size - 1) == 0 for size in (rows, width))
    return (
        powers
        and (count_x, count_y, planes) == (4, 8, 8)
        and channels == 32
        and 4 * modes == 128
        and 2 * capacity == 128
        and rows // count_x == 128
        and width % 256 == 0
        and modes // count_x == 8
    )


def solution(mesh):
    placed = (
        P(None, "py", "px", None),
        P(None, "py", "px", None),
        P(None, None, "px", "py", None),
        P(("px", "py"), None, None, None),
        P("py", "px"),
        P(),
        P(),
        P(),
        P(),
    )

    def run(*args):
        channels, planes, rows, width = args[0].shape
        capacity = args[3].shape[0] // mesh.size
        packed = packs(mesh, channels, planes, rows, width, args[5].shape[0], capacity)
        return jax.shard_map(
            on_device_packed if packed else on_device,
            mesh=mesh,
            in_specs=placed,
            out_specs=(P(None, "py", "px", None), P(("px", "py"), None, None, None)),
            check_vma=False,
        )(*args)

    return run
```
